32 devices in a mesh: dp: 2 (over x), wide: 16 (over z, y, core).
Axes of the slice: x: 2, y: 2, z: 4, core: 2. Of those that a mesh axis runs over, the one named last changes fastest.
Arguments:
- latents: bfloat16 [2, 32, 8, 16, 256], P('dp', 'wide'), may hold values from -36 to 36
- cotangent: bfloat16 [2, 32, 8, 16, 256], P('dp', 'wide'), may hold values from -41 to 41
- norm_gain: float32 [256], replicated, may hold values from 0.25 to 1.75
- norm_bias: float32 [256], replicated, may hold values from -3 to 3
- w_spatial: bfloat16 [2304, 256], P('dp'), may hold values from -0.125 to 0.125
- w_temporal: bfloat16 [768, 256], P('dp'), may hold values from -0.21875 to 0.21875
Outputs:
- block_out: bfloat16 [2, 32, 8, 16, 256], P('dp', 'wide')
- grad_latents: bfloat16 [2, 32, 8, 16, 256], P('dp', 'wide')
- grad_spatial: float32 [2304, 256], P('dp', 'wide')
- grad_temporal: float32 [768, 256], P('dp', 'wide')
- grad_norm: float32 [2, 256], P(None, 'wide')
The draws below stay inside these ranges and needn't reach their ends.
All inputs are finite; a program needn't handle non-finite values.
Results may differ from the reference program's by a relative error of at most 0.012.
Values may be sent and summed in bfloat16 or wider, within the bound.
No kernel may reach another device: no remote copies, remote signals or barrier semaphores. Data moves between devices by JAX's collectives and lax.ppermute only.
A program may use at most 64 MiB of HBM per device.

```python
import math
import jax
import jax.numpy as jnp
from jax import lax

C = 256
GROUPS = 32
F_DEV = 2
ROWS = 8
COLS = 16
CLIPS = 2
FRAMES = 32


def draw_latents(key, part):
    key_noise, key_frame, key_chan = jax.random.split(key, 3)
    shape = (CLIPS, FRAMES, ROWS, COLS, C)
    position = jnp.arange(FRAMES).astype(jnp.float32) / (FRAMES - 1)
    ramp = jnp.exp(math.log(3.0) * position)
    jitter = jnp.exp(jax.random.uniform(key_frame, (CLIPS, FRAMES), minval=0.0, maxval=math.log(3.4))) / 3.4
    frame_scale = ramp[None, :] * jitter
    chan_scale = jnp.exp(jax.random.uniform(key_chan, (C,), minval=math.log(0.3), maxval=math.log(3.0)))
    noise = jax.random.truncated_normal(key_noise, -4.0, 4.0, shape)
    value = noise * frame_scale[:, :, None, None, None] * chan_scale
    return value.astype(jnp.bfloat16)


def draw_cotangent(key, part):
    base = jax.random.fold_in(key, 7177)
    key_noise, key_frame, key_offset, key_pair = jax.random.split(base, 4)
    shape = (CLIPS, FRAMES, ROWS, COLS, C)
    position = jnp.arange(FRAMES).astype(jnp.float32) / (FRAMES - 1)
    ramp = jnp.exp(math.log(3.0) * position)
    jitter = jnp.exp(jax.random.uniform(key_frame, (CLIPS, FRAMES), minval=math.log(0.5), maxval=0.0))
    frame_scale = ramp[None, :] * jitter
    blocks = FRAMES // F_DEV
    chan_block = C // blocks
    pairing = jax.random.permutation(key_pair, blocks)
    frame_block = jnp.arange(FRAMES) // F_DEV
    chan_owner = jnp.arange(C) // chan_block
    boosted = (pairing[frame_block][:, None] == chan_owner[None, :]).astype(jnp.float32)
    boost = 1.0 + 2.0 * boosted
    offset = jax.random.uniform(key_offset, (C,), minval=-0.5, maxval=0.5)
    noise = jax.random.truncated_normal(key_noise, -4.0, 4.0, shape) + offset
    value = noise * frame_scale[:, :, None, None, None] * boost[None, :, None, None, :]
    return value.astype(jnp.bfloat16)


def levels(stream_key, dims, cuts, smallest, largest):
    gain, own = 1.0, jax.random.fold_in(stream_key, 6)
    for axis_at, parts in cuts:
        draws = jnp.exp(jax.random.uniform(jax.random.fold_in(own, axis_at), (parts,), jnp.float32, smallest / len(cuts), largest / len(cuts)))
        gain = gain * jnp.repeat(draws, dims[axis_at] // parts).reshape([-1 if axis == axis_at else 1 for axis in range(len(dims))])
    return gain


def bell_draw(key, shape, scale, bound, cuts=(), kind=jnp.bfloat16):
    result = jax.random.normal(key, shape, jnp.float32) * scale
    if len(cuts) > 0:
        result = levels(key, shape, cuts, -0.22, 0.18) * result
    return jnp.clip(result, min=-bound, max=bound).astype(kind)


def setup_inputs(seed: int = 0) -> dict:
    splits = jax.random.split(jax.random.key(seed), 7)
    return {
        "latents": draw_latents(jax.random.fold_in(splits[6], 71), 0),
        "cotangent": draw_cotangent(jax.random.fold_in(splits[6], 71), 0),
        "norm_gain": jnp.clip(1.0 + 0.15 * jax.random.normal(splits[2], (C,), jnp.float32), 0.25, 1.75),
        "norm_bias": bell_draw(splits[3], (C,), 0.5, 3.0, (), jnp.float32),
        "w_spatial": bell_draw(splits[4], (9 * C, C), (9 * C) ** -0.5, 0.125, ((0, 2),)),
        "w_temporal": bell_draw(splits[5], (3 * C, C), (3 * C) ** -0.5, 0.21875, ((0, 2),)),
    }


epsilon = 1e-05

def contract(left, right):
    return lax.dot_general(left, right, (((0,), (0,)), ((), ())), preferred_element_type=jnp.float32)

def spatial_forward(activated, weights):
    frames, rows_here, cols_here, channels = activated.shape
    padded = jnp.pad(activated, ((0, 0), (1, 1), (1, 1), (0, 0)))
    running = jnp.zeros((frames * rows_here * cols_here, channels), jnp.float32)
    for tap_row in range(3):
        for tap_col in range(3):
            tap_index = 3 * tap_row + tap_col
            window = padded[:, tap_row:tap_row + rows_here, tap_col:tap_col + cols_here, :].reshape(-1, channels)
            running = running + jnp.dot(window, weights[tap_index * channels:(tap_index + 1) * channels], preferred_element_type=jnp.float32)
    return running.reshape(frames, rows_here, cols_here, channels)

def spatial_backward(activated, grad_out, weights):
    frames, rows_here, cols_here, channels = activated.shape
    pad_act = jnp.pad(activated, ((0, 0), (1, 1), (1, 1), (0, 0)))
    pad_grad = jnp.pad(grad_out, ((0, 0), (1, 1), (1, 1), (0, 0)))
    flat_grad = grad_out.reshape(-1, channels)
    running = jnp.zeros((frames * rows_here * cols_here, channels), jnp.float32)
    pieces = []
    for tap_row in range(3):
        for tap_col in range(3):
            tap_index = 3 * tap_row + tap_col
            block = weights[tap_index * channels:(tap_index + 1) * channels]
            window_grad = pad_grad[:, 2 - tap_row:2 - tap_row + rows_here, 2 - tap_col:2 - tap_col + cols_here, :].reshape(-1, channels)
            running = running + jnp.dot(window_grad, block.T, preferred_element_type=jnp.float32)
            window_act = pad_act[:, tap_row:tap_row + rows_here, tap_col:tap_col + cols_here, :].reshape(-1, channels)
            pieces.append(contract(window_act, flat_grad))
    return (running.reshape(frames, rows_here, cols_here, channels), jnp.concatenate(pieces, axis=0))

def temporal_apply(extended, weights, frames):
    channels = extended.shape[-1]
    shape_out = (extended.shape[0], frames, extended.shape[2], channels)
    running = jnp.zeros((shape_out[0] * frames * shape_out[2], channels), jnp.float32)
    for time_delay in range(3):
        earlier = extended[:, 2 - time_delay:2 - time_delay + frames].reshape(-1, channels)
        running = running + jnp.dot(earlier, weights[time_delay * channels:(time_delay + 1) * channels], preferred_element_type=jnp.float32)
    return running.reshape(shape_out)

def temporal_adjoint(earlier_ext, later_ext, grad_rows, weights):
    frames = grad_rows.shape[1]
    channels = grad_rows.shape[-1]
    flat_grad = grad_rows.reshape(-1, channels)
    running = jnp.zeros(flat_grad.shape, jnp.float32)
    pieces = []
    for time_delay in range(3):
        block = weights[time_delay * channels:(time_delay + 1) * channels]
        later_rows = later_ext[:, time_delay:time_delay + frames].reshape(-1, channels)
        running = running + jnp.dot(later_rows, block.T, preferred_element_type=jnp.float32)
        earlier = earlier_ext[:, 2 - time_delay:2 - time_delay + frames].reshape(-1, channels)
        pieces.append(contract(earlier, flat_grad))
    return (running.reshape(grad_rows.shape), jnp.concatenate(pieces, axis=0))

def clip_pass(latents, cotangent, norm_gain, norm_bias, w_spatial, w_temporal):
    latents = latents[None]
    cotangent = cotangent[None]
    clip_count, frames, rows_here, cols_here, channels = latents.shape
    per_group = channels // GROUPS
    widened = latents.astype(jnp.float32).reshape(clip_count, frames, rows_here, cols_here, GROUPS, per_group)
    cells_count = frames * rows_here * cols_here * per_group
    group_mean = lax.optimization_barrier(jnp.sum(widened, axis=(1, 2, 3, 5))) / cells_count
    variance = lax.optimization_barrier(jnp.sum(widened * widened, axis=(1, 2, 3, 5))) / cells_count - group_mean * group_mean
    inv_std = 1.0 / jnp.sqrt(variance + epsilon)
    mean_wide = group_mean[:, None, None, None, :, None]
    std_wide = inv_std[:, None, None, None, :, None]
    whitened = (widened - mean_wide) * std_wide
    flat_white = whitened.reshape(latents.shape)
    normed = flat_white * norm_gain + norm_bias
    sigmoid = jax.nn.sigmoid(normed)
    activated = (normed * sigmoid).astype(jnp.bfloat16)
    silu_slope = sigmoid * (1.0 + normed * (1.0 - sigmoid))
    cell_count = rows_here * cols_here
    stacked = activated.reshape(clip_count * frames, rows_here, cols_here, channels)
    spatial = spatial_forward(stacked, w_spatial).astype(jnp.bfloat16).reshape(clip_count, frames, cell_count, channels)
    earlier_ext = jnp.pad(spatial, ((0, 0), (2, 0), (0, 0), (0, 0)))
    temporal = temporal_apply(earlier_ext, w_temporal, frames)
    block_out = (latents.astype(jnp.float32) + temporal.reshape(latents.shape)).astype(jnp.bfloat16)
    grad_rows = cotangent.reshape(clip_count, frames, cell_count, channels)
    later_ext = jnp.pad(grad_rows, ((0, 0), (0, 2), (0, 0), (0, 0)))
    grad_wide, grads_temporal = temporal_adjoint(earlier_ext, later_ext, grad_rows, w_temporal)
    grad_spatial_act = grad_wide.astype(jnp.bfloat16).reshape(clip_count * frames, rows_here, cols_here, channels)
    grad_activated, grads_spatial = spatial_backward(stacked, grad_spatial_act, w_spatial)
    grad_normed = grad_activated.reshape(latents.shape) * silu_slope
    gain_term = lax.optimization_barrier(jnp.sum(grad_normed * flat_white, axis=(0, 1, 2, 3)))
    bias_term = lax.optimization_barrier(jnp.sum(grad_normed, axis=(0, 1, 2, 3)))
    grad_white = (grad_normed * norm_gain).reshape(widened.shape)
    grad_mean = lax.optimization_barrier(jnp.sum(grad_white, axis=(1, 2, 3, 5))) / cells_count
    grad_cross = lax.optimization_barrier(jnp.sum(grad_white * whitened, axis=(1, 2, 3, 5))) / cells_count
    inner = (grad_white - grad_mean[:, None, None, None, :, None] - whitened * grad_cross[:, None, None, None, :, None]) * std_wide
    grad_input = (cotangent.astype(jnp.float32) + inner.reshape(latents.shape)).astype(jnp.bfloat16)
    return (block_out[0], grad_input[0], grads_spatial, grads_temporal, jnp.stack([gain_term, bias_term]))

def reference(latents, cotangent, norm_gain, norm_bias, w_spatial, w_temporal):

    def one_clip(clip_pair):
        return clip_pass(clip_pair[0], clip_pair[1], norm_gain, norm_bias, w_spatial, w_temporal)
    results = lax.map(one_clip, (latents, cotangent))
    grad_scale = 1.0 / math.sqrt(CLIPS * FRAMES * ROWS * COLS)
    return (results[0], results[1], lax.optimization_barrier(jnp.sum(results[2], axis=0)) * grad_scale, lax.optimization_barrier(jnp.sum(results[3], axis=0)) * grad_scale, lax.optimization_barrier(jnp.sum(results[4], axis=0)) * grad_scale)
```

```python
import functools
import math

import jax
import jax.numpy as jnp
from jax import lax
from jax.experimental import pallas as pl
from jax.experimental.pallas import tpu as pltpu
from jax.sharding import PartitionSpec as P

GROUPS = 32
EPSILON = 1e-05
F32 = jnp.float32
BF16 = jnp.bfloat16
VMEM = pl.BlockSpec(memory_space=pltpu.VMEM)
NT = (((1,), (1,)), ((), ()))
NN = (((1,), (0,)), ((), ()))


def call(body, out_shapes, scratch=(), flops=0, moved=0):
    many = isinstance(out_shapes, (tuple, list))

    def run(*operands):
        return pl.pallas_call(
            body,
            out_shape=out_shapes,
            in_specs=[VMEM] * len(operands),
            out_specs=[VMEM] * len(out_shapes) if many else VMEM,
            scratch_shapes=list(scratch),
            compiler_params=pltpu.CompilerParams(vmem_limit_bytes=40 * 1024 * 1024),
            cost_estimate=pl.CostEstimate(
                flops=flops, bytes_accessed=moved, transcendentals=0
            ),
        )(*operands)

    return run


def shape(dims, kind):
    return jax.ShapeDtypeStruct(dims, kind)


def mm(left, right, dims=NN):
    return lax.dot_general(left, right, dims, preferred_element_type=F32)


def group_total(rows, per_group):
    channels = rows.shape[-1]
    first = lax.broadcasted_iota(jnp.int32, (channels, channels), 0) // per_group
    second = lax.broadcasted_iota(jnp.int32, (channels, channels), 1) // per_group
    same = (first == second).astype(F32)
    return lax.dot_general(
        rows, same, NN, precision=lax.Precision.HIGHEST, preferred_element_type=F32
    )


def stats_body(lat_ref, out_ref):
    x = lat_ref[...].astype(F32)
    both = jnp.concatenate(
        [jnp.sum(x, axis=0, keepdims=True), jnp.sum(x * x, axis=0, keepdims=True)], axis=0
    )
    out_ref[...] = jnp.broadcast_to(both[None], out_ref.shape)


def whiten(lat, stats, count, per_group):
    total = group_total(jnp.sum(stats, axis=0), per_group) / count
    mean = total[0:1]
    inv_std = 1.0 / jnp.sqrt(total[1:2] - mean * mean + EPSILON)
    return (lat.astype(F32) - mean) * inv_std, inv_std


def store_shifted(pad_ref, values, frames, cells, cols):
    total = frames * cells
    column = lax.broadcasted_iota(jnp.int32, (total, 1), 0) % cols
    left = jnp.where(column == 0, 0.0, pltpu.roll(values, 1, 0))
    right = jnp.where(column == cols - 1, 0.0, pltpu.roll(values, total - 1, 0))
    edge = jnp.zeros((cols, values.shape[1]), BF16)
    for at, form in enumerate((left, values, right)):
        low = form.astype(BF16)
        for f in range(frames):
            pad_ref[at, f, 0:cols] = edge
            pad_ref[at, f, cols : cols + cells] = low[f * cells : (f + 1) * cells]
            pad_ref[at, f, cols + cells :] = edge


def window(pad_ref, dy, dx, frames, cells, cols):
    return jnp.concatenate(
        [pad_ref[dx, f, dy * cols : dy * cols + cells] for f in range(frames)], axis=0
    )


def main_body(
    sizes,
    lat_ref,
    cot_ref,
    halo_ref,
    stats_ref,
    gain_ref,
    bias_ref,
    ws_ref,
    wt_ref,
    *rest,
):
    D, W, frames, cells, cols, count, per_group, aligned = sizes
    pieces = rest[: 4 * (D - 1)]
    rest = rest[4 * (D - 1) :]
    spatial_ref, sums_ref, grad_ref, keep_ref, send_ref = rest[:5]
    full_ws, full_wt, act_pad, gsa_pad, gsa_t, cot_t = rest[5:]
    channels = lat_ref.shape[1]
    d = lax.axis_index("dp")
    core = lax.rem(lax.axis_index("wide"), 2)

    for shard_ref, full, offset in ((ws_ref, full_ws, 0), (wt_ref, full_wt, 1)):
        n = shard_ref.shape[0]
        full[pl.ds(pl.multiple_of(d * n, 16), n)] = shard_ref[...]
        for s in range(1, D):
            source = lax.rem(d + D - s, D)
            for which in range(2):
                piece = pieces[4 * (s - 1) + 2 * which + offset]
                half = n // 2
                holder = core if which == 0 else 1 - core
                start = pl.multiple_of(source * n + holder * half, 16)
                full[pl.ds(start, half)] = piece[...]

    cot = cot_ref[...]
    extended = jnp.concatenate([cot, halo_ref[...]], axis=0)
    rows = frames * cells
    gsa = jnp.zeros((rows, channels), F32)
    for k in range(3):
        gsa += mm(
            extended[k * cells : k * cells + rows],
            full_wt[k * channels : (k + 1) * channels],
            NT,
        )
    gsa = gsa.astype(BF16).astype(F32)
    store_shifted(gsa_pad, gsa, frames, cells, cols)

    white, _ = whiten(lat_ref[...], stats_ref[...], count, per_group)
    gain = gain_ref[...]
    normed = white * gain + bias_ref[...]
    sig = jax.nn.sigmoid(normed)
    act = (normed * sig).astype(BF16).astype(F32)
    store_shifted(act_pad, act, frames, cells, cols)

    gsa_t[...] = gsa.T.astype(BF16)
    for f in range(frames + 2):
        cot_t[:, f * cells : (f + 1) * cells] = (
            extended[f * cells : (f + 1) * cells].astype(F32).T.astype(BF16)
        )
    if aligned:
        step = channels // W
        order = [pl.ds(pl.multiple_of((2 * j + core) * step, 16), step) for j in range(W // 2)]
        order += [
            pl.ds(pl.multiple_of((2 * j + 1 - core) * step, 16), step) for j in range(W // 2)
        ]
        left_s = jnp.concatenate([gsa_t[at] for at in order], axis=0)
        left_t = jnp.concatenate([cot_t[at] for at in order], axis=0)
    else:
        left_s, left_t = gsa_t[...], cot_t[...]

    def put(block, column, shard, offset):
        if not aligned:
            keep_ref[:, offset + column : offset + column + channels] = block.astype(BF16)
            return
        low = block.astype(BF16)
        half = channels // 2
        for at in range(0, channels, 128):
            owner, place = (column + at) // shard, (column + at) % shard + offset
            keep_ref[owner, :, place : place + 128] = low[:half, at : at + 128]
            send_ref[owner, :, place : place + 128] = low[half:, at : at + 128]

    shard_s, shard_t = ws_ref.shape[0], wt_ref.shape[0]
    out = jnp.zeros((rows, channels), F32)
    for dy in range(3):
        for dx in range(3):
            tap = 3 * dy + dx
            seen = window(act_pad, dy, dx, frames, cells, cols)
            out += mm(seen, full_ws[tap * channels : (tap + 1) * channels])
            put(mm(left_s, seen), tap * channels, shard_s, 0)
    spatial = out.astype(BF16)
    spatial_ref[...] = spatial
    for k in range(3):
        put(
            mm(left_t[:, k * cells : k * cells + rows], spatial),
            k * channels,
            shard_t,
            shard_s if aligned else shard_s * D,
        )

    grad = jnp.zeros((rows, channels), F32)
    for dy in range(3):
        for dx in range(3):
            tap = 3 * dy + dx
            seen = window(gsa_pad, 2 - dy, 2 - dx, frames, cells, cols)
            grad += mm(seen, full_ws[tap * channels : (tap + 1) * channels], NT)
    grad = grad * (sig * (1.0 + normed * (1.0 - sig)))
    grad_ref[...] = grad
    both = jnp.concatenate(
        [
            jnp.sum(grad * white, axis=0, keepdims=True),
            jnp.sum(grad, axis=0, keepdims=True),
        ],
        axis=0,
    )
    sums_ref[...] = jnp.broadcast_to(both[None], sums_ref.shape)


def finish_body(
    sizes,
    lat_ref,
    cot_ref,
    stats_ref,
    gain_ref,
    grad_ref,
    sums_ref,
    spatial_ref,
    before_ref,
    wt_ref,
    *rest,
):
    D, W, frames, cells, cols, count, per_group, aligned = sizes
    pieces = rest[: 2 * (D - 1)]
    block_ref, glat_ref, norm_ref, full_wt = rest[2 * (D - 1) :]
    channels = lat_ref.shape[1]
    d = lax.axis_index("dp")
    core = lax.rem(lax.axis_index("wide"), 2)
    n = wt_ref.shape[0]
    full_wt[pl.ds(pl.multiple_of(d * n, 16), n)] = wt_ref[...]
    for s in range(1, D):
        source = lax.rem(d + D - s, D)
        for which in range(2):
            holder = core if which == 0 else 1 - core
            start = pl.multiple_of(source * n + holder * (n // 2), 16)
            full_wt[pl.ds(start, n // 2)] = pieces[2 * (s - 1) + which][...]
    extended = jnp.concatenate([before_ref[...], spatial_ref[...]], axis=0)
    rows = frames * cells
    temporal = jnp.zeros((rows, channels), F32)
    for k in range(3):
        start = (2 - k) * cells
        temporal += mm(
            extended[start : start + rows], full_wt[k * channels : (k + 1) * channels]
        )
    lat = lat_ref[...]
    block_ref[...] = (lat.astype(F32) + temporal).astype(BF16)

    white, inv_std = whiten(lat, stats_ref[...], count, per_group)
    gain = gain_ref[...]
    total = jnp.sum(sums_ref[...], axis=0)
    norm_ref[...] = total
    means = group_total(total * gain, per_group) / count
    inner = inv_std * (grad_ref[...] * gain - means[1:2] - white * means[0:1])
    glat_ref[...] = (cot_ref[...].astype(F32) + inner).astype(BF16)


def plane_body(sizes, keep_ref, got_ref, *outs):
    D = sizes[0]
    d = lax.axis_index("dp")
    y = lax.rem(lax.axis_index("wide") // 2, 2)
    at = 0
    for a in range(D):
        for b in range(2):
            owner, side = lax.rem(d + a, D), lax.rem(y + b, 2)
            outs[at][...] = (
                keep_ref[owner, :, side].astype(F32) + got_ref[owner, :, side].astype(F32)
            ).astype(BF16)
            at += 1


def line_body(depth, *refs):
    outs = refs[-depth:]
    z = lax.axis_index("wide") // 4
    for s in range(depth):
        owner = lax.rem(z + s, depth)
        total = refs[0][owner].astype(F32)
        for term in refs[1:-depth]:
            total += term[owner].astype(F32)
        outs[s][...] = total.astype(BF16)


def last_body(scale, split, terms, *refs):
    spatial_ref, temporal_ref, norm_ref = refs[-3:]
    total = refs[0][...].astype(F32)
    for term in refs[1:terms]:
        total += term[...].astype(F32)
    total = total * scale
    spatial_ref[...] = total[:, :split]
    temporal_ref[...] = total[:, split:]
    norm_columns(scale, refs[terms:-3], norm_ref)


def norm_columns(scale, terms, norm_ref):
    norm = terms[0][...]
    for term in terms[1:]:
        norm += term[...]
    channels, width = norm.shape[1], norm_ref.shape[1]
    row = lax.broadcasted_iota(jnp.int32, (channels, width), 0)
    column = lax.broadcasted_iota(jnp.int32, (channels, width), 1)
    pick = (row == column + lax.axis_index("wide") * width).astype(F32)
    norm_ref[...] = (
        lax.dot_general(
            norm, pick, NN, precision=lax.Precision.HIGHEST, preferred_element_type=F32
        )
        * scale
    )


def only_norm_body(scale, *refs):
    norm_columns(scale, refs[:-1], refs[-1])


def local(latents, cotangent, norm_gain, norm_bias, w_spatial, w_temporal):
    D, W = lax.axis_size("dp"), lax.axis_size("wide")
    _, frames, rows_here, cols, channels = latents.shape
    cells = rows_here * cols
    rows = frames * cells
    per_group = channels // GROUPS
    count = W * frames * cells * per_group
    shard_s, shard_t = w_spatial.shape[0], w_temporal.shape[0]
    aligned = (channels // W) % 16 == 0 and shard_s % 128 == 0 and shard_t % 128 == 0
    aligned = aligned and W % 4 == 0
    sizes = (D, W, frames, cells, cols, count, per_group, aligned)
    scale = 1.0 / math.sqrt(D * W * frames * cells)

    lat, cot = latents.reshape(rows, channels), cotangent.reshape(rows, channels)
    gain, bias = norm_gain.reshape(1, channels), norm_bias.reshape(1, channels)

    def over_all(moves):
        pairs = []
        for d in range(D):
            for w in range(W):
                to = moves(d, w)
                pairs.append((d * W + w, to[0] * W + to[1]))
        return pairs

    def send(value, moves):
        return lax.ppermute(value, ("dp", "wide"), over_all(moves))

    stats = call(stats_body, shape((W, 2, channels), F32))(lat)
    stats = lax.all_to_all(stats, "wide", split_axis=0, concat_axis=0, tiled=True)

    halo = lax.ppermute(cot, "wide", [(w + 1, w) for w in range(W - 1)])
    core = lax.rem(lax.axis_index("wide"), 2)
    half_s = lax.dynamic_slice_in_dim(w_spatial, core * (shard_s // 2), shard_s // 2, 0)
    half_t = lax.dynamic_slice_in_dim(w_temporal, core * (shard_t // 2), shard_t // 2, 0)
    pieces, pieces_t = [], []
    for s in range(1, D):
        here_t = send(half_t, lambda d, w: ((d + s) % D, w))
        here_s = send(half_s, lambda d, w: ((d + s) % D, w))
        there_t = send(here_t, lambda d, w: (d, w ^ 1))
        there_s = send(here_s, lambda d, w: (d, w ^ 1))
        pieces += [here_s, here_t, there_s, there_t]
        pieces_t += [here_t, there_t]

    R = shard_s + shard_t
    if aligned:
        grads = [shape((D, channels // 2, R), BF16)] * 2
    else:
        grads = [shape((channels, D * R), BF16), shape((8, 128), BF16)]
    spatial, sums, grad, keep, away = call(
        functools.partial(main_body, sizes),
        [
            shape((rows, channels), BF16),
            shape((W, 2, channels), F32),
            shape((rows, channels), F32),
        ]
        + grads,
        [
            pltpu.VMEM((D * shard_s, channels), BF16),
            pltpu.VMEM((D * shard_t, channels), BF16),
            pltpu.VMEM((3, frames, cells + 2 * cols, channels), BF16),
            pltpu.VMEM((3, frames, cells + 2 * cols, channels), BF16),
            pltpu.VMEM((channels, rows), BF16),
            pltpu.VMEM((channels, rows + 2 * cells), BF16),
        ],
        flops=2 * 33 * rows * channels * channels,
        moved=5_000_000,
    )(lat, cot, halo, stats, gain, bias, w_spatial, w_temporal, *pieces)

    sums = lax.all_to_all(sums, "wide", split_axis=0, concat_axis=0, tiled=True)
    before = lax.ppermute(spatial, "wide", [(w, w + 1) for w in range(W - 1)])

    def finish():
        return call(
            functools.partial(finish_body, sizes),
            [
                shape((rows, channels), BF16),
                shape((rows, channels), BF16),
                shape((2, channels), F32),
            ],
            [pltpu.VMEM((D * shard_t, channels), BF16)],
            flops=2 * 3 * rows * channels * channels,
            moved=2_000_000,
        )(lat, cot, stats, gain, grad, sums, spatial, before, w_temporal, *pieces_t)

    width = channels // W
    if aligned:
        Z = W // 4
        got = send(away, lambda d, w: (d, w ^ 1))
        view = (D, Z, 2, width, R)
        plane = call(
            functools.partial(plane_body, sizes),
            [shape((Z, width, R), BF16)] * (2 * D),
            moved=5_000_000,
        )(keep.reshape(view), got.reshape(view))
        terms, at = [plane[0]], 0
        for a in range(D):
            for b in range(2):
                if at > 0:
                    terms.append(
                        send(plane[at], lambda d, w: ((d + a) % D, w ^ (2 * b)))
                    )
                at += 1
        block_out, grad_latents, norm = finish()
        norms = [norm] + [send(norm, lambda d, w: ((d + s) % D, w)) for s in range(1, D)]
        line = call(
            functools.partial(line_body, Z),
            [shape((width, R), BF16)] * Z,
            moved=1_000_000,
        )(*terms)
        terms = [line[0]]
        for s in range(1, Z):
            terms.append(send(line[s], lambda d, w: (d, (w + 4 * s) % W)))
        grad_s, grad_t, norm = call(
            functools.partial(last_body, scale, shard_s, len(terms)),
            [
                shape((width, shard_s), F32),
                shape((width, shard_t), F32),
                shape((2, width), F32),
            ],
        )(*terms, *norms)
        grad_s, grad_t = grad_s.T, grad_t.T
    else:
        block_out, grad_latents, norm = finish()
        norms = [norm] + [send(norm, lambda d, w: ((d + s) % D, w)) for s in range(1, D)]
        norm = call(functools.partial(only_norm_body, scale), shape((2, width), F32))(*norms)
        part = lax.psum_scatter(keep.astype(F32), "wide", scatter_dimension=0, tiled=True)
        part = part.T.astype(BF16)
        grad_s, grad_t = (
            lax.psum_scatter(term, "dp", scatter_dimension=0, tiled=True).astype(F32) * scale
            for term in (part[: D * shard_s], part[D * shard_s :])
        )
    return (
        block_out.reshape(latents.shape),
        grad_latents.reshape(latents.shape),
        grad_s,
        grad_t,
        norm,
    )


def solution(mesh):
    return jax.shard_map(
        local,
        mesh=mesh,
        in_specs=(
            P("dp", "wide", None, None, None),
            P("dp", "wide", None, None, None),
            P(),
            P(),
            P("dp", None),
            P("dp", None),
        ),
        out_specs=(
            P("dp", "wide", None, None, None),
            P("dp", "wide", None, None, None),
            P("dp", "wide"),
            P("dp", "wide"),
            P(None, "wide"),
        ),
        check_vma=False,
    )
```

```python
import functools
import math

import jax
import jax.numpy as jnp
from jax import lax
from jax.experimental import pallas as pl
from jax.experimental.pallas import tpu as pltpu
from jax.sharding import PartitionSpec as P

GROUPS = 32
EPSILON = 1e-05
F32 = jnp.float32
BF16 = jnp.bfloat16
VMEM = pl.BlockSpec(memory_space=pltpu.VMEM)
ANY = pl.BlockSpec(memory_space=pl.ANY)
NT = (((1,), (1,)), ((), ()))
NN = (((1,), (0,)), ((), ()))


def call(body, out_shapes, scratch=(), flops=0, moved=0, in_specs=None, out_specs=None):
    many = isinstance(out_shapes, (tuple, list))

    def run(*operands):
        return pl.pallas_call(
            body,
            out_shape=out_shapes,
            in_specs=in_specs or [VMEM] * len(operands),
            out_specs=out_specs or ([VMEM] * len(out_shapes) if many else VMEM),
            scratch_shapes=list(scratch),
            compiler_params=pltpu.CompilerParams(vmem_limit_bytes=40 * 1024 * 1024),
            cost_estimate=pl.CostEstimate(
                flops=flops, bytes_accessed=moved, transcendentals=0
            ),
        )(*operands)

    return run


def shape(dims, kind):
    return jax.ShapeDtypeStruct(dims, kind)


def mm(left, right, dims=NN):
    return lax.dot_general(left, right, dims, preferred_element_type=F32)


def group_total(rows, per_group):
    channels = rows.shape[-1]
    first = lax.broadcasted_iota(jnp.int32, (channels, channels), 0) // per_group
    second = lax.broadcasted_iota(jnp.int32, (channels, channels), 1) // per_group
    same = (first == second).astype(F32)
    return lax.dot_general(
        rows, same, NN, precision=lax.Precision.HIGHEST, preferred_element_type=F32
    )


def stats_body(lat_ref, ws_ref, wt_ref, out_ref, half_s_ref, half_t_ref, sem):
    core = lax.rem(lax.axis_index("wide"), 2)
    copies = []
    for at, (source, target) in enumerate(((wt_ref, half_t_ref), (ws_ref, half_s_ref))):
        half = target.shape[0]
        start = pl.multiple_of(core * half, 16)
        copies.append(
            pltpu.make_async_copy(source.at[pl.ds(start, half)], target, sem.at[at])
        )
        copies[-1].start()
    x = lat_ref[...].astype(F32)
    both = jnp.concatenate(
        [jnp.sum(x, axis=0, keepdims=True), jnp.sum(x * x, axis=0, keepdims=True)], axis=0
    )
    out_ref[...] = jnp.broadcast_to(both[None], out_ref.shape)
    for copy in copies:
        copy.wait()


def whiten(lat, stats, count, per_group):
    total = group_total(jnp.sum(stats, axis=0), per_group) / count
    mean = total[0:1]
    inv_std = 1.0 / jnp.sqrt(total[1:2] - mean * mean + EPSILON)
    return (lat.astype(F32) - mean) * inv_std, inv_std


def store_shifted(pad_ref, values, frames, cells, cols):
    total = frames * cells
    column = lax.broadcasted_iota(jnp.int32, (total, 1), 0) % cols
    left = jnp.where(column == 0, 0.0, pltpu.roll(values, 1, 0))
    right = jnp.where(column == cols - 1, 0.0, pltpu.roll(values, total - 1, 0))
    edge = jnp.zeros((cols, values.shape[1]), BF16)
    for at, form in enumerate((left, values, right)):
        low = form.astype(BF16)
        for f in range(frames):
            pad_ref[at, f, 0:cols] = edge
            pad_ref[at, f, cols : cols + cells] = low[f * cells : (f + 1) * cells]
            pad_ref[at, f, cols + cells :] = edge


def window(pad_ref, dy, dx, frames, cells, cols):
    return jnp.concatenate(
        [pad_ref[dx, f, dy * cols : dy * cols + cells] for f in range(frames)], axis=0
    )


def fill_weights(full, shard_ref, pieces, D, d, core):
    n = shard_ref.shape[0]
    full[pl.ds(pl.multiple_of(d * n, 16), n)] = shard_ref[...]
    for s in range(1, D):
        source = lax.rem(d + D - s, D)
        for which in range(2):
            holder = core if which == 0 else 1 - core
            start = pl.multiple_of(source * n + holder * (n // 2), 16)
            full[pl.ds(start, n // 2)] = pieces[2 * (s - 1) + which][...]


def core_order(transposed_ref, W, core):
    step = transposed_ref.shape[0] // W
    order = [(2 * j + core) * step for j in range(W // 2)]
    order += [(2 * j + 1 - core) * step for j in range(W // 2)]
    return jnp.concatenate(
        [transposed_ref[pl.ds(pl.multiple_of(at, 16), step)] for at in order], axis=0
    )


def put(block, column, shard, keep_ref, send_ref):
    low = block.astype(BF16)
    if send_ref is None:
        keep_ref[:, column : column + block.shape[1]] = low
        return
    half = block.shape[0] // 2
    for at in range(0, block.shape[1], 128):
        owner, place = (column + at) // shard, (column + at) % shard
        keep_ref[owner, :, place : place + 128] = low[:half, at : at + 128]
        send_ref[owner, :, place : place + 128] = low[half:, at : at + 128]


def normalise(lat_ref, stats_ref, gain_ref, bias_ref, count, per_group):
    white, inv_std = whiten(lat_ref[...], stats_ref[...], count, per_group)
    normed = white * gain_ref[...] + bias_ref[...]
    return white, normed, jax.nn.sigmoid(normed)


def first_body(sizes, lat_ref, cot_ref, halo_ref, stats_ref, gain_ref, bias_ref, wt_ref, *rest):
    D, W, frames, cells, cols, count, per_group, aligned = sizes
    pieces, rest = rest[: 2 * (D - 1)], rest[2 * (D - 1) :]
    full_wt, act_pad, gsa_t = rest[-3:]
    gsa_ref, keep_ref = rest[:2]
    send_ref = rest[2] if aligned else None
    channels = lat_ref.shape[1]
    d = lax.axis_index("dp")
    core = lax.rem(lax.axis_index("wide"), 2)
    fill_weights(full_wt, wt_ref, pieces, D, d, core)
    rows = frames * cells
    extended = jnp.concatenate([cot_ref[...], halo_ref[...]], axis=0)
    gsa = jnp.zeros((rows, channels), F32)
    for k in range(3):
        gsa += mm(
            extended[k * cells : k * cells + rows],
            full_wt[k * channels : (k + 1) * channels],
            NT,
        )
    gsa_ref[...] = gsa.astype(BF16)
    gsa_t[...] = gsa.astype(BF16).astype(F32).T.astype(BF16)
    _, normed, sig = normalise(lat_ref, stats_ref, gain_ref, bias_ref, count, per_group)
    act = (normed * sig).astype(BF16).astype(F32)
    store_shifted(act_pad, act, frames, cells, cols)
    left = core_order(gsa_t, W, core) if aligned else gsa_t[...]
    shard = wt_ref.shape[0] * 3
    for dy in range(3):
        for dx in range(3):
            seen = window(act_pad, dy, dx, frames, cells, cols)
            put(mm(left, seen), (3 * dy + dx) * channels, shard, keep_ref, send_ref)


def second_body(
    sizes, lat_ref, cot_ref, halo_ref, stats_ref, gain_ref, bias_ref, gsa_ref, ws_ref, *rest
):
    D, W, frames, cells, cols, count, per_group, aligned = sizes
    pieces, rest = rest[: 2 * (D - 1)], rest[2 * (D - 1) :]
    full_ws, act_pad, gsa_pad, cot_t = rest[-4:]
    spatial_ref, sums_ref, grad_ref, keep_ref = rest[:4]
    send_ref = rest[4] if aligned else None
    channels = lat_ref.shape[1]
    d = lax.axis_index("dp")
    core = lax.rem(lax.axis_index("wide"), 2)
    fill_weights(full_ws, ws_ref, pieces, D, d, core)
    rows = frames * cells
    white, normed, sig = normalise(lat_ref, stats_ref, gain_ref, bias_ref, count, per_group)
    act = (normed * sig).astype(BF16).astype(F32)
    store_shifted(act_pad, act, frames, cells, cols)
    store_shifted(gsa_pad, gsa_ref[...].astype(F32), frames, cells, cols)
    extended = jnp.concatenate([cot_ref[...], halo_ref[...]], axis=0)
    for f in range(frames + 2):
        cot_t[:, f * cells : (f + 1) * cells] = (
            extended[f * cells : (f + 1) * cells].astype(F32).T.astype(BF16)
        )
    left = core_order(cot_t, W, core) if aligned else cot_t[...]
    out = jnp.zeros((rows, channels), F32)
    for dy in range(3):
        for dx in range(3):
            tap = 3 * dy + dx
            seen = window(act_pad, dy, dx, frames, cells, cols)
            out += mm(seen, full_ws[tap * channels : (tap + 1) * channels])
    spatial = out.astype(BF16)
    spatial_ref[...] = spatial
    shard = ws_ref.shape[0] // 3
    for k in range(3):
        block = mm(left[:, k * cells : k * cells + rows], spatial)
        put(block, k * channels, shard, keep_ref, send_ref)

    grad = jnp.zeros((rows, channels), F32)
    for dy in range(3):
        for dx in range(3):
            tap = 3 * dy + dx
            seen = window(gsa_pad, 2 - dy, 2 - dx, frames, cells, cols)
            grad += mm(seen, full_ws[tap * channels : (tap + 1) * channels], NT)
    grad = grad * (sig * (1.0 + normed * (1.0 - sig)))
    grad_ref[...] = grad
    both = jnp.concatenate(
        [
            jnp.sum(grad * white, axis=0, keepdims=True),
            jnp.sum(grad, axis=0, keepdims=True),
        ],
        axis=0,
    )
    sums_ref[...] = jnp.broadcast_to(both[None], sums_ref.shape)


def finish_body(
    sizes,
    lat_ref,
    cot_ref,
    stats_ref,
    gain_ref,
    grad_ref,
    sums_ref,
    spatial_ref,
    before_ref,
    wt_ref,
    *rest,
):
    D, W, frames, cells, cols, count, per_group, aligned = sizes
    pieces = rest[: 2 * (D - 1)]
    block_ref, glat_ref, norm_ref, full_wt = rest[2 * (D - 1) :]
    channels = lat_ref.shape[1]
    d = lax.axis_index("dp")
    core = lax.rem(lax.axis_index("wide"), 2)
    fill_weights(full_wt, wt_ref, pieces, D, d, core)
    extended = jnp.concatenate([before_ref[...], spatial_ref[...]], axis=0)
    rows = frames * cells
    temporal = jnp.zeros((rows, channels), F32)
    for k in range(3):
        start = (2 - k) * cells
        temporal += mm(
            extended[start : start + rows], full_wt[k * channels : (k + 1) * channels]
        )
    lat = lat_ref[...]
    block_ref[...] = (lat.astype(F32) + temporal).astype(BF16)

    white, inv_std = whiten(lat, stats_ref[...], count, per_group)
    gain = gain_ref[...]
    total = jnp.sum(sums_ref[...], axis=0)
    norm_ref[...] = total
    means = group_total(total * gain, per_group) / count
    inner = inv_std * (grad_ref[...] * gain - means[1:2] - white * means[0:1])
    glat_ref[...] = (cot_ref[...].astype(F32) + inner).astype(BF16)


def plane_body(keep_ref, got_ref, out_ref):
    for a in range(keep_ref.shape[0]):
        for b in range(2):
            out_ref[2 * a + b] = (
                keep_ref[a, :, b].astype(F32) + got_ref[a, :, b].astype(F32)
            ).astype(BF16)


def sum_body(scale, terms_ref, out_ref):
    total = terms_ref[0].astype(F32)
    for at in range(1, terms_ref.shape[0]):
        total += terms_ref[at].astype(F32)
    if scale is not None:
        total = total * scale
    out_ref[...] = total.astype(out_ref.dtype)


def norm_columns(scale, terms, norm_ref):
    norm = terms[0][...]
    for term in terms[1:]:
        norm += term[...]
    channels, width = norm.shape[1], norm_ref.shape[1]
    row = lax.broadcasted_iota(jnp.int32, (channels, width), 0)
    column = lax.broadcasted_iota(jnp.int32, (channels, width), 1)
    pick = (row == column + lax.axis_index("wide") * width).astype(F32)
    norm_ref[...] = (
        lax.dot_general(
            norm, pick, NN, precision=lax.Precision.HIGHEST, preferred_element_type=F32
        )
        * scale
    )


def only_norm_body(scale, *refs):
    norm_columns(scale, refs[:-1], refs[-1])


def local(latents, cotangent, norm_gain, norm_bias, w_spatial, w_temporal):
    D, W = lax.axis_size("dp"), lax.axis_size("wide")
    _, frames, rows_here, cols, channels = latents.shape
    cells = rows_here * cols
    rows = frames * cells
    per_group = channels // GROUPS
    count = W * frames * cells * per_group
    shard_s, shard_t = w_spatial.shape[0], w_temporal.shape[0]
    aligned = (channels // W) % 16 == 0 and shard_s % 128 == 0 and shard_t % 128 == 0
    aligned = aligned and W % 4 == 0
    sizes = (D, W, frames, cells, cols, count, per_group, aligned)
    scale = 1.0 / math.sqrt(D * W * frames * cells)

    lat, cot = latents.reshape(rows, channels), cotangent.reshape(rows, channels)
    gain, bias = norm_gain.reshape(1, channels), norm_bias.reshape(1, channels)

    def over_all(moves):
        pairs = []
        for d in range(D):
            for w in range(W):
                to = moves(d, w)
                pairs.append((d * W + w, to[0] * W + to[1]))
        return pairs

    def send(value, moves):
        return lax.ppermute(value, ("dp", "wide"), over_all(moves))

    half_s, half_t = shard_s // 2, shard_t // 2
    stats, half_s, half_t = call(
        stats_body,
        [
            shape((W, 2, channels), F32),
            shape((half_s, channels), BF16),
            shape((half_t, channels), BF16),
        ],
        [pltpu.SemaphoreType.DMA((2,))],
        in_specs=[VMEM, ANY, ANY],
        out_specs=[VMEM, ANY, ANY],
    )(lat, w_spatial, w_temporal)
    stats = lax.all_to_all(stats, "wide", split_axis=0, concat_axis=0, tiled=True)

    halo = lax.ppermute(cot, "wide", [(w + 1, w) for w in range(W - 1)])
    pieces_s, pieces_t = [], []
    for s in range(1, D):
        here_t = send(half_t, lambda d, w: ((d + s) % D, w))
        here_s = send(half_s, lambda d, w: ((d + s) % D, w))
        there_t = send(here_t, lambda d, w: (d, w ^ 1))
        there_s = send(here_s, lambda d, w: (d, w ^ 1))
        pieces_s += [here_s, there_s]
        pieces_t += [here_t, there_t]

    def terms(shard):
        if aligned:
            return [shape((D, channels // 2, shard), BF16)] * 2
        return [shape((channels, D * shard), BF16)]

    pad = pltpu.VMEM((3, frames, cells + 2 * cols, channels), BF16)
    gsa, *grads_s = call(
        functools.partial(first_body, sizes),
        [shape((rows, channels), BF16)] + terms(shard_s),
        [pltpu.VMEM((D * shard_t, channels), BF16), pad, pltpu.VMEM((channels, rows), BF16)],
        flops=2 * 12 * rows * channels * channels,
        moved=3_000_000,
    )(lat, cot, halo, stats, gain, bias, w_temporal, *pieces_t)
    spatial, sums, grad, *grads_t = call(
        functools.partial(second_body, sizes),
        [
            shape((rows, channels), BF16),
            shape((W, 2, channels), F32),
            shape((rows, channels), F32),
        ]
        + terms(shard_t),
        [
            pltpu.VMEM((D * shard_s, channels), BF16),
            pad,
            pad,
            pltpu.VMEM((channels, rows + 2 * cells), BF16),
        ],
        flops=2 * 21 * rows * channels * channels,
        moved=3_000_000,
    )(lat, cot, halo, stats, gain, bias, gsa, w_spatial, *pieces_s)

    sums = lax.all_to_all(sums, "wide", split_axis=0, concat_axis=0, tiled=True)
    before = lax.ppermute(spatial, "wide", [(w, w + 1) for w in range(W - 1)])

    width = channels // W
    Z = W // 4

    def reduced(keep, away, shard):
        got = send(away, lambda d, w: (d, w ^ 1))
        view = (D, Z, 2, width, shard)
        plane = call(plane_body, shape((2 * D, Z, width, shard), BF16), moved=3_000_000)(
            keep.reshape(view), got.reshape(view)
        )
        groups = [
            [d * W + z * 4 + y * 2 + core for d in range(D) for y in range(2)]
            for z in range(Z)
            for core in range(2)
        ]
        plane = lax.all_to_all(
            plane,
            ("dp", "wide"),
            split_axis=0,
            concat_axis=0,
            axis_index_groups=groups,
            tiled=True,
        )
        line = call(
            functools.partial(sum_body, None), shape((Z, width, shard), BF16), moved=1_000_000
        )(plane)
        groups = [
            [d * W + z * 4 + at for z in range(Z)] for d in range(D) for at in range(4)
        ]
        line = lax.all_to_all(
            line,
            ("dp", "wide"),
            split_axis=0,
            concat_axis=0,
            axis_index_groups=groups,
            tiled=True,
        )
        return call(
            functools.partial(sum_body, scale), shape((width, shard), F32), moved=300_000
        )(line).T

    if aligned:
        grad_s = reduced(*grads_s, shard_s)
        grad_t = reduced(*grads_t, shard_t)
    else:
        outs = []
        for (full,) in (grads_s, grads_t):
            part = lax.psum_scatter(
                full.astype(F32), "wide", scatter_dimension=0, tiled=True
            ).T.astype(BF16)
            part = lax.psum_scatter(part, "dp", scatter_dimension=0, tiled=True)
            outs.append(part.astype(F32) * scale)
        grad_s, grad_t = outs

    block_out, grad_latents, norm = call(
        functools.partial(finish_body, sizes),
        [
            shape((rows, channels), BF16),
            shape((rows, channels), BF16),
            shape((2, channels), F32),
        ],
        [pltpu.VMEM((D * shard_t, channels), BF16)],
        flops=2 * 3 * rows * channels * channels,
        moved=2_000_000,
    )(lat, cot, stats, gain, grad, sums, spatial, before, w_temporal, *pieces_t)
    norms = [norm] + [send(norm, lambda d, w: ((d + s) % D, w)) for s in range(1, D)]
    norm = call(functools.partial(only_norm_body, scale), shape((2, width), F32))(*norms)
    return (
        block_out.reshape(latents.shape),
        grad_latents.reshape(latents.shape),
        grad_s,
        grad_t,
        norm,
    )


def solution(mesh):
    return jax.shard_map(
        local,
        mesh=mesh,
        in_specs=(
            P("dp", "wide", None, None, None),
            P("dp", "wide", None, None, None),
            P(),
            P(),
            P("dp", None),
            P("dp", None),
        ),
        out_specs=(
            P("dp", "wide", None, None, None),
            P("dp", "wide", None, None, None),
            P("dp", "wide"),
            P("dp", "wide"),
            P(None, "wide"),
        ),
        check_vma=False,
    )
```

```python
import functools
import math

import jax
import jax.numpy as jnp
from jax import lax
from jax.experimental import pallas as pl
from jax.experimental.pallas import tpu as pltpu
from jax.sharding import PartitionSpec as P

GROUPS = 32
EPSILON = 1e-05
F32 = jnp.float32
BF16 = jnp.bfloat16
VMEM = pl.BlockSpec(memory_space=pltpu.VMEM)
HBM = pl.BlockSpec(memory_space=pltpu.HBM)
NT = (((1,), (1,)), ((), ()))
NN = (((1,), (0,)), ((), ()))


def call(body, out_shapes, scratch=(), flops=0, moved=0, in_specs=None, out_specs=None):
    many = isinstance(out_shapes, (tuple, list))

    def run(*operands):
        return pl.pallas_call(
            body,
            out_shape=out_shapes,
            in_specs=in_specs or [VMEM] * len(operands),
            out_specs=out_specs or ([VMEM] * len(out_shapes) if many else VMEM),
            scratch_shapes=list(scratch),
            compiler_params=pltpu.CompilerParams(vmem_limit_bytes=40 * 1024 * 1024),
            cost_estimate=pl.CostEstimate(
                flops=flops, bytes_accessed=moved, transcendentals=0
            ),
        )(*operands)

    return run


def shape(dims, kind):
    return jax.ShapeDtypeStruct(dims, kind)


def mm(left, right, dims=NN):
    return lax.dot_general(left, right, dims, preferred_element_type=F32)


def group_total(rows, per_group):
    channels = rows.shape[-1]
    first = lax.broadcasted_iota(jnp.int32, (channels, channels), 0) // per_group
    second = lax.broadcasted_iota(jnp.int32, (channels, channels), 1) // per_group
    same = (first == second).astype(F32)
    return lax.dot_general(
        rows, same, NN, precision=lax.Precision.HIGHEST, preferred_element_type=F32
    )


def stats_body(lat_ref, ws_ref, wt_ref, out_ref, half_ref, sem):
    core = lax.rem(lax.axis_index("wide"), 2)
    copies, place = [], 0
    for at, source in enumerate((ws_ref, wt_ref)):
        half = source.shape[0] // 2
        start = pl.multiple_of(core * half, 16)
        copies.append(
            pltpu.make_async_copy(
                source.at[pl.ds(start, half)], half_ref.at[pl.ds(place, half)], sem.at[at]
            )
        )
        copies[-1].start()
        place += half
    x = lat_ref[...].astype(F32)
    both = jnp.concatenate(
        [jnp.sum(x, axis=0, keepdims=True), jnp.sum(x * x, axis=0, keepdims=True)], axis=0
    )
    out_ref[...] = jnp.broadcast_to(both[None], out_ref.shape)
    for copy in copies:
        copy.wait()


def fill_weights(full, shard_ref, pieces, offset, D):
    d = lax.axis_index("dp")
    core = lax.rem(lax.axis_index("wide"), 2)
    n = shard_ref.shape[0]
    half = n // 2
    full[pl.ds(pl.multiple_of(d * n, 16), n)] = shard_ref[...]
    for s in range(1, D):
        source = lax.rem(d + D - s, D)
        for which in range(2):
            holder = core if which == 0 else 1 - core
            start = pl.multiple_of(source * n + holder * half, 16)
            full[pl.ds(start, half)] = pieces[2 * (s - 1) + which][offset : offset + half]


def whiten(lat, stats, count, per_group):
    total = group_total(jnp.sum(stats, axis=0), per_group) / count
    mean = total[0:1]
    inv_std = 1.0 / jnp.sqrt(total[1:2] - mean * mean + EPSILON)
    return (lat.astype(F32) - mean) * inv_std, inv_std


def store_shifted(pad_ref, values, frames, cells, cols):
    total = frames * cells
    column = lax.broadcasted_iota(jnp.int32, (total, 1), 0) % cols
    left = jnp.where(column == 0, 0.0, pltpu.roll(values, 1, 0))
    right = jnp.where(column == cols - 1, 0.0, pltpu.roll(values, total - 1, 0))
    edge = jnp.zeros((cols, values.shape[1]), BF16)
    for at, form in enumerate((left, values, right)):
        low = form.astype(BF16)
        for f in range(frames):
            pad_ref[at, f, 0:cols] = edge
            pad_ref[at, f, cols : cols + cells] = low[f * cells : (f + 1) * cells]
            pad_ref[at, f, cols + cells :] = edge


def window(pad_ref, dy, dx, frames, cells, cols):
    return jnp.concatenate(
        [pad_ref[dx, f, dy * cols : dy * cols + cells] for f in range(frames)], axis=0
    )


def main_body(
    sizes,
    lat_ref,
    cot_ref,
    halo_ref,
    stats_ref,
    gain_ref,
    bias_ref,
    ws_ref,
    wt_ref,
    *rest,
):
    D, W, frames, cells, cols, count, per_group, aligned = sizes
    pieces, rest = rest[: 2 * (D - 1)], rest[2 * (D - 1) :]
    spatial_ref, sums_ref, grad_ref, keep_ref, send_ref = rest[:5]
    full_ws, full_wt, act_pad, gsa_pad, gsa_t, cot_t = rest[5:]
    channels = lat_ref.shape[1]
    core = lax.rem(lax.axis_index("wide"), 2)

    fill_weights(full_ws, ws_ref, pieces, 0, D)
    fill_weights(full_wt, wt_ref, pieces, ws_ref.shape[0] // 2, D)

    cot = cot_ref[...]
    extended = jnp.concatenate([cot, halo_ref[...]], axis=0)
    rows = frames * cells
    gsa = jnp.zeros((rows, channels), F32)
    for k in range(3):
        gsa += mm(
            extended[k * cells : k * cells + rows],
            full_wt[k * channels : (k + 1) * channels],
            NT,
        )
    gsa = gsa.astype(BF16).astype(F32)
    store_shifted(gsa_pad, gsa, frames, cells, cols)

    white, _ = whiten(lat_ref[...], stats_ref[...], count, per_group)
    gain = gain_ref[...]
    normed = white * gain + bias_ref[...]
    sig = jax.nn.sigmoid(normed)
    act = (normed * sig).astype(BF16).astype(F32)
    store_shifted(act_pad, act, frames, cells, cols)

    gsa_t[...] = gsa.T.astype(BF16)
    for f in range(frames + 2):
        cot_t[:, f * cells : (f + 1) * cells] = (
            extended[f * cells : (f + 1) * cells].astype(F32).T.astype(BF16)
        )
    if aligned:
        step = channels // W
        order = [pl.ds(pl.multiple_of((2 * j + core) * step, 16), step) for j in range(W // 2)]
        order += [
            pl.ds(pl.multiple_of((2 * j + 1 - core) * step, 16), step) for j in range(W // 2)
        ]
        left_s = jnp.concatenate([gsa_t[at] for at in order], axis=0)
        left_t = jnp.concatenate([cot_t[at] for at in order], axis=0)
    else:
        left_s, left_t = gsa_t[...], cot_t[...]

    def put(block, column, shard, offset):
        if not aligned:
            keep_ref[:, offset + column : offset + column + channels] = block.astype(BF16)
            return
        low = block.astype(BF16)
        half = channels // 2
        for at in range(0, channels, 128):
            owner, place = (column + at) // shard, (column + at) % shard + offset
            keep_ref[owner, :, place : place + 128] = low[:half, at : at + 128]
            send_ref[owner, :, place : place + 128] = low[half:, at : at + 128]

    shard_s, shard_t = ws_ref.shape[0], wt_ref.shape[0]
    out = jnp.zeros((rows, channels), F32)
    for dy in range(3):
        for dx in range(3):
            tap = 3 * dy + dx
            seen = window(act_pad, dy, dx, frames, cells, cols)
            out += mm(seen, full_ws[tap * channels : (tap + 1) * channels])
            put(mm(left_s, seen), tap * channels, shard_s, 0)
    spatial = out.astype(BF16)
    spatial_ref[...] = spatial
    for k in range(3):
        put(
            mm(left_t[:, k * cells : k * cells + rows], spatial),
            k * channels,
            shard_t,
            shard_s if aligned else shard_s * D,
        )

    grad = jnp.zeros((rows, channels), F32)
    for dy in range(3):
        for dx in range(3):
            tap = 3 * dy + dx
            seen = window(gsa_pad, 2 - dy, 2 - dx, frames, cells, cols)
            grad += mm(seen, full_ws[tap * channels : (tap + 1) * channels], NT)
    grad = grad * (sig * (1.0 + normed * (1.0 - sig)))
    grad_ref[...] = grad
    both = jnp.concatenate(
        [
            jnp.sum(grad * white, axis=0, keepdims=True),
            jnp.sum(grad, axis=0, keepdims=True),
        ],
        axis=0,
    )
    sums_ref[...] = jnp.broadcast_to(both[None], sums_ref.shape)


def finish_body(
    sizes,
    lat_ref,
    cot_ref,
    stats_ref,
    gain_ref,
    grad_ref,
    sums_ref,
    spatial_ref,
    before_ref,
    wt_ref,
    *rest,
):
    D, W, frames, cells, cols, count, per_group, aligned = sizes
    pieces = rest[: 2 * (D - 1)]
    block_ref, glat_ref, norm_ref, full_wt = rest[2 * (D - 1) :]
    channels = lat_ref.shape[1]
    fill_weights(full_wt, wt_ref, pieces, pieces[0].shape[0] - wt_ref.shape[0] // 2, D)
    extended = jnp.concatenate([before_ref[...], spatial_ref[...]], axis=0)
    rows = frames * cells
    temporal = jnp.zeros((rows, channels), F32)
    for k in range(3):
        start = (2 - k) * cells
        temporal += mm(
            extended[start : start + rows], full_wt[k * channels : (k + 1) * channels]
        )
    lat = lat_ref[...]
    block_ref[...] = (lat.astype(F32) + temporal).astype(BF16)

    white, inv_std = whiten(lat, stats_ref[...], count, per_group)
    gain = gain_ref[...]
    d = lax.axis_index("dp")
    total = jnp.sum(sums_ref[pl.ds(d * W, W)], axis=0)
    norm_ref[...] = jnp.sum(sums_ref[...], axis=0)
    means = group_total(total * gain, per_group) / count
    inner = inv_std * (grad_ref[...] * gain - means[1:2] - white * means[0:1])
    glat_ref[...] = (cot_ref[...].astype(F32) + inner).astype(BF16)


def plane_body(sizes, keep_ref, got_ref, *outs):
    D = sizes[0]
    d = lax.axis_index("dp")
    y = lax.rem(lax.axis_index("wide") // 2, 2)
    at = 0
    for a in range(D):
        for b in range(2):
            owner, side = lax.rem(d + a, D), lax.rem(y + b, 2)
            outs[at][...] = (
                keep_ref[owner, :, side].astype(F32) + got_ref[owner, :, side].astype(F32)
            ).astype(BF16)
            at += 1


def line_body(depth, *refs):
    outs = refs[-depth:]
    z = lax.axis_index("wide") // 4
    for s in range(depth):
        owner = lax.rem(z + s, depth)
        total = refs[0][owner].astype(F32)
        for term in refs[1:-depth]:
            total += term[owner].astype(F32)
        outs[s][...] = total.astype(BF16)


def last_body(scale, split, terms, *refs):
    spatial_ref, temporal_ref, norm_ref = refs[-3:]
    total = refs[0][...].astype(F32)
    for term in refs[1:terms]:
        total += term[...].astype(F32)
    total = total * scale
    spatial_ref[...] = total[:, :split]
    temporal_ref[...] = total[:, split:]
    norm_columns(scale, refs[terms], norm_ref)


def norm_columns(scale, term_ref, norm_ref):
    norm = term_ref[...]
    channels, width = norm.shape[1], norm_ref.shape[1]
    row = lax.broadcasted_iota(jnp.int32, (channels, width), 0)
    column = lax.broadcasted_iota(jnp.int32, (channels, width), 1)
    pick = (row == column + lax.axis_index("wide") * width).astype(F32)
    norm_ref[...] = (
        lax.dot_general(
            norm, pick, NN, precision=lax.Precision.HIGHEST, preferred_element_type=F32
        )
        * scale
    )


def only_norm_body(scale, term_ref, norm_ref):
    norm_columns(scale, term_ref, norm_ref)


def local(latents, cotangent, norm_gain, norm_bias, w_spatial, w_temporal):
    D, W = lax.axis_size("dp"), lax.axis_size("wide")
    _, frames, rows_here, cols, channels = latents.shape
    cells = rows_here * cols
    rows = frames * cells
    per_group = channels // GROUPS
    count = W * frames * cells * per_group
    shard_s, shard_t = w_spatial.shape[0], w_temporal.shape[0]
    aligned = (channels // W) % 16 == 0 and shard_s % 128 == 0 and shard_t % 128 == 0
    aligned = aligned and W % 4 == 0
    sizes = (D, W, frames, cells, cols, count, per_group, aligned)
    scale = 1.0 / math.sqrt(D * W * frames * cells)

    lat, cot = latents.reshape(rows, channels), cotangent.reshape(rows, channels)
    gain, bias = norm_gain.reshape(1, channels), norm_bias.reshape(1, channels)

    def over_all(moves):
        pairs = []
        for d in range(D):
            for w in range(W):
                to = moves(d, w)
                pairs.append((d * W + w, to[0] * W + to[1]))
        return pairs

    def send(value, moves):
        return lax.ppermute(value, ("dp", "wide"), over_all(moves))

    R = shard_s + shard_t
    stats, half = call(
        stats_body,
        [shape((W, 2, channels), F32), shape((R // 2, channels), BF16)],
        [pltpu.SemaphoreType.DMA((2,))],
        in_specs=[VMEM, HBM, HBM],
    )(lat, w_spatial, w_temporal)
    firsts = [send(half, lambda d, w: ((d + s) % D, w)) for s in range(1, D)]

    halo = lax.ppermute(cot, "wide", [(w + 1, w) for w in range(W - 1)])
    stats = lax.all_to_all(stats, "wide", split_axis=0, concat_axis=0, tiled=True)
    firsts, stats = lax.optimization_barrier((firsts, stats))
    pieces = []
    for first in firsts:
        pieces += [first, send(first, lambda d, w: (d, w ^ 1))]

    if aligned:
        grads = [shape((D, channels // 2, R), BF16)] * 2
    else:
        grads = [shape((channels, D * R), BF16), shape((8, 128), BF16)]
    spatial, sums, grad, keep, away = call(
        functools.partial(main_body, sizes),
        [
            shape((rows, channels), BF16),
            shape((D * W, 2, channels), F32),
            shape((rows, channels), F32),
        ]
        + grads,
        [
            pltpu.VMEM((D * shard_s, channels), BF16),
            pltpu.VMEM((D * shard_t, channels), BF16),
            pltpu.VMEM((3, frames, cells + 2 * cols, channels), BF16),
            pltpu.VMEM((3, frames, cells + 2 * cols, channels), BF16),
            pltpu.VMEM((channels, rows), BF16),
            pltpu.VMEM((channels, rows + 2 * cells), BF16),
        ],
        flops=2 * 33 * rows * channels * channels,
        moved=5_000_000,
    )(lat, cot, halo, stats, gain, bias, w_spatial, w_temporal, *pieces)

    sums = lax.all_to_all(sums, ("dp", "wide"), split_axis=0, concat_axis=0, tiled=True)
    before = lax.ppermute(spatial, "wide", [(w, w + 1) for w in range(W - 1)])

    def finish():
        return call(
            functools.partial(finish_body, sizes),
            [
                shape((rows, channels), BF16),
                shape((rows, channels), BF16),
                shape((2, channels), F32),
            ],
            [pltpu.VMEM((D * shard_t, channels), BF16)],
            flops=2 * 3 * rows * channels * channels,
            moved=2_000_000,
        )(lat, cot, stats, gain, grad, sums, spatial, before, w_temporal, *pieces)

    width = channels // W
    if aligned:
        Z = W // 4
        got = send(away, lambda d, w: (d, w ^ 1))
        view = (D, Z, 2, width, R)
        plane = call(
            functools.partial(plane_body, sizes),
            [shape((Z, width, R), BF16)] * (2 * D),
            moved=5_000_000,
        )(keep.reshape(view), got.reshape(view))
        terms, at = [plane[0]], 0
        for a in range(D):
            for b in range(2):
                if at > 0:
                    terms.append(
                        send(plane[at], lambda d, w: ((d + a) % D, w ^ (2 * b)))
                    )
                at += 1
        block_out, grad_latents, norm = finish()
        line = call(
            functools.partial(line_body, Z),
            [shape((width, R), BF16)] * Z,
            moved=1_000_000,
        )(*terms)
        terms = [line[0]]
        for s in range(1, Z):
            terms.append(send(line[s], lambda d, w: (d, (w + 4 * s) % W)))
        grad_s, grad_t, norm = call(
            functools.partial(last_body, scale, shard_s, len(terms)),
            [
                shape((width, shard_s), F32),
                shape((width, shard_t), F32),
                shape((2, width), F32),
            ],
        )(*terms, norm)
        grad_s, grad_t = grad_s.T, grad_t.T
    else:
        block_out, grad_latents, norm = finish()
        norm = call(functools.partial(only_norm_body, scale), shape((2, width), F32))(norm)
        part = lax.psum_scatter(keep.astype(F32), "wide", scatter_dimension=0, tiled=True)
        part = part.T.astype(BF16)
        grad_s, grad_t = (
            lax.psum_scatter(term, "dp", scatter_dimension=0, tiled=True).astype(F32) * scale
            for term in (part[: D * shard_s], part[D * shard_s :])
        )
    return (
        block_out.reshape(latents.shape),
        grad_latents.reshape(latents.shape),
        grad_s,
        grad_t,
        norm,
    )


def solution(mesh):
    return jax.shard_map(
        local,
        mesh=mesh,
        in_specs=(
            P("dp", "wide", None, None, None),
            P("dp", "wide", None, None, None),
            P(),
            P(),
            P("dp", None),
            P("dp", None),
        ),
        out_specs=(
            P("dp", "wide", None, None, None),
            P("dp", "wide", None, None, None),
            P("dp", "wide"),
            P("dp", "wide"),
            P(None, "wide"),
        ),
        check_vma=False,
    )
```

```python
import functools
import math

import jax
import jax.numpy as jnp
from jax import lax
from jax.experimental import pallas as pl
from jax.experimental.pallas import tpu as pltpu
from jax.sharding import PartitionSpec as P

GROUPS = 32
EPSILON = 1e-05
F32 = jnp.float32
BF16 = jnp.bfloat16
VMEM = pl.BlockSpec(memory_space=pltpu.VMEM)
HBM = pl.BlockSpec(memory_space=pltpu.HBM)
NT = (((1,), (1,)), ((), ()))
NN = (((1,), (0,)), ((), ()))


def call(body, out_shapes, scratch=(), flops=0, moved=0, in_specs=None, vmem=40):
    many = isinstance(out_shapes, (tuple, list))

    def run(*operands):
        return pl.pallas_call(
            body,
            out_shape=out_shapes,
            in_specs=in_specs or [VMEM] * len(operands),
            out_specs=[VMEM] * len(out_shapes) if many else VMEM,
            scratch_shapes=list(scratch),
            compiler_params=pltpu.CompilerParams(vmem_limit_bytes=vmem * 1024 * 1024),
            cost_estimate=pl.CostEstimate(
                flops=flops, bytes_accessed=moved, transcendentals=0
            ),
        )(*operands)

    return run


def shape(dims, kind):
    return jax.ShapeDtypeStruct(dims, kind)


def mm(left, right, dims=NN):
    return lax.dot_general(left, right, dims, preferred_element_type=F32)


def group_total(rows, per_group):
    channels = rows.shape[-1]
    first = lax.broadcasted_iota(jnp.int32, (channels, channels), 0) // per_group
    second = lax.broadcasted_iota(jnp.int32, (channels, channels), 1) // per_group
    same = (first == second).astype(F32)
    return lax.dot_general(
        rows, same, NN, precision=lax.Precision.HIGHEST, preferred_element_type=F32
    )


def stats_body(lat_ref, gain_ref, bias_ref, ws_ref, wt_ref, out_ref, affine_ref, half_ref, sem):
    core = lax.rem(lax.axis_index("wide"), 2)
    copies, place = [], 0
    for at, source in enumerate((ws_ref, wt_ref)):
        half = source.shape[0] // 2
        start = pl.multiple_of(core * half, 16)
        copies.append(
            pltpu.make_async_copy(
                source.at[pl.ds(start, half)], half_ref.at[pl.ds(place, half)], sem.at[at]
            )
        )
        copies[-1].start()
        place += half
    affine_ref[0:1] = gain_ref[...]
    affine_ref[1:2] = bias_ref[...]
    x = lat_ref[...].astype(F32)
    both = jnp.concatenate(
        [jnp.sum(x, axis=0, keepdims=True), jnp.sum(x * x, axis=0, keepdims=True)], axis=0
    )
    out_ref[...] = jnp.broadcast_to(both[None], out_ref.shape)
    for copy in copies:
        copy.wait()


def fill_weights(full, shard_ref, pieces, offset, D):
    d = lax.axis_index("dp")
    core = lax.rem(lax.axis_index("wide"), 2)
    n = shard_ref.shape[0]
    half = n // 2
    full[pl.ds(pl.multiple_of(d * n, 16), n)] = shard_ref[...]
    for s in range(1, D):
        source = lax.rem(d + D - s, D)
        for which in range(2):
            holder = core if which == 0 else 1 - core
            start = pl.multiple_of(source * n + holder * half, 16)
            full[pl.ds(start, half)] = pieces[2 * (s - 1) + which][offset : offset + half]


def whiten(lat, stats, count, per_group):
    total = group_total(jnp.sum(stats, axis=0), per_group) / count
    mean = total[0:1]
    inv_std = 1.0 / jnp.sqrt(total[1:2] - mean * mean + EPSILON)
    return (lat.astype(F32) - mean) * inv_std, inv_std


def store_shifted(pad_ref, values, frames, cells, cols):
    total = frames * cells
    column = lax.broadcasted_iota(jnp.int32, (total, 1), 0) % cols
    left = jnp.where(column == 0, 0.0, pltpu.roll(values, 1, 0))
    right = jnp.where(column == cols - 1, 0.0, pltpu.roll(values, total - 1, 0))
    edge = jnp.zeros((cols, values.shape[1]), BF16)
    for at, form in enumerate((left, values, right)):
        low = form.astype(BF16)
        for f in range(frames):
            pad_ref[at, f, 0:cols] = edge
            pad_ref[at, f, cols : cols + cells] = low[f * cells : (f + 1) * cells]
            pad_ref[at, f, cols + cells :] = edge


def window(pad_ref, dy, dx, frames, cells, cols):
    return jnp.concatenate(
        [pad_ref[dx, f, dy * cols : dy * cols + cells] for f in range(frames)], axis=0
    )


def in_parts(total):
    high = total.astype(BF16).astype(F32)
    return jnp.concatenate([high, total - high], axis=0).astype(BF16)


def from_parts(terms):
    total = 0.0
    for term in terms:
        wide = term.astype(F32)
        total = total + (wide[0:8] + wide[8:16])
    return total


def add(terms):
    total = terms[0].astype(F32)
    for term in terms[1:]:
        total += term.astype(F32)
    return total


def core_order(transposed_ref, W, core):
    step = transposed_ref.shape[0] // W
    order = [(2 * j + core) * step for j in range(W // 2)]
    order += [(2 * j + 1 - core) * step for j in range(W // 2)]
    return jnp.concatenate(
        [transposed_ref[pl.ds(pl.multiple_of(at, 16), step)] for at in order], axis=0
    )


def put(block, column, shard, keep_ref, send_ref):
    low = block.astype(BF16)
    if send_ref is None:
        keep_ref[:, column : column + block.shape[1]] = low
        return
    half = block.shape[0] // 2
    for at in range(0, block.shape[1], 128):
        owner, place = (column + at) // shard, (column + at) % shard
        keep_ref[owner, :, place : place + 128] = low[:half, at : at + 128]
        send_ref[owner, :, place : place + 128] = low[half:, at : at + 128]


def normalise(lat_ref, stats_ref, affine_ref, count, per_group):
    white, inv_std = whiten(lat_ref[...], stats_ref[...], count, per_group)
    normed = white * affine_ref[0:1] + affine_ref[1:2]
    return white, normed, jax.nn.sigmoid(normed)


def first_body(sizes, lat_ref, cot_ref, halo_ref, stats_ref, affine_ref, wt_ref, *rest):
    D, W, frames, cells, cols, count, per_group, aligned = sizes
    pieces, rest = rest[: 2 * (D - 1)], rest[2 * (D - 1) :]
    full_wt, act_pad, gsa_t = rest[-3:]
    gsa_ref, keep_ref = rest[:2]
    send_ref = rest[2] if aligned else None
    channels = lat_ref.shape[1]
    core = lax.rem(lax.axis_index("wide"), 2)
    fill_weights(full_wt, wt_ref, pieces, pieces[0].shape[0] - wt_ref.shape[0] // 2, D)
    rows = frames * cells
    extended = jnp.concatenate([cot_ref[...], halo_ref[...]], axis=0)
    gsa = jnp.zeros((rows, channels), F32)
    for k in range(3):
        gsa += mm(
            extended[k * cells : k * cells + rows],
            full_wt[k * channels : (k + 1) * channels],
            NT,
        )
    gsa_ref[...] = gsa.astype(BF16)
    gsa_t[...] = gsa.astype(BF16).astype(F32).T.astype(BF16)
    _, normed, sig = normalise(lat_ref, stats_ref, affine_ref, count, per_group)
    act = (normed * sig).astype(BF16).astype(F32)
    store_shifted(act_pad, act, frames, cells, cols)
    left = core_order(gsa_t, W, core) if aligned else gsa_t[...]
    shard = wt_ref.shape[0] * 3
    for dy in range(3):
        for dx in range(3):
            seen = window(act_pad, dy, dx, frames, cells, cols)
            put(mm(left, seen), (3 * dy + dx) * channels, shard, keep_ref, send_ref)


def second_body(
    sizes, lat_ref, cot_ref, halo_ref, stats_ref, affine_ref, gsa_ref, ws_ref, *rest
):
    D, W, frames, cells, cols, count, per_group, aligned = sizes
    pieces, rest = rest[: 2 * (D - 1)], rest[2 * (D - 1) :]
    full_ws, act_pad, gsa_pad, cot_t = rest[-4:]
    spatial_ref, grad_ref, keep_ref, other_ref = rest[:4]
    send_ref = other_ref if aligned else None
    channels = lat_ref.shape[1]
    core = lax.rem(lax.axis_index("wide"), 2)
    fill_weights(full_ws, ws_ref, pieces, 0, D)
    rows = frames * cells
    white, normed, sig = normalise(lat_ref, stats_ref, affine_ref, count, per_group)
    act = (normed * sig).astype(BF16).astype(F32)
    store_shifted(act_pad, act, frames, cells, cols)
    store_shifted(gsa_pad, gsa_ref[...].astype(F32), frames, cells, cols)
    extended = jnp.concatenate([cot_ref[...], halo_ref[...]], axis=0)
    for f in range(frames + 2):
        cot_t[:, f * cells : (f + 1) * cells] = (
            extended[f * cells : (f + 1) * cells].astype(F32).T.astype(BF16)
        )
    left = core_order(cot_t, W, core) if aligned else cot_t[...]
    out = jnp.zeros((rows, channels), F32)
    for dy in range(3):
        for dx in range(3):
            tap = 3 * dy + dx
            seen = window(act_pad, dy, dx, frames, cells, cols)
            out += mm(seen, full_ws[tap * channels : (tap + 1) * channels])
    spatial = out.astype(BF16)
    spatial_ref[...] = spatial
    shard = ws_ref.shape[0] // 3
    for k in range(3):
        block = mm(left[:, k * cells : k * cells + rows], spatial)
        put(block, k * channels, shard, keep_ref, send_ref)

    grad = jnp.zeros((rows, channels), F32)
    for dy in range(3):
        for dx in range(3):
            tap = 3 * dy + dx
            seen = window(gsa_pad, 2 - dy, 2 - dx, frames, cells, cols)
            grad += mm(seen, full_ws[tap * channels : (tap + 1) * channels], NT)
    grad = grad * (sig * (1.0 + normed * (1.0 - sig)))
    grad_ref[...] = grad
    gain_term = jnp.sum(grad * white, axis=0, keepdims=True)
    bias_term = jnp.sum(grad, axis=0, keepdims=True)
    if not aligned:
        both = jnp.concatenate([gain_term, bias_term], axis=0)
        other_ref[...] = jnp.broadcast_to(both[None], other_ref.shape)
        return
    d = lax.axis_index("dp")
    quarter = jnp.concatenate(
        [term[:, at : at + 128] for term in (gain_term, bias_term) for at in (0, 128)], axis=0
    )
    low = in_parts(
        jnp.concatenate([jnp.where(d == s, quarter, 0.0) for s in range(2)], axis=0)
    )
    for target in (keep_ref, send_ref):
        for owner in range(D):
            for at in range(0, channels // 2, 16):
                target[owner, at : at + 16, shard:] = low


def block_body(sizes, lat_ref, spatial_ref, before_ref, wt_ref, *rest):
    D, W, frames, cells, cols, count, per_group, aligned = sizes
    pieces = rest[: 2 * (D - 1)]
    block_ref, full_wt = rest[2 * (D - 1) :]
    channels = lat_ref.shape[1]
    fill_weights(full_wt, wt_ref, pieces, pieces[0].shape[0] - wt_ref.shape[0] // 2, D)
    extended = jnp.concatenate([before_ref[...], spatial_ref[...]], axis=0)
    rows = frames * cells
    temporal = jnp.zeros((rows, channels), F32)
    for k in range(3):
        start = (2 - k) * cells
        temporal += mm(
            extended[start : start + rows], full_wt[k * channels : (k + 1) * channels]
        )
    block_ref[...] = (lat_ref[...].astype(F32) + temporal).astype(BF16)


def latent_gradient(sizes, total, lat_ref, cot_ref, stats_ref, affine_ref, grad_ref):
    D, W, frames, cells, cols, count, per_group, aligned = sizes
    white, inv_std = whiten(lat_ref[...], stats_ref[...], count, per_group)
    gain = affine_ref[0:1]
    means = group_total(total * gain, per_group) / count
    inner = inv_std * (grad_ref[...] * gain - means[1:2] - white * means[0:1])
    return (cot_ref[...].astype(F32) + inner).astype(BF16)


def plane_body(keep_s, got_s, keep_t, got_t, *outs):
    d = lax.axis_index("dp")
    y = lax.rem(lax.axis_index("wide") // 2, 2)
    split = keep_s.shape[-1]
    ride = outs[0].shape[-1] - 128
    for a in range(2):
        for b in range(2):
            owner, side = lax.rem(d + a, 2), lax.rem(y + b, 2)
            out = outs[2 * a + b]
            for z in range(out.shape[0]):
                out[z, :, :split] = add([keep_s[owner, z, side], got_s[owner, z, side]]).astype(
                    BF16
                )
                both = [keep_t[owner, z, side], got_t[owner, z, side]]
                out[z, :, split:ride] = add([t[:, : ride - split] for t in both]).astype(BF16)
                out[z, :, ride:] = in_parts(from_parts([t[:, ride - split :] for t in both]))


def line_body(depth, *refs):
    terms, outs = refs[:4], refs[4:]
    z = lax.axis_index("wide") // 4
    ride = outs[0].shape[-1] - 128
    for s in range(depth):
        owner = lax.rem(z + s, depth)
        seen = [term[owner] for term in terms]
        outs[s][:, :ride] = add([t[:, :ride] for t in seen]).astype(BF16)
        outs[s][:, ride:] = in_parts(from_parts([t[:, ride:] for t in seen]))


def last_body(sizes, scale, depth, *refs):
    terms, operands, outs = refs[:depth], refs[depth:-4], refs[-4:]
    spatial_ref, temporal_ref, norm_ref, glat_ref = outs
    split = spatial_ref.shape[1]
    ride = terms[0].shape[1] - 128
    sums = from_parts([term[:, ride:] for term in terms])

    def rows_of(part):
        return jnp.concatenate(
            [jnp.concatenate([part[at : at + 1], part[at + 1 : at + 2]], axis=1) for at in (0, 2)],
            axis=0,
        )

    first, second = rows_of(sums[0:4]), rows_of(sums[4:8])
    own = jnp.where(lax.axis_index("dp") == 0, first, second)
    glat_ref[...] = latent_gradient(sizes, own, *operands)
    norm_columns(scale, first + second, norm_ref)
    total = add([term[:, :ride] for term in terms]) * scale
    spatial_ref[...] = total[:, :split]
    temporal_ref[...] = total[:, split:]


def apart_body(sizes, scale, sums_ref, *refs):
    norm_ref, glat_ref = refs[-2:]
    W = sizes[1]
    own = jnp.sum(sums_ref[pl.ds(lax.axis_index("dp") * W, W)], axis=0)
    norm_columns(scale, jnp.sum(sums_ref[...], axis=0), norm_ref)
    glat_ref[...] = latent_gradient(sizes, own, *refs[:-2])


def norm_columns(scale, norm, norm_ref):
    channels, width = norm.shape[1], norm_ref.shape[1]
    row = lax.broadcasted_iota(jnp.int32, (channels, width), 0)
    column = lax.broadcasted_iota(jnp.int32, (channels, width), 1)
    pick = (row == column + lax.axis_index("wide") * width).astype(F32)
    norm_ref[...] = (
        lax.dot_general(
            norm, pick, NN, precision=lax.Precision.HIGHEST, preferred_element_type=F32
        )
        * scale
    )


def local(latents, cotangent, norm_gain, norm_bias, w_spatial, w_temporal):
    D, W = lax.axis_size("dp"), lax.axis_size("wide")
    _, frames, rows_here, cols, channels = latents.shape
    cells = rows_here * cols
    rows = frames * cells
    per_group = channels // GROUPS
    count = W * frames * cells * per_group
    shard_s, shard_t = w_spatial.shape[0], w_temporal.shape[0]
    aligned = (channels // W) % 16 == 0 and shard_s % 128 == 0 and shard_t % 128 == 0
    aligned = aligned and W % 4 == 0 and D == 2 and channels == 256
    sizes = (D, W, frames, cells, cols, count, per_group, aligned)
    scale = 1.0 / math.sqrt(D * W * frames * cells)

    lat, cot = latents.reshape(rows, channels), cotangent.reshape(rows, channels)
    gain, bias = norm_gain.reshape(1, channels), norm_bias.reshape(1, channels)

    def over_all(moves):
        pairs = []
        for d in range(D):
            for w in range(W):
                to = moves(d, w)
                pairs.append((d * W + w, to[0] * W + to[1]))
        return pairs

    def send(value, moves):
        return lax.ppermute(value, ("dp", "wide"), over_all(moves))

    R = shard_s + shard_t
    stats, affine, half = call(
        stats_body,
        [
            shape((W, 2, channels), F32),
            shape((2, channels), F32),
            shape((R // 2, channels), BF16),
        ],
        [pltpu.SemaphoreType.DMA((2,))],
        in_specs=[VMEM, VMEM, VMEM, HBM, HBM],
        vmem=60,
    )(lat, gain, bias, w_spatial, w_temporal)
    firsts = [send(half, lambda d, w: ((d + s) % D, w)) for s in range(1, D)]

    halo = lax.ppermute(cot, "wide", [(w + 1, w) for w in range(W - 1)])
    stats = lax.all_to_all(stats, "wide", split_axis=0, concat_axis=0, tiled=True)
    firsts, stats, halo = lax.optimization_barrier((firsts, stats, halo))
    pieces = []
    for first in firsts:
        pieces += [first, send(first, lambda d, w: (d, w ^ 1))]

    ride = 128 if aligned else 0
    if aligned:
        terms_s = [shape((D, channels // 2, shard_s), BF16)] * 2
        terms_t = [shape((D, channels // 2, shard_t + ride), BF16)] * 2
    else:
        terms_s = [shape((channels, D * shard_s), BF16)]
        terms_t = [shape((channels, D * shard_t), BF16), shape((D * W, 2, channels), F32)]
    pad = pltpu.VMEM((3, frames, cells + 2 * cols, channels), BF16)
    gsa, *grads_s = call(
        functools.partial(first_body, sizes),
        [shape((rows, channels), BF16)] + terms_s,
        [pltpu.VMEM((D * shard_t, channels), BF16), pad, pltpu.VMEM((channels, rows), BF16)],
        flops=2 * 12 * rows * channels * channels,
        moved=3_000_000,
    )(lat, cot, halo, stats, affine, w_temporal, *pieces)
    spatial, grad, *grads_t = call(
        functools.partial(second_body, sizes),
        [shape((rows, channels), BF16), shape((rows, channels), F32)] + terms_t,
        [
            pltpu.VMEM((D * shard_s, channels), BF16),
            pad,
            pad,
            pltpu.VMEM((channels, rows + 2 * cells), BF16),
        ],
        flops=2 * 21 * rows * channels * channels,
        moved=3_000_000,
    )(lat, cot, halo, stats, affine, gsa, w_spatial, *pieces)
    before = lax.ppermute(spatial, "wide", [(w, w + 1) for w in range(W - 1)])
    block_out = call(
        functools.partial(block_body, sizes),
        shape((rows, channels), BF16),
        [pltpu.VMEM((D * shard_t, channels), BF16)],
        flops=2 * 3 * rows * channels * channels,
        moved=1_000_000,
    )(lat, spatial, before, w_temporal, *pieces)

    width = channels // W
    operands = (lat, cot, stats, affine, grad)
    if aligned:
        Z = W // 4

        def over_core(away):
            return send(away, lambda d, w: (d, w ^ 1))

        pairs = []
        for keep, away in (grads_s, grads_t):
            view = (D, Z, 2, width, keep.shape[-1])
            pairs += [keep.reshape(view), over_core(away).reshape(view)]
        plane = call(
            plane_body, [shape((Z, width, R + ride), BF16)] * (2 * D), moved=3_000_000
        )(*pairs)
        seen = [plane[0]] + [
            send(plane[2 * a + b], lambda d, w: ((d + a) % D, w ^ (2 * b)))
            for a, b in ((0, 1), (1, 0), (1, 1))
        ]
        line = call(
            functools.partial(line_body, Z),
            [shape((width, R + ride), BF16)] * Z,
            moved=1_000_000,
        )(*seen)
        terms = [line[0]]
        for s in range(1, Z):
            terms.append(send(line[s], lambda d, w: (d, (w + 4 * s) % W)))
        grad_s, grad_t, norm, grad_latents = call(
            functools.partial(last_body, sizes, scale, Z),
            [
                shape((width, shard_s), F32),
                shape((width, shard_t), F32),
                shape((2, width), F32),
                shape((rows, channels), BF16),
            ],
            moved=1_000_000,
        )(*terms, *operands)
        grad_s, grad_t = grad_s.T, grad_t.T
    else:
        sums = lax.all_to_all(
            grads_t[1], ("dp", "wide"), split_axis=0, concat_axis=0, tiled=True
        )
        norm, grad_latents = call(
            functools.partial(apart_body, sizes, scale),
            [shape((2, width), F32), shape((rows, channels), BF16)],
        )(sums, *operands)
        outs = []
        for full in (grads_s[0], grads_t[0]):
            part = lax.psum_scatter(
                full.astype(F32), "wide", scatter_dimension=0, tiled=True
            ).T.astype(BF16)
            part = lax.psum_scatter(part, "dp", scatter_dimension=0, tiled=True)
            outs.append(part.astype(F32) * scale)
        grad_s, grad_t = outs
    return (
        block_out.reshape(latents.shape),
        grad_latents.reshape(latents.shape),
        grad_s,
        grad_t,
        norm,
    )


def solution(mesh):
    return jax.shard_map(
        local,
        mesh=mesh,
        in_specs=(
            P("dp", "wide", None, None, None),
            P("dp", "wide", None, None, None),
            P(),
            P(),
            P("dp", None),
            P("dp", None),
        ),
        out_specs=(
            P("dp", "wide", None, None, None),
            P("dp", "wide", None, None, None),
            P("dp", "wide"),
            P("dp", "wide"),
            P(None, "wide"),
        ),
        check_vma=False,
    )
```

```python
import functools
import math

import jax
import jax.numpy as jnp
from jax import lax
from jax.experimental import pallas as pl
from jax.experimental.pallas import tpu as pltpu
from jax.sharding import PartitionSpec as P

GROUPS = 32
EPSILON = 1e-05
F32 = jnp.float32
BF16 = jnp.bfloat16
VMEM = pl.BlockSpec(memory_space=pltpu.VMEM)
HBM = pl.BlockSpec(memory_space=pltpu.HBM)
OTHERS = ((0, 0, 0), (1, 1, 1), (1, 1, 0), (0, 1, 1), (1, 0, 1), (1, 0, 0), (0, 1, 0), (0, 0, 1))
NT = (((1,), (1,)), ((), ()))
NN = (((1,), (0,)), ((), ()))


def call(body, out_shapes, scratch=(), flops=0, moved=0, in_specs=None, out_specs=None, vmem=40):
    many = isinstance(out_shapes, (tuple, list))

    def run(*operands):
        return pl.pallas_call(
            body,
            out_shape=out_shapes,
            in_specs=in_specs or [VMEM] * len(operands),
            out_specs=out_specs or ([VMEM] * len(out_shapes) if many else VMEM),
            scratch_shapes=list(scratch),
            compiler_params=pltpu.CompilerParams(vmem_limit_bytes=vmem * 1024 * 1024),
            cost_estimate=pl.CostEstimate(
                flops=flops, bytes_accessed=moved, transcendentals=0
            ),
        )(*operands)

    return run


def shape(dims, kind):
    return jax.ShapeDtypeStruct(dims, kind)


def mm(left, right, dims=NN):
    return lax.dot_general(left, right, dims, preferred_element_type=F32)


def group_total(rows, per_group):
    channels = rows.shape[-1]
    first = lax.broadcasted_iota(jnp.int32, (channels, channels), 0) // per_group
    second = lax.broadcasted_iota(jnp.int32, (channels, channels), 1) // per_group
    same = (first == second).astype(F32)
    return lax.dot_general(
        rows, same, NN, precision=lax.Precision.HIGHEST, preferred_element_type=F32
    )


def stats_body(lat_ref, gain_ref, bias_ref, ws_ref, wt_ref, out_ref, affine_ref, half_ref, *scratch):
    lat_here, gain_here, bias_here, sems = scratch
    core = lax.rem(lax.axis_index("wide"), 2)
    moves, place = [(lat_ref, lat_here), (gain_ref, gain_here), (bias_ref, bias_here)], 0
    for source in (ws_ref, wt_ref):
        half = source.shape[0] // 2
        start = pl.multiple_of(core * half, 16)
        moves.append((source.at[pl.ds(start, half)], half_ref.at[pl.ds(place, half)]))
        place += half
    copies = [pltpu.make_async_copy(*move, sems.at[at]) for at, move in enumerate(moves)]
    for copy in copies:
        copy.start()
    for copy in copies[:3]:
        copy.wait()
    affine_ref[0:1] = gain_here[...]
    affine_ref[1:2] = bias_here[...]
    x = lat_here[...].astype(F32)
    both = jnp.concatenate(
        [jnp.sum(x, axis=0, keepdims=True), jnp.sum(x * x, axis=0, keepdims=True)], axis=0
    )
    out_ref[...] = jnp.broadcast_to(both[None], out_ref.shape)
    for copy in copies[3:]:
        copy.wait()


def fill_weights(full, shard_ref, pieces, offset, D):
    d = lax.axis_index("dp")
    core = lax.rem(lax.axis_index("wide"), 2)
    n = shard_ref.shape[0]
    half = n // 2
    full[pl.ds(pl.multiple_of(d * n, 16), n)] = shard_ref[...]
    for s in range(1, D):
        source = lax.rem(d + D - s, D)
        for which in range(2):
            holder = core if which == 0 else 1 - core
            start = pl.multiple_of(source * n + holder * half, 16)
            full[pl.ds(start, half)] = pieces[2 * (s - 1) + which][offset : offset + half]


def whiten(lat, stats, count, per_group):
    total = group_total(jnp.sum(stats, axis=0), per_group) / count
    mean = total[0:1]
    inv_std = 1.0 / jnp.sqrt(total[1:2] - mean * mean + EPSILON)
    return (lat.astype(F32) - mean) * inv_std, inv_std


def store_shifted(pad_ref, values, frames, cells, cols):
    total = frames * cells
    column = lax.broadcasted_iota(jnp.int32, (total, 1), 0) % cols
    left = jnp.where(column == 0, 0.0, pltpu.roll(values, 1, 0))
    right = jnp.where(column == cols - 1, 0.0, pltpu.roll(values, total - 1, 0))
    edge = jnp.zeros((cols, values.shape[1]), BF16)
    for at, form in enumerate((left, values, right)):
        low = form.astype(BF16)
        for f in range(frames):
            pad_ref[at, f, 0:cols] = edge
            pad_ref[at, f, cols : cols + cells] = low[f * cells : (f + 1) * cells]
            pad_ref[at, f, cols + cells :] = edge


def window(pad_ref, dy, dx, frames, cells, cols):
    return jnp.concatenate(
        [pad_ref[dx, f, dy * cols : dy * cols + cells] for f in range(frames)], axis=0
    )


def in_parts(total):
    high = total.astype(BF16).astype(F32)
    return jnp.concatenate([high, total - high], axis=0).astype(BF16)


def from_parts(terms):
    total = 0.0
    for term in terms:
        wide = term.astype(F32)
        total = total + (wide[0:8] + wide[8:16])
    return total


def add(terms):
    total = terms[0].astype(F32)
    for term in terms[1:]:
        total += term.astype(F32)
    return total


def core_order(transposed_ref, W, core):
    step = transposed_ref.shape[0] // W
    order = [(2 * j + core) * step for j in range(W // 2)]
    order += [(2 * j + 1 - core) * step for j in range(W // 2)]
    return jnp.concatenate(
        [transposed_ref[pl.ds(pl.multiple_of(at, 16), step)] for at in order], axis=0
    )


def put(block, column, shard, keep_ref, send_ref):
    low = block.astype(BF16)
    if send_ref is None:
        keep_ref[:, column : column + block.shape[1]] = low
        return
    half = block.shape[0] // 2
    for at in range(0, block.shape[1], 128):
        owner, place = (column + at) // shard, (column + at) % shard
        keep_ref[owner, :, place : place + 128] = low[:half, at : at + 128]
        send_ref[owner, :, place : place + 128] = low[half:, at : at + 128]


def normalise(lat_ref, stats_ref, affine_ref, count, per_group):
    white, inv_std = whiten(lat_ref[...], stats_ref[...], count, per_group)
    normed = white * affine_ref[0:1] + affine_ref[1:2]
    return white, normed, jax.nn.sigmoid(normed)


def first_body(sizes, lat_ref, cot_ref, halo_ref, stats_ref, affine_ref, wt_ref, *rest):
    D, W, frames, cells, cols, count, per_group, aligned = sizes
    pieces, rest = rest[: 2 * (D - 1)], rest[2 * (D - 1) :]
    full_wt, act_pad, gsa_t = rest[-3:]
    gsa_ref, keep_ref = rest[:2]
    send_ref = rest[2] if aligned else None
    channels = lat_ref.shape[1]
    core = lax.rem(lax.axis_index("wide"), 2)
    fill_weights(full_wt, wt_ref, pieces, pieces[0].shape[0] - wt_ref.shape[0] // 2, D)
    rows = frames * cells
    extended = jnp.concatenate([cot_ref[...], halo_ref[...]], axis=0)
    gsa = jnp.zeros((rows, channels), F32)
    for k in range(3):
        gsa += mm(
            extended[k * cells : k * cells + rows],
            full_wt[k * channels : (k + 1) * channels],
            NT,
        )
    gsa_ref[...] = gsa.astype(BF16)
    gsa_t[...] = gsa.astype(BF16).astype(F32).T.astype(BF16)
    _, normed, sig = normalise(lat_ref, stats_ref, affine_ref, count, per_group)
    act = (normed * sig).astype(BF16).astype(F32)
    store_shifted(act_pad, act, frames, cells, cols)
    left = core_order(gsa_t, W, core) if aligned else gsa_t[...]
    shard = wt_ref.shape[0] * 3
    for dy in range(3):
        for dx in range(3):
            seen = window(act_pad, dy, dx, frames, cells, cols)
            put(mm(left, seen), (3 * dy + dx) * channels, shard, keep_ref, send_ref)


def second_body(
    sizes, lat_ref, cot_ref, halo_ref, stats_ref, affine_ref, gsa_ref, ws_ref, *rest
):
    D, W, frames, cells, cols, count, per_group, aligned = sizes
    pieces, rest = rest[: 2 * (D - 1)], rest[2 * (D - 1) :]
    full_ws, act_pad, gsa_pad, cot_t = rest[-4:]
    spatial_ref, grad_ref, keep_ref, other_ref = rest[:4]
    send_ref = other_ref if aligned else None
    channels = lat_ref.shape[1]
    core = lax.rem(lax.axis_index("wide"), 2)
    fill_weights(full_ws, ws_ref, pieces, 0, D)
    rows = frames * cells
    white, normed, sig = normalise(lat_ref, stats_ref, affine_ref, count, per_group)
    act = (normed * sig).astype(BF16).astype(F32)
    store_shifted(act_pad, act, frames, cells, cols)
    store_shifted(gsa_pad, gsa_ref[...].astype(F32), frames, cells, cols)
    extended = jnp.concatenate([cot_ref[...], halo_ref[...]], axis=0)
    for f in range(frames + 2):
        cot_t[:, f * cells : (f + 1) * cells] = (
            extended[f * cells : (f + 1) * cells].astype(F32).T.astype(BF16)
        )
    left = core_order(cot_t, W, core) if aligned else cot_t[...]
    out = jnp.zeros((rows, channels), F32)
    for dy in range(3):
        for dx in range(3):
            tap = 3 * dy + dx
            seen = window(act_pad, dy, dx, frames, cells, cols)
            out += mm(seen, full_ws[tap * channels : (tap + 1) * channels])
    spatial = out.astype(BF16)
    spatial_ref[...] = spatial
    shard = ws_ref.shape[0] // 3
    for k in range(3):
        block = mm(left[:, k * cells : k * cells + rows], spatial)
        put(block, k * channels, shard, keep_ref, send_ref)

    grad = jnp.zeros((rows, channels), F32)
    for dy in range(3):
        for dx in range(3):
            tap = 3 * dy + dx
            seen = window(gsa_pad, 2 - dy, 2 - dx, frames, cells, cols)
            grad += mm(seen, full_ws[tap * channels : (tap + 1) * channels], NT)
    grad = grad * (sig * (1.0 + normed * (1.0 - sig)))
    grad_ref[...] = grad
    gain_term = jnp.sum(grad * white, axis=0, keepdims=True)
    bias_term = jnp.sum(grad, axis=0, keepdims=True)
    if not aligned:
        both = jnp.concatenate([gain_term, bias_term], axis=0)
        other_ref[...] = jnp.broadcast_to(both[None], other_ref.shape)
        return
    d = lax.axis_index("dp")
    quarter = jnp.concatenate(
        [term[:, at : at + 128] for term in (gain_term, bias_term) for at in (0, 128)], axis=0
    )
    low = in_parts(
        jnp.concatenate([jnp.where(d == s, quarter, 0.0) for s in range(2)], axis=0)
    )
    for target in (keep_ref, send_ref):
        for owner in range(D):
            for at in range(0, channels // 2, 16):
                target[owner, at : at + 16, shard:] = low


def block_body(sizes, lat_ref, spatial_ref, before_ref, wt_ref, *rest):
    D, W, frames, cells, cols, count, per_group, aligned = sizes
    pieces = rest[: 2 * (D - 1)]
    block_ref, full_wt = rest[2 * (D - 1) :]
    channels = lat_ref.shape[1]
    fill_weights(full_wt, wt_ref, pieces, pieces[0].shape[0] - wt_ref.shape[0] // 2, D)
    extended = jnp.concatenate([before_ref[...], spatial_ref[...]], axis=0)
    rows = frames * cells
    temporal = jnp.zeros((rows, channels), F32)
    for k in range(3):
        start = (2 - k) * cells
        temporal += mm(
            extended[start : start + rows], full_wt[k * channels : (k + 1) * channels]
        )
    block_ref[...] = (lat_ref[...].astype(F32) + temporal).astype(BF16)


def latent_gradient(sizes, total, lat_ref, cot_ref, stats_ref, affine_ref, grad_ref):
    D, W, frames, cells, cols, count, per_group, aligned = sizes
    white, inv_std = whiten(lat_ref[...], stats_ref[...], count, per_group)
    gain = affine_ref[0:1]
    means = group_total(total * gain, per_group) / count
    inner = inv_std * (grad_ref[...] * gain - means[1:2] - white * means[0:1])
    return (cot_ref[...].astype(F32) + inner).astype(BF16)


def block_terms_body(keep_s, got_s, keep_t, got_t, *outs):
    d = lax.axis_index("dp")
    w = lax.axis_index("wide")
    y, pair = lax.rem(w // 2, 2), lax.rem(w // 4, 2)
    split = keep_s.shape[-1]
    ride = outs[0].shape[-1] - 128
    for at, (a, b, c) in enumerate(OTHERS):
        owner, side, near = lax.rem(d + a, 2), lax.rem(y + b, 2), lax.rem(pair + c, 2)
        out = outs[at]
        for far in range(out.shape[0]):
            z = 2 * far + near
            out[far, :, :split] = add([keep_s[owner, z, side], got_s[owner, z, side]]).astype(BF16)
            both = [keep_t[owner, z, side], got_t[owner, z, side]]
            out[far, :, split:ride] = add([t[:, : ride - split] for t in both]).astype(BF16)
            out[far, :, ride:] = in_parts(from_parts([t[:, ride - split :] for t in both]))


def line_body(depth, *refs):
    terms, outs = refs[:-depth], refs[-depth:]
    far = lax.axis_index("wide") // 8
    ride = outs[0].shape[-1] - 128
    for s in range(depth):
        owner = lax.rem(far + s, depth)
        seen = [term[owner] for term in terms]
        outs[s][:, :ride] = add([t[:, :ride] for t in seen]).astype(BF16)
        outs[s][:, ride:] = in_parts(from_parts([t[:, ride:] for t in seen]))


def last_body(sizes, scale, depth, *refs):
    terms, operands, outs = refs[:depth], refs[depth:-4], refs[-4:]
    spatial_ref, temporal_ref, norm_ref, glat_ref = outs
    split = spatial_ref.shape[1]
    ride = terms[0].shape[1] - 128
    sums = from_parts([term[:, ride:] for term in terms])

    def rows_of(part):
        return jnp.concatenate(
            [jnp.concatenate([part[at : at + 1], part[at + 1 : at + 2]], axis=1) for at in (0, 2)],
            axis=0,
        )

    first, second = rows_of(sums[0:4]), rows_of(sums[4:8])
    own = jnp.where(lax.axis_index("dp") == 0, first, second)
    glat_ref[...] = latent_gradient(sizes, own, *operands)
    norm_columns(scale, first + second, norm_ref)
    total = add([term[:, :ride] for term in terms]) * scale
    spatial_ref[...] = total[:, :split]
    temporal_ref[...] = total[:, split:]


def apart_body(sizes, scale, sums_ref, *refs):
    norm_ref, glat_ref = refs[-2:]
    W = sizes[1]
    own = jnp.sum(sums_ref[pl.ds(lax.axis_index("dp") * W, W)], axis=0)
    norm_columns(scale, jnp.sum(sums_ref[...], axis=0), norm_ref)
    glat_ref[...] = latent_gradient(sizes, own, *refs[:-2])


def norm_columns(scale, norm, norm_ref):
    channels, width = norm.shape[1], norm_ref.shape[1]
    row = lax.broadcasted_iota(jnp.int32, (channels, width), 0)
    column = lax.broadcasted_iota(jnp.int32, (channels, width), 1)
    pick = (row == column + lax.axis_index("wide") * width).astype(F32)
    norm_ref[...] = (
        lax.dot_general(
            norm, pick, NN, precision=lax.Precision.HIGHEST, preferred_element_type=F32
        )
        * scale
    )


def local(latents, cotangent, norm_gain, norm_bias, w_spatial, w_temporal):
    D, W = lax.axis_size("dp"), lax.axis_size("wide")
    _, frames, rows_here, cols, channels = latents.shape
    cells = rows_here * cols
    rows = frames * cells
    per_group = channels // GROUPS
    count = W * frames * cells * per_group
    shard_s, shard_t = w_spatial.shape[0], w_temporal.shape[0]
    aligned = (channels // W) % 16 == 0 and shard_s % 128 == 0 and shard_t % 128 == 0
    aligned = aligned and W % 8 == 0 and D == 2 and channels == 256
    sizes = (D, W, frames, cells, cols, count, per_group, aligned)
    scale = 1.0 / math.sqrt(D * W * frames * cells)

    lat, cot = latents.reshape(rows, channels), cotangent.reshape(rows, channels)
    gain, bias = norm_gain.reshape(1, channels), norm_bias.reshape(1, channels)

    def over_all(moves):
        pairs = []
        for d in range(D):
            for w in range(W):
                to = moves(d, w)
                pairs.append((d * W + w, to[0] * W + to[1]))
        return pairs

    def send(value, moves):
        return lax.ppermute(value, ("dp", "wide"), over_all(moves))

    R = shard_s + shard_t
    stats, affine, half = call(
        stats_body,
        [
            shape((W, 2, channels), F32),
            shape((2, channels), F32),
            shape((R // 2, channels), BF16),
        ],
        [
            pltpu.VMEM((rows, channels), BF16),
            pltpu.VMEM((1, channels), F32),
            pltpu.VMEM((1, channels), F32),
            pltpu.SemaphoreType.DMA((5,)),
        ],
        in_specs=[HBM] * 5,
        out_specs=[VMEM, VMEM, HBM],
        vmem=60,
    )(lat, gain, bias, w_spatial, w_temporal)
    firsts = [send(half, lambda d, w: ((d + s) % D, w)) for s in range(1, D)]

    halo = lax.ppermute(cot, "wide", [(w + 1, w) for w in range(W - 1)])
    stats = lax.all_to_all(stats, "wide", split_axis=0, concat_axis=0, tiled=True)
    firsts, stats, halo = lax.optimization_barrier((firsts, stats, halo))
    pieces = []
    for first in firsts:
        pieces += [first, send(first, lambda d, w: (d, w ^ 1))]

    ride = 128 if aligned else 0
    if aligned:
        terms_s = [shape((D, channels // 2, shard_s), BF16)] * 2
        terms_t = [shape((D, channels // 2, shard_t + ride), BF16)] * 2
    else:
        terms_s = [shape((channels, D * shard_s), BF16)]
        terms_t = [shape((channels, D * shard_t), BF16), shape((D * W, 2, channels), F32)]
    pad = pltpu.VMEM((3, frames, cells + 2 * cols, channels), BF16)
    gsa, *grads_s = call(
        functools.partial(first_body, sizes),
        [shape((rows, channels), BF16)] + terms_s,
        [pltpu.VMEM((D * shard_t, channels), BF16), pad, pltpu.VMEM((channels, rows), BF16)],
        flops=2 * 12 * rows * channels * channels,
        moved=3_000_000,
    )(lat, cot, halo, stats, affine, w_temporal, *pieces)
    spatial, grad, *grads_t = call(
        functools.partial(second_body, sizes),
        [shape((rows, channels), BF16), shape((rows, channels), F32)] + terms_t,
        [
            pltpu.VMEM((D * shard_s, channels), BF16),
            pad,
            pad,
            pltpu.VMEM((channels, rows + 2 * cells), BF16),
        ],
        flops=2 * 21 * rows * channels * channels,
        moved=3_000_000,
    )(lat, cot, halo, stats, affine, gsa, w_spatial, *pieces)
    before = lax.ppermute(spatial, "wide", [(w, w + 1) for w in range(W - 1)])
    block_out = call(
        functools.partial(block_body, sizes),
        shape((rows, channels), BF16),
        [pltpu.VMEM((D * shard_t, channels), BF16)],
        flops=2 * 3 * rows * channels * channels,
        moved=1_000_000,
    )(lat, spatial, before, w_temporal, *pieces)

    width = channels // W
    operands = (lat, cot, stats, affine, grad)
    if aligned:
        Z, far = W // 4, W // 8

        def over_core(away):
            return send(away, lambda d, w: (d, w ^ 1))

        pairs = []
        for keep, away in (grads_s, grads_t):
            view = (D, Z, 2, width, keep.shape[-1])
            pairs += [keep.reshape(view), over_core(away).reshape(view)]
        sums = call(
            block_terms_body,
            [shape((far, width, R + ride), BF16)] * len(OTHERS),
            moved=3_000_000,
        )(*pairs)
        seen = [sums[0]]
        for value, (a, b, c) in zip(sums[1:], OTHERS[1:]):
            seen.append(send(value, lambda d, w: (d ^ a, w ^ (2 * b + 4 * c))))
        line = call(
            functools.partial(line_body, far),
            [shape((width, R + ride), BF16)] * far,
            moved=1_000_000,
        )(*seen)
        terms = [line[0]]
        for s in range(1, far):
            terms.append(send(line[s], lambda d, w: (d, (w + 8 * s) % W)))
        grad_s, grad_t, norm, grad_latents = call(
            functools.partial(last_body, sizes, scale, far),
            [
                shape((width, shard_s), F32),
                shape((width, shard_t), F32),
                shape((2, width), F32),
                shape((rows, channels), BF16),
            ],
            moved=1_000_000,
        )(*terms, *operands)
        grad_s, grad_t = grad_s.T, grad_t.T
    else:
        sums = lax.all_to_all(
            grads_t[1], ("dp", "wide"), split_axis=0, concat_axis=0, tiled=True
        )
        norm, grad_latents = call(
            functools.partial(apart_body, sizes, scale),
            [shape((2, width), F32), shape((rows, channels), BF16)],
        )(sums, *operands)
        outs = []
        for full in (grads_s[0], grads_t[0]):
            part = lax.psum_scatter(
                full.astype(F32), "wide", scatter_dimension=0, tiled=True
            ).T.astype(BF16)
            part = lax.psum_scatter(part, "dp", scatter_dimension=0, tiled=True)
            outs.append(part.astype(F32) * scale)
        grad_s, grad_t = outs
    return (
        block_out.reshape(latents.shape),
        grad_latents.reshape(latents.shape),
        grad_s,
        grad_t,
        norm,
    )


def solution(mesh):
    return jax.shard_map(
        local,
        mesh=mesh,
        in_specs=(
            P("dp", "wide", None, None, None),
            P("dp", "wide", None, None, None),
            P(),
            P(),
            P("dp", None),
            P("dp", None),
        ),
        out_specs=(
            P("dp", "wide", None, None, None),
            P("dp", "wide", None, None, None),
            P("dp", "wide"),
            P("dp", "wide"),
            P(None, "wide"),
        ),
        check_vma=False,
    )
```

```python
import functools
import math

import jax
import jax.numpy as jnp
from jax import lax
from jax.experimental import pallas as pl
from jax.experimental.pallas import tpu as pltpu
from jax.sharding import PartitionSpec as P

GROUPS = 32
EPSILON = 1e-05
F32 = jnp.float32
BF16 = jnp.bfloat16
VMEM = pl.BlockSpec(memory_space=pltpu.VMEM)
HBM = pl.BlockSpec(memory_space=pltpu.HBM)
FIRST_VMEM = 60 << 20
NT = (((1,), (1,)), ((), ()))
NN = (((1,), (0,)), ((), ()))


def call(body, out_shapes, scratch=(), flops=0, moved=0, in_specs=None, vmem=40 << 20):
    many = isinstance(out_shapes, (tuple, list))

    def run(*operands):
        return pl.pallas_call(
            body,
            out_shape=out_shapes,
            in_specs=in_specs or [VMEM] * len(operands),
            out_specs=[VMEM] * len(out_shapes) if many else VMEM,
            scratch_shapes=list(scratch),
            compiler_params=pltpu.CompilerParams(vmem_limit_bytes=vmem),
            cost_estimate=pl.CostEstimate(
                flops=flops, bytes_accessed=moved, transcendentals=0
            ),
        )(*operands)

    return run


def shape(dims, kind):
    return jax.ShapeDtypeStruct(dims, kind)


def mm(left, right, dims=NN):
    return lax.dot_general(left, right, dims, preferred_element_type=F32)


def group_total(rows, per_group):
    channels = rows.shape[-1]
    first = lax.broadcasted_iota(jnp.int32, (channels, channels), 0) // per_group
    second = lax.broadcasted_iota(jnp.int32, (channels, channels), 1) // per_group
    same = (first == second).astype(F32)
    return lax.dot_general(
        rows, same, NN, precision=lax.Precision.HIGHEST, preferred_element_type=F32
    )


def stats_body(lat_ref, gain_ref, bias_ref, ws_ref, wt_ref, out_ref, affine_ref, half_ref, *scratch):
    lat_here, gain_here, bias_here, sems = scratch
    core = lax.rem(lax.axis_index("wide"), 2)
    moves, place = [(lat_ref, lat_here), (gain_ref, gain_here), (bias_ref, bias_here)], 0
    for source in (ws_ref, wt_ref):
        half = source.shape[0] // 2
        start = pl.multiple_of(core * half, 16)
        moves.append((source.at[pl.ds(start, half)], half_ref.at[pl.ds(place, half)]))
        place += half
    copies = [pltpu.make_async_copy(*move, sems.at[at]) for at, move in enumerate(moves)]
    for copy in copies:
        copy.start()
    for copy in copies[:3]:
        copy.wait()
    affine_ref[0:1] = gain_here[...]
    affine_ref[1:2] = bias_here[...]
    x = lat_here[...].astype(F32)
    both = jnp.concatenate(
        [jnp.sum(x, axis=0, keepdims=True), jnp.sum(x * x, axis=0, keepdims=True)], axis=0
    )
    out_ref[...] = jnp.broadcast_to(both[None], out_ref.shape)
    for copy in copies[3:]:
        copy.wait()


def transpose_body(cot_ref, out_ref):
    out_ref[...] = cot_ref[...].astype(F32).T.astype(BF16)


def fill_weights(full, shard_ref, pieces, offset, D):
    d = lax.axis_index("dp")
    core = lax.rem(lax.axis_index("wide"), 2)
    n = shard_ref.shape[0]
    half = n // 2
    full[pl.ds(pl.multiple_of(d * n, 16), n)] = shard_ref[...]
    for s in range(1, D):
        source = lax.rem(d + D - s, D)
        for which in range(2):
            holder = core if which == 0 else 1 - core
            start = pl.multiple_of(source * n + holder * half, 16)
            full[pl.ds(start, half)] = pieces[2 * (s - 1) + which][offset : offset + half]


def whiten(lat, stats, count, per_group):
    total = group_total(jnp.sum(stats, axis=0), per_group) / count
    mean = total[0:1]
    inv_std = 1.0 / jnp.sqrt(total[1:2] - mean * mean + EPSILON)
    return (lat.astype(F32) - mean) * inv_std, inv_std


def store_shifted(pad_ref, values, frames, cells, cols):
    total = frames * cells
    column = lax.broadcasted_iota(jnp.int32, (total, 1), 0) % cols
    left = jnp.where(column == 0, 0.0, pltpu.roll(values, 1, 0))
    right = jnp.where(column == cols - 1, 0.0, pltpu.roll(values, total - 1, 0))
    edge = jnp.zeros((cols, values.shape[1]), BF16)
    for at, form in enumerate((left, values, right)):
        low = form.astype(BF16)
        for f in range(frames):
            pad_ref[at, f, 0:cols] = edge
            pad_ref[at, f, cols : cols + cells] = low[f * cells : (f + 1) * cells]
            pad_ref[at, f, cols + cells :] = edge


def window(pad_ref, dy, dx, frames, cells, cols):
    return jnp.concatenate(
        [pad_ref[dx, f, dy * cols : dy * cols + cells] for f in range(frames)], axis=0
    )


def in_parts(total):
    high = total.astype(BF16).astype(F32)
    return jnp.concatenate([high, total - high], axis=0).astype(BF16)


def from_parts(terms):
    total = 0.0
    for term in terms:
        wide = term.astype(F32)
        total = total + (wide[0:8] + wide[8:16])
    return total


def add(terms):
    total = terms[0].astype(F32)
    for term in terms[1:]:
        total += term.astype(F32)
    return total


def core_order(transposed_ref, W, core):
    step = transposed_ref.shape[0] // W
    order = [(2 * j + core) * step for j in range(W // 2)]
    order += [(2 * j + 1 - core) * step for j in range(W // 2)]
    return jnp.concatenate(
        [transposed_ref[pl.ds(pl.multiple_of(at, 16), step)] for at in order], axis=0
    )


def put(block, column, shard, keep_ref, send_ref):
    low = block.astype(BF16)
    if send_ref is None:
        keep_ref[:, column : column + block.shape[1]] = low
        return
    half = block.shape[0] // 2
    for at in range(0, block.shape[1], 128):
        owner, place = (column + at) // shard, (column + at) % shard
        keep_ref[owner, :, place : place + 128] = low[:half, at : at + 128]
        send_ref[owner, :, place : place + 128] = low[half:, at : at + 128]


def normalise(lat_ref, stats_ref, affine_ref, count, per_group):
    white, inv_std = whiten(lat_ref[...], stats_ref[...], count, per_group)
    normed = white * affine_ref[0:1] + affine_ref[1:2]
    return white, normed, jax.nn.sigmoid(normed)


def first_body(sizes, lat_ref, cot_ref, halo_ref, stats_ref, affine_ref, wt_ref, *rest):
    D, W, frames, cells, cols, count, per_group, aligned = sizes
    pieces, rest = rest[: 2 * (D - 1)], rest[2 * (D - 1) :]
    full_wt, act_pad, gsa_t = rest[-3:]
    gsa_ref, keep_ref = rest[:2]
    send_ref = rest[2] if aligned else None
    channels = lat_ref.shape[1]
    core = lax.rem(lax.axis_index("wide"), 2)
    fill_weights(full_wt, wt_ref, pieces, pieces[0].shape[0] - wt_ref.shape[0] // 2, D)
    rows = frames * cells
    extended = jnp.concatenate([cot_ref[...], halo_ref[...]], axis=0)
    gsa = jnp.zeros((rows, channels), F32)
    for k in range(3):
        gsa += mm(
            extended[k * cells : k * cells + rows],
            full_wt[k * channels : (k + 1) * channels],
            NT,
        )
    gsa_ref[...] = gsa.astype(BF16)
    gsa_t[...] = gsa.astype(BF16).astype(F32).T.astype(BF16)
    _, normed, sig = normalise(lat_ref, stats_ref, affine_ref, count, per_group)
    act = (normed * sig).astype(BF16).astype(F32)
    store_shifted(act_pad, act, frames, cells, cols)
    left = core_order(gsa_t, W, core) if aligned else gsa_t[...]
    shard = wt_ref.shape[0] * 3
    for dy in range(3):
        for dx in range(3):
            seen = window(act_pad, dy, dx, frames, cells, cols)
            put(mm(left, seen), (3 * dy + dx) * channels, shard, keep_ref, send_ref)


def second_body(
    sizes, lat_ref, cot_t_ref, halo_ref, stats_ref, affine_ref, gsa_ref, ws_ref, *rest
):
    D, W, frames, cells, cols, count, per_group, aligned = sizes
    pieces, rest = rest[: 2 * (D - 1)], rest[2 * (D - 1) :]
    full_ws, act_pad, gsa_pad, cot_t = rest[-4:]
    spatial_ref, grad_ref, keep_ref, other_ref = rest[:4]
    send_ref = other_ref if aligned else None
    channels = lat_ref.shape[1]
    core = lax.rem(lax.axis_index("wide"), 2)
    fill_weights(full_ws, ws_ref, pieces, 0, D)
    rows = frames * cells
    white, normed, sig = normalise(lat_ref, stats_ref, affine_ref, count, per_group)
    act = (normed * sig).astype(BF16).astype(F32)
    store_shifted(act_pad, act, frames, cells, cols)
    store_shifted(gsa_pad, gsa_ref[...].astype(F32), frames, cells, cols)
    cot_t[:, :rows] = cot_t_ref[...]
    for f in range(2):
        cot_t[:, rows + f * cells : rows + (f + 1) * cells] = (
            halo_ref[f * cells : (f + 1) * cells].astype(F32).T.astype(BF16)
        )
    left = core_order(cot_t, W, core) if aligned else cot_t[...]
    out = jnp.zeros((rows, channels), F32)
    for dy in range(3):
        for dx in range(3):
            tap = 3 * dy + dx
            seen = window(act_pad, dy, dx, frames, cells, cols)
            out += mm(seen, full_ws[tap * channels : (tap + 1) * channels])
    spatial = out.astype(BF16)
    spatial_ref[...] = spatial
    shard = ws_ref.shape[0] // 3
    for k in range(3):
        block = mm(left[:, k * cells : k * cells + rows], spatial)
        put(block, k * channels, shard, keep_ref, send_ref)

    grad = jnp.zeros((rows, channels), F32)
    for dy in range(3):
        for dx in range(3):
            tap = 3 * dy + dx
            seen = window(gsa_pad, 2 - dy, 2 - dx, frames, cells, cols)
            grad += mm(seen, full_ws[tap * channels : (tap + 1) * channels], NT)
    grad = grad * (sig * (1.0 + normed * (1.0 - sig)))
    grad_ref[...] = grad
    gain_term = jnp.sum(grad * white, axis=0, keepdims=True)
    bias_term = jnp.sum(grad, axis=0, keepdims=True)
    if not aligned:
        both = jnp.concatenate([gain_term, bias_term], axis=0)
        other_ref[...] = jnp.broadcast_to(both[None], other_ref.shape)
        return
    d = lax.axis_index("dp")
    quarter = jnp.concatenate(
        [term[:, at : at + 128] for term in (gain_term, bias_term) for at in (0, 128)], axis=0
    )
    low = in_parts(
        jnp.concatenate([jnp.where(d == s, quarter, 0.0) for s in range(2)], axis=0)
    )
    for target in (keep_ref, send_ref):
        for owner in range(D):
            for at in range(0, channels // 2, 16):
                target[owner, at : at + 16, shard:] = low


def block_body(sizes, lat_ref, spatial_ref, before_ref, wt_ref, *rest):
    D, W, frames, cells, cols, count, per_group, aligned = sizes
    pieces = rest[: 2 * (D - 1)]
    block_ref, full_wt = rest[2 * (D - 1) :]
    channels = lat_ref.shape[1]
    fill_weights(full_wt, wt_ref, pieces, pieces[0].shape[0] - wt_ref.shape[0] // 2, D)
    extended = jnp.concatenate([before_ref[...], spatial_ref[...]], axis=0)
    rows = frames * cells
    temporal = jnp.zeros((rows, channels), F32)
    for k in range(3):
        start = (2 - k) * cells
        temporal += mm(
            extended[start : start + rows], full_wt[k * channels : (k + 1) * channels]
        )
    block_ref[...] = (lat_ref[...].astype(F32) + temporal).astype(BF16)


def latent_gradient(sizes, total, lat_ref, cot_ref, stats_ref, affine_ref, grad_ref):
    D, W, frames, cells, cols, count, per_group, aligned = sizes
    white, inv_std = whiten(lat_ref[...], stats_ref[...], count, per_group)
    gain = affine_ref[0:1]
    means = group_total(total * gain, per_group) / count
    inner = inv_std * (grad_ref[...] * gain - means[1:2] - white * means[0:1])
    return (cot_ref[...].astype(F32) + inner).astype(BF16)


def plane_body(keep_s, got_s, keep_t, got_t, *outs):
    d = lax.axis_index("dp")
    y = lax.rem(lax.axis_index("wide") // 2, 2)
    split = keep_s.shape[-1]
    ride = outs[0].shape[-1] - 128
    for a in range(2):
        for b in range(2):
            owner, side = lax.rem(d + a, 2), lax.rem(y + b, 2)
            out = outs[2 * a + b]
            for z in range(out.shape[0]):
                out[z, :, :split] = add([keep_s[owner, z, side], got_s[owner, z, side]]).astype(
                    BF16
                )
                both = [keep_t[owner, z, side], got_t[owner, z, side]]
                out[z, :, split:ride] = add([t[:, : ride - split] for t in both]).astype(BF16)
                out[z, :, ride:] = in_parts(from_parts([t[:, ride - split :] for t in both]))


def line_body(depth, *refs):
    terms, outs = refs[:4], refs[4:]
    z = lax.axis_index("wide") // 4
    ride = outs[0].shape[-1] - 128
    for s in range(depth):
        owner = lax.rem(z + s, depth)
        seen = [term[owner] for term in terms]
        outs[s][:, :ride] = add([t[:, :ride] for t in seen]).astype(BF16)
        outs[s][:, ride:] = in_parts(from_parts([t[:, ride:] for t in seen]))


def last_body(sizes, scale, depth, *refs):
    terms, operands, outs = refs[:depth], refs[depth:-4], refs[-4:]
    spatial_ref, temporal_ref, norm_ref, glat_ref = outs
    split = spatial_ref.shape[1]
    ride = terms[0].shape[1] - 128
    sums = from_parts([term[:, ride:] for term in terms])

    def rows_of(part):
        return jnp.concatenate(
            [jnp.concatenate([part[at : at + 1], part[at + 1 : at + 2]], axis=1) for at in (0, 2)],
            axis=0,
        )

    first, second = rows_of(sums[0:4]), rows_of(sums[4:8])
    own = jnp.where(lax.axis_index("dp") == 0, first, second)
    glat_ref[...] = latent_gradient(sizes, own, *operands)
    norm_columns(scale, first + second, norm_ref)
    total = add([term[:, :ride] for term in terms]) * scale
    spatial_ref[...] = total[:, :split]
    temporal_ref[...] = total[:, split:]


def apart_body(sizes, scale, sums_ref, *refs):
    norm_ref, glat_ref = refs[-2:]
    W = sizes[1]
    own = jnp.sum(sums_ref[pl.ds(lax.axis_index("dp") * W, W)], axis=0)
    norm_columns(scale, jnp.sum(sums_ref[...], axis=0), norm_ref)
    glat_ref[...] = latent_gradient(sizes, own, *refs[:-2])


def norm_columns(scale, norm, norm_ref):
    channels, width = norm.shape[1], norm_ref.shape[1]
    row = lax.broadcasted_iota(jnp.int32, (channels, width), 0)
    column = lax.broadcasted_iota(jnp.int32, (channels, width), 1)
    pick = (row == column + lax.axis_index("wide") * width).astype(F32)
    norm_ref[...] = (
        lax.dot_general(
            norm, pick, NN, precision=lax.Precision.HIGHEST, preferred_element_type=F32
        )
        * scale
    )


def local(latents, cotangent, norm_gain, norm_bias, w_spatial, w_temporal):
    D, W = lax.axis_size("dp"), lax.axis_size("wide")
    _, frames, rows_here, cols, channels = latents.shape
    cells = rows_here * cols
    rows = frames * cells
    per_group = channels // GROUPS
    count = W * frames * cells * per_group
    shard_s, shard_t = w_spatial.shape[0], w_temporal.shape[0]
    aligned = (channels // W) % 16 == 0 and shard_s % 128 == 0 and shard_t % 128 == 0
    aligned = aligned and W % 4 == 0 and D == 2 and channels == 256
    sizes = (D, W, frames, cells, cols, count, per_group, aligned)
    scale = 1.0 / math.sqrt(D * W * frames * cells)

    lat, cot = latents.reshape(rows, channels), cotangent.reshape(rows, channels)
    gain, bias = norm_gain.reshape(1, channels), norm_bias.reshape(1, channels)

    def over_all(moves):
        pairs = []
        for d in range(D):
            for w in range(W):
                to = moves(d, w)
                pairs.append((d * W + w, to[0] * W + to[1]))
        return pairs

    def send(value, moves):
        return lax.ppermute(value, ("dp", "wide"), over_all(moves))

    R = shard_s + shard_t
    stats, affine, half = call(
        stats_body,
        [
            shape((W, 2, channels), F32),
            shape((2, channels), F32),
            shape((R // 2, channels), BF16),
        ],
        [
            pltpu.VMEM((rows, channels), BF16),
            pltpu.VMEM((1, channels), F32),
            pltpu.VMEM((1, channels), F32),
            pltpu.SemaphoreType.DMA((5,)),
        ],
        in_specs=[HBM] * 5,
        vmem=FIRST_VMEM,
    )(lat, gain, bias, w_spatial, w_temporal)
    cot_t = call(transpose_body, shape((channels, rows), BF16), moved=300_000)(cot)
    firsts = [send(half, lambda d, w: ((d + s) % D, w)) for s in range(1, D)]

    halo = lax.ppermute(cot, "wide", [(w + 1, w) for w in range(W - 1)])
    stats = lax.all_to_all(stats, "wide", split_axis=0, concat_axis=0, tiled=True)
    firsts, stats, halo, cot_t = lax.optimization_barrier((firsts, stats, halo, cot_t))
    pieces = []
    for first in firsts:
        pieces += [first, send(first, lambda d, w: (d, w ^ 1))]

    ride = 128 if aligned else 0
    if aligned:
        terms_s = [shape((D, channels // 2, shard_s), BF16)] * 2
        terms_t = [shape((D, channels // 2, shard_t + ride), BF16)] * 2
    else:
        terms_s = [shape((channels, D * shard_s), BF16)]
        terms_t = [shape((channels, D * shard_t), BF16), shape((D * W, 2, channels), F32)]
    pad = pltpu.VMEM((3, frames, cells + 2 * cols, channels), BF16)
    gsa, *grads_s = call(
        functools.partial(first_body, sizes),
        [shape((rows, channels), BF16)] + terms_s,
        [pltpu.VMEM((D * shard_t, channels), BF16), pad, pltpu.VMEM((channels, rows), BF16)],
        flops=2 * 12 * rows * channels * channels,
        moved=3_000_000,
    )(lat, cot, halo, stats, affine, w_temporal, *pieces)
    spatial, grad, *grads_t = call(
        functools.partial(second_body, sizes),
        [shape((rows, channels), BF16), shape((rows, channels), F32)] + terms_t,
        [
            pltpu.VMEM((D * shard_s, channels), BF16),
            pad,
            pad,
            pltpu.VMEM((channels, rows + 2 * cells), BF16),
        ],
        flops=2 * 21 * rows * channels * channels,
        moved=3_000_000,
    )(lat, cot_t, halo, stats, affine, gsa, w_spatial, *pieces)
    before = lax.ppermute(spatial, "wide", [(w, w + 1) for w in range(W - 1)])
    block_out = call(
        functools.partial(block_body, sizes),
        shape((rows, channels), BF16),
        [pltpu.VMEM((D * shard_t, channels), BF16)],
        flops=2 * 3 * rows * channels * channels,
        moved=1_000_000,
    )(lat, spatial, before, w_temporal, *pieces)

    width = channels // W
    operands = (lat, cot, stats, affine, grad)
    if aligned:
        Z = W // 4

        def over_core(away):
            return send(away, lambda d, w: (d, w ^ 1))

        pairs = []
        for keep, away in (grads_s, grads_t):
            view = (D, Z, 2, width, keep.shape[-1])
            pairs += [keep.reshape(view), over_core(away).reshape(view)]
        plane = call(
            plane_body, [shape((Z, width, R + ride), BF16)] * (2 * D), moved=3_000_000
        )(*pairs)
        seen = [plane[0]] + [
            send(plane[2 * a + b], lambda d, w: ((d + a) % D, w ^ (2 * b)))
            for a, b in ((0, 1), (1, 0), (1, 1))
        ]
        line = call(
            functools.partial(line_body, Z),
            [shape((width, R + ride), BF16)] * Z,
            moved=1_000_000,
        )(*seen)
        terms = [line[0]]
        for s in range(1, Z):
            terms.append(send(line[s], lambda d, w: (d, (w + 4 * s) % W)))
        grad_s, grad_t, norm, grad_latents = call(
            functools.partial(last_body, sizes, scale, Z),
            [
                shape((width, shard_s), F32),
                shape((width, shard_t), F32),
                shape((2, width), F32),
                shape((rows, channels), BF16),
            ],
            moved=1_000_000,
        )(*terms, *operands)
        grad_s, grad_t = grad_s.T, grad_t.T
    else:
        sums = lax.all_to_all(
            grads_t[1], ("dp", "wide"), split_axis=0, concat_axis=0, tiled=True
        )
        norm, grad_latents = call(
            functools.partial(apart_body, sizes, scale),
            [shape((2, width), F32), shape((rows, channels), BF16)],
        )(sums, *operands)
        outs = []
        for full in (grads_s[0], grads_t[0]):
            part = lax.psum_scatter(
                full.astype(F32), "wide", scatter_dimension=0, tiled=True
            ).T.astype(BF16)
            part = lax.psum_scatter(part, "dp", scatter_dimension=0, tiled=True)
            outs.append(part.astype(F32) * scale)
        grad_s, grad_t = outs
    return (
        block_out.reshape(latents.shape),
        grad_latents.reshape(latents.shape),
        grad_s,
        grad_t,
        norm,
    )


def solution(mesh):
    return jax.shard_map(
        local,
        mesh=mesh,
        in_specs=(
            P("dp", "wide", None, None, None),
            P("dp", "wide", None, None, None),
            P(),
            P(),
            P("dp", None),
            P("dp", None),
        ),
        out_specs=(
            P("dp", "wide", None, None, None),
            P("dp", "wide", None, None, None),
            P("dp", "wide"),
            P("dp", "wide"),
            P(None, "wide"),
        ),
        check_vma=False,
    )
```

```python
import functools
import math

import jax
import jax.numpy as jnp
from jax import lax
from jax.experimental import pallas as pl
from jax.experimental.pallas import tpu as pltpu
from jax.sharding import PartitionSpec as P

GROUPS = 32
EPSILON = 1e-05
F32 = jnp.float32
BF16 = jnp.bfloat16
VMEM = pl.BlockSpec(memory_space=pltpu.VMEM)
HBM = pl.BlockSpec(memory_space=pltpu.HBM)
FIRST_VMEM = 60 << 20
NT = (((1,), (1,)), ((), ()))
NN = (((1,), (0,)), ((), ()))


def call(body, out_shapes, scratch=(), flops=0, moved=0, in_specs=None, vmem=40 << 20):
    many = isinstance(out_shapes, (tuple, list))

    def run(*operands):
        return pl.pallas_call(
            body,
            out_shape=out_shapes,
            in_specs=in_specs or [VMEM] * len(operands),
            out_specs=[VMEM] * len(out_shapes) if many else VMEM,
            scratch_shapes=list(scratch),
            compiler_params=pltpu.CompilerParams(vmem_limit_bytes=vmem),
            cost_estimate=pl.CostEstimate(
                flops=flops, bytes_accessed=moved, transcendentals=0
            ),
        )(*operands)

    return run


def shape(dims, kind):
    return jax.ShapeDtypeStruct(dims, kind)


def mm(left, right, dims=NN):
    return lax.dot_general(left, right, dims, preferred_element_type=F32)


def group_total(rows, per_group):
    channels = rows.shape[-1]
    first = lax.broadcasted_iota(jnp.int32, (channels, channels), 0) // per_group
    second = lax.broadcasted_iota(jnp.int32, (channels, channels), 1) // per_group
    same = (first == second).astype(F32)
    return lax.dot_general(
        rows, same, NN, precision=lax.Precision.HIGHEST, preferred_element_type=F32
    )


def stats_body(lat_ref, gain_ref, bias_ref, ws_ref, wt_ref, out_ref, affine_ref, half_ref, *scratch):
    lat_here, gain_here, bias_here, sems = scratch
    core = lax.rem(lax.axis_index("wide"), 2)
    moves, place = [(lat_ref, lat_here), (gain_ref, gain_here), (bias_ref, bias_here)], 0
    for source in (ws_ref, wt_ref):
        half = source.shape[0] // 2
        start = pl.multiple_of(core * half, 16)
        moves.append((source.at[pl.ds(start, half)], half_ref.at[pl.ds(place, half)]))
        place += half
    copies = [pltpu.make_async_copy(*move, sems.at[at]) for at, move in enumerate(moves)]
    for copy in copies:
        copy.start()
    for copy in copies[:3]:
        copy.wait()
    affine_ref[0:1] = gain_here[...]
    affine_ref[1:2] = bias_here[...]
    x = lat_here[...].astype(F32)
    both = jnp.concatenate(
        [jnp.sum(x, axis=0, keepdims=True), jnp.sum(x * x, axis=0, keepdims=True)], axis=0
    )
    out_ref[...] = jnp.broadcast_to(both[None], out_ref.shape)
    for copy in copies[3:]:
        copy.wait()


def transpose_body(cot_ref, out_ref):
    out_ref[...] = cot_ref[...].astype(F32).T.astype(BF16)


def fill_weights(full, shard_ref, pieces, offset, D):
    d = lax.axis_index("dp")
    core = lax.rem(lax.axis_index("wide"), 2)
    n = shard_ref.shape[0]
    half = n // 2
    full[pl.ds(pl.multiple_of(d * n, 16), n)] = shard_ref[...]
    for s in range(1, D):
        source = lax.rem(d + D - s, D)
        for which in range(2):
            holder = core if which == 0 else 1 - core
            start = pl.multiple_of(source * n + holder * half, 16)
            full[pl.ds(start, half)] = pieces[2 * (s - 1) + which][offset : offset + half]


def whiten(lat, stats, count, per_group):
    total = group_total(jnp.sum(stats, axis=0), per_group) / count
    mean = total[0:1]
    inv_std = 1.0 / jnp.sqrt(total[1:2] - mean * mean + EPSILON)
    return (lat.astype(F32) - mean) * inv_std, inv_std


def store_shifted(pad_ref, values, frames, cells, cols):
    total = frames * cells
    column = lax.broadcasted_iota(jnp.int32, (total, 1), 0) % cols
    left = jnp.where(column == 0, 0.0, pltpu.roll(values, 1, 0))
    right = jnp.where(column == cols - 1, 0.0, pltpu.roll(values, total - 1, 0))
    edge = jnp.zeros((cols, values.shape[1]), BF16)
    for at, form in enumerate((left, values, right)):
        low = form.astype(BF16)
        for f in range(frames):
            pad_ref[at, f, 0:cols] = edge
            pad_ref[at, f, cols : cols + cells] = low[f * cells : (f + 1) * cells]
            pad_ref[at, f, cols + cells :] = edge


def window(pad_ref, dy, dx, frames, cells, cols):
    return jnp.concatenate(
        [pad_ref[dx, f, dy * cols : dy * cols + cells] for f in range(frames)], axis=0
    )


def in_parts(total):
    high = total.astype(BF16).astype(F32)
    return jnp.concatenate([high, total - high], axis=0).astype(BF16)


def from_parts(terms):
    total = 0.0
    for term in terms:
        wide = term.astype(F32)
        total = total + (wide[0:8] + wide[8:16])
    return total


def add(terms):
    total = terms[0].astype(F32)
    for term in terms[1:]:
        total += term.astype(F32)
    return total


def core_order(transposed_ref, W, core):
    step = transposed_ref.shape[0] // W
    order = [(2 * j + core) * step for j in range(W // 2)]
    order += [(2 * j + 1 - core) * step for j in range(W // 2)]
    return jnp.concatenate(
        [transposed_ref[pl.ds(pl.multiple_of(at, 16), step)] for at in order], axis=0
    )


def put(block, column, shard, keep_ref, send_ref):
    low = block.astype(BF16)
    if send_ref is None:
        keep_ref[:, column : column + block.shape[1]] = low
        return
    half = block.shape[0] // 2
    for at in range(0, block.shape[1], 128):
        owner, place = (column + at) // shard, (column + at) % shard
        keep_ref[owner, :, place : place + 128] = low[:half, at : at + 128]
        send_ref[owner, :, place : place + 128] = low[half:, at : at + 128]


def normalise(lat_ref, stats_ref, affine_ref, count, per_group):
    white, inv_std = whiten(lat_ref[...], stats_ref[...], count, per_group)
    normed = white * affine_ref[0:1] + affine_ref[1:2]
    return white, normed, jax.nn.sigmoid(normed)


def first_body(sizes, lat_ref, cot_ref, halo_ref, stats_ref, affine_ref, wt_ref, *rest):
    D, W, frames, cells, cols, count, per_group, aligned = sizes
    pieces, rest = rest[: 2 * (D - 1)], rest[2 * (D - 1) :]
    full_wt, act_pad, gsa_t = rest[-3:]
    gsa_ref, keep_ref = rest[:2]
    send_ref = rest[2] if aligned else None
    channels = lat_ref.shape[1]
    core = lax.rem(lax.axis_index("wide"), 2)
    fill_weights(full_wt, wt_ref, pieces, pieces[0].shape[0] - wt_ref.shape[0] // 2, D)
    rows = frames * cells
    extended = jnp.concatenate([cot_ref[...], halo_ref[...]], axis=0)
    gsa = jnp.zeros((rows, channels), F32)
    for k in range(3):
        gsa += mm(
            extended[k * cells : k * cells + rows],
            full_wt[k * channels : (k + 1) * channels],
            NT,
        )
    gsa_ref[...] = gsa.astype(BF16)
    gsa_t[...] = gsa.astype(BF16).astype(F32).T.astype(BF16)
    _, normed, sig = normalise(lat_ref, stats_ref, affine_ref, count, per_group)
    act = (normed * sig).astype(BF16).astype(F32)
    store_shifted(act_pad, act, frames, cells, cols)
    left = core_order(gsa_t, W, core) if aligned else gsa_t[...]
    shard = wt_ref.shape[0] * 3
    for dy in range(3):
        for dx in range(3):
            seen = window(act_pad, dy, dx, frames, cells, cols)
            put(mm(left, seen), (3 * dy + dx) * channels, shard, keep_ref, send_ref)


def second_body(
    sizes, lat_ref, cot_t_ref, halo_ref, stats_ref, affine_ref, gsa_ref, ws_ref, *rest
):
    D, W, frames, cells, cols, count, per_group, aligned = sizes
    pieces, rest = rest[: 2 * (D - 1)], rest[2 * (D - 1) :]
    full_ws, act_pad, gsa_pad, cot_t = rest[-4:]
    spatial_ref, grad_ref, keep_ref, other_ref = rest[:4]
    send_ref = other_ref if aligned else None
    channels = lat_ref.shape[1]
    core = lax.rem(lax.axis_index("wide"), 2)
    fill_weights(full_ws, ws_ref, pieces, 0, D)
    rows = frames * cells
    white, normed, sig = normalise(lat_ref, stats_ref, affine_ref, count, per_group)
    act = (normed * sig).astype(BF16).astype(F32)
    store_shifted(act_pad, act, frames, cells, cols)
    store_shifted(gsa_pad, gsa_ref[...].astype(F32), frames, cells, cols)
    cot_t[:, :rows] = cot_t_ref[...]
    for f in range(2):
        cot_t[:, rows + f * cells : rows + (f + 1) * cells] = (
            halo_ref[f * cells : (f + 1) * cells].astype(F32).T.astype(BF16)
        )
    left = core_order(cot_t, W, core) if aligned else cot_t[...]
    out = jnp.zeros((rows, channels), F32)
    for dy in range(3):
        for dx in range(3):
            tap = 3 * dy + dx
            seen = window(act_pad, dy, dx, frames, cells, cols)
            out += mm(seen, full_ws[tap * channels : (tap + 1) * channels])
    spatial = out.astype(BF16)
    spatial_ref[...] = spatial
    shard = ws_ref.shape[0] // 3
    for k in range(3):
        block = mm(left[:, k * cells : k * cells + rows], spatial)
        put(block, k * channels, shard, keep_ref, send_ref)

    grad = jnp.zeros((rows, channels), F32)
    for dy in range(3):
        for dx in range(3):
            tap = 3 * dy + dx
            seen = window(gsa_pad, 2 - dy, 2 - dx, frames, cells, cols)
            grad += mm(seen, full_ws[tap * channels : (tap + 1) * channels], NT)
    grad = grad * (sig * (1.0 + normed * (1.0 - sig)))
    grad_ref[...] = grad
    gain_term = jnp.sum(grad * white, axis=0, keepdims=True)
    bias_term = jnp.sum(grad, axis=0, keepdims=True)
    if not aligned:
        both = jnp.concatenate([gain_term, bias_term], axis=0)
        other_ref[...] = jnp.broadcast_to(both[None], other_ref.shape)
        return
    d = lax.axis_index("dp")
    quarter = jnp.concatenate(
        [term[:, at : at + 128] for term in (gain_term, bias_term) for at in (0, 128)], axis=0
    )
    low = in_parts(
        jnp.concatenate([jnp.where(d == s, quarter, 0.0) for s in range(2)], axis=0)
    )
    for target in (keep_ref, send_ref):
        for owner in range(D):
            for at in range(0, channels // 2, 16):
                target[owner, at : at + 16, shard:] = low


def block_body(sizes, lat_ref, spatial_ref, before_ref, wt_ref, *rest):
    D, W, frames, cells, cols, count, per_group, aligned = sizes
    pieces = rest[: 2 * (D - 1)]
    block_ref, full_wt = rest[2 * (D - 1) :]
    channels = lat_ref.shape[1]
    fill_weights(full_wt, wt_ref, pieces, pieces[0].shape[0] - wt_ref.shape[0] // 2, D)
    extended = jnp.concatenate([before_ref[...], spatial_ref[...]], axis=0)
    rows = frames * cells
    temporal = jnp.zeros((rows, channels), F32)
    for k in range(3):
        start = (2 - k) * cells
        temporal += mm(
            extended[start : start + rows], full_wt[k * channels : (k + 1) * channels]
        )
    block_ref[...] = (lat_ref[...].astype(F32) + temporal).astype(BF16)


def latent_gradient(sizes, total, lat_ref, cot_ref, stats_ref, affine_ref, grad_ref):
    D, W, frames, cells, cols, count, per_group, aligned = sizes
    white, inv_std = whiten(lat_ref[...], stats_ref[...], count, per_group)
    gain = affine_ref[0:1]
    means = group_total(total * gain, per_group) / count
    inner = inv_std * (grad_ref[...] * gain - means[1:2] - white * means[0:1])
    return (cot_ref[...].astype(F32) + inner).astype(BF16)


def plane_body(keep_s, got_s, keep_t, got_t, *outs):
    d = lax.axis_index("dp")
    y = lax.rem(lax.axis_index("wide") // 2, 2)
    for a in range(2):
        for b in range(2):
            owner, side = lax.rem(d + a, 2), lax.rem(y + b, 2)
            out_s, out_t = outs[2 * a + b], outs[4 + 2 * a + b]
            ride = out_t.shape[-1] - 128
            for z in range(out_s.shape[0]):
                out_s[z] = add([keep_s[owner, z, side], got_s[owner, z, side]]).astype(BF16)
                both = [keep_t[owner, z, side], got_t[owner, z, side]]
                out_t[z, :, :ride] = add([t[:, :ride] for t in both]).astype(BF16)
                out_t[z, :, ride:] = in_parts(from_parts([t[:, ride:] for t in both]))


def line_body(depth, ride, *refs):
    terms, outs = refs[:4], refs[4:]
    z = lax.axis_index("wide") // 4
    width = outs[0].shape[-1] - ride
    for s in range(depth):
        owner = lax.rem(z + s, depth)
        seen = [term[owner] for term in terms]
        outs[s][:, :width] = add([t[:, :width] for t in seen]).astype(BF16)
        if ride:
            outs[s][:, width:] = in_parts(from_parts([t[:, width:] for t in seen]))


def last_body(sizes, scale, depth, *refs):
    terms_s, terms_t = refs[:depth], refs[depth : 2 * depth]
    operands, outs = refs[2 * depth : -4], refs[-4:]
    spatial_ref, temporal_ref, norm_ref, glat_ref = outs
    ride = temporal_ref.shape[1]
    sums = from_parts([term[:, ride:] for term in terms_t])

    def rows_of(part):
        return jnp.concatenate(
            [jnp.concatenate([part[at : at + 1], part[at + 1 : at + 2]], axis=1) for at in (0, 2)],
            axis=0,
        )

    first, second = rows_of(sums[0:4]), rows_of(sums[4:8])
    own = jnp.where(lax.axis_index("dp") == 0, first, second)
    glat_ref[...] = latent_gradient(sizes, own, *operands)
    norm_columns(scale, first + second, norm_ref)
    spatial_ref[...] = add([term[...] for term in terms_s]) * scale
    temporal_ref[...] = add([term[:, :ride] for term in terms_t]) * scale


def apart_body(sizes, scale, sums_ref, *refs):
    norm_ref, glat_ref = refs[-2:]
    W = sizes[1]
    own = jnp.sum(sums_ref[pl.ds(lax.axis_index("dp") * W, W)], axis=0)
    norm_columns(scale, jnp.sum(sums_ref[...], axis=0), norm_ref)
    glat_ref[...] = latent_gradient(sizes, own, *refs[:-2])


def norm_columns(scale, norm, norm_ref):
    channels, width = norm.shape[1], norm_ref.shape[1]
    row = lax.broadcasted_iota(jnp.int32, (channels, width), 0)
    column = lax.broadcasted_iota(jnp.int32, (channels, width), 1)
    pick = (row == column + lax.axis_index("wide") * width).astype(F32)
    norm_ref[...] = (
        lax.dot_general(
            norm, pick, NN, precision=lax.Precision.HIGHEST, preferred_element_type=F32
        )
        * scale
    )


def local(latents, cotangent, norm_gain, norm_bias, w_spatial, w_temporal):
    D, W = lax.axis_size("dp"), lax.axis_size("wide")
    _, frames, rows_here, cols, channels = latents.shape
    cells = rows_here * cols
    rows = frames * cells
    per_group = channels // GROUPS
    count = W * frames * cells * per_group
    shard_s, shard_t = w_spatial.shape[0], w_temporal.shape[0]
    aligned = (channels // W) % 16 == 0 and shard_s % 128 == 0 and shard_t % 128 == 0
    aligned = aligned and W % 4 == 0 and D == 2 and channels == 256
    sizes = (D, W, frames, cells, cols, count, per_group, aligned)
    scale = 1.0 / math.sqrt(D * W * frames * cells)

    lat, cot = latents.reshape(rows, channels), cotangent.reshape(rows, channels)
    gain, bias = norm_gain.reshape(1, channels), norm_bias.reshape(1, channels)

    def over_all(moves):
        pairs = []
        for d in range(D):
            for w in range(W):
                to = moves(d, w)
                pairs.append((d * W + w, to[0] * W + to[1]))
        return pairs

    def send(value, moves):
        return lax.ppermute(value, ("dp", "wide"), over_all(moves))

    R = shard_s + shard_t
    stats, affine, half = call(
        stats_body,
        [
            shape((W, 2, channels), F32),
            shape((2, channels), F32),
            shape((R // 2, channels), BF16),
        ],
        [
            pltpu.VMEM((rows, channels), BF16),
            pltpu.VMEM((1, channels), F32),
            pltpu.VMEM((1, channels), F32),
            pltpu.SemaphoreType.DMA((5,)),
        ],
        in_specs=[HBM] * 5,
        vmem=FIRST_VMEM,
    )(lat, gain, bias, w_spatial, w_temporal)
    cot_t = call(transpose_body, shape((channels, rows), BF16), moved=300_000)(cot)
    firsts = [send(half, lambda d, w: ((d + s) % D, w)) for s in range(1, D)]

    halo = lax.ppermute(cot, "wide", [(w + 1, w) for w in range(W - 1)])
    stats = lax.all_to_all(stats, "wide", split_axis=0, concat_axis=0, tiled=True)
    firsts, stats, halo, cot_t = lax.optimization_barrier((firsts, stats, halo, cot_t))
    pieces = []
    for first in firsts:
        pieces += [first, send(first, lambda d, w: (d, w ^ 1))]

    ride = 128 if aligned else 0
    if aligned:
        terms_s = [shape((D, channels // 2, shard_s), BF16)] * 2
        terms_t = [shape((D, channels // 2, shard_t + ride), BF16)] * 2
    else:
        terms_s = [shape((channels, D * shard_s), BF16)]
        terms_t = [shape((channels, D * shard_t), BF16), shape((D * W, 2, channels), F32)]
    pad = pltpu.VMEM((3, frames, cells + 2 * cols, channels), BF16)
    gsa, *grads_s = call(
        functools.partial(first_body, sizes),
        [shape((rows, channels), BF16)] + terms_s,
        [pltpu.VMEM((D * shard_t, channels), BF16), pad, pltpu.VMEM((channels, rows), BF16)],
        flops=2 * 12 * rows * channels * channels,
        moved=3_000_000,
    )(lat, cot, halo, stats, affine, w_temporal, *pieces)
    spatial, grad, *grads_t = call(
        functools.partial(second_body, sizes),
        [shape((rows, channels), BF16), shape((rows, channels), F32)] + terms_t,
        [
            pltpu.VMEM((D * shard_s, channels), BF16),
            pad,
            pad,
            pltpu.VMEM((channels, rows + 2 * cells), BF16),
        ],
        flops=2 * 21 * rows * channels * channels,
        moved=3_000_000,
    )(lat, cot_t, halo, stats, affine, gsa, w_spatial, *pieces)
    before = lax.ppermute(spatial, "wide", [(w, w + 1) for w in range(W - 1)])
    block_out = call(
        functools.partial(block_body, sizes),
        shape((rows, channels), BF16),
        [pltpu.VMEM((D * shard_t, channels), BF16)],
        flops=2 * 3 * rows * channels * channels,
        moved=1_000_000,
    )(lat, spatial, before, w_temporal, *pieces)

    width = channels // W
    operands = (lat, cot, stats, affine, grad)
    if aligned:
        Z = W // 4

        def over_core(away):
            return send(away, lambda d, w: (d, w ^ 1))

        pairs = []
        for keep, away in (grads_s, grads_t):
            view = (D, Z, 2, width, keep.shape[-1])
            pairs += [keep.reshape(view), over_core(away).reshape(view)]
        plane = call(
            plane_body,
            [shape((Z, width, shard_s), BF16)] * 4 + [shape((Z, width, shard_t + ride), BF16)] * 4,
            moved=3_000_000,
        )(*pairs)
        parts = []
        for sums, extra in ((plane[:4], 0), (plane[4:], ride)):
            seen = [sums[0]] + [
                send(sums[2 * a + b], lambda d, w: ((d + a) % D, w ^ (2 * b)))
                for a, b in ((0, 1), (1, 0), (1, 1))
            ]
            line = call(
                functools.partial(line_body, Z, extra),
                [shape((width, sums[0].shape[-1]), BF16)] * Z,
                moved=1_000_000,
            )(*seen)
            parts.append([line[0]])
            for s in range(1, Z):
                parts[-1].append(send(line[s], lambda d, w: (d, (w + 4 * s) % W)))
        terms = parts[0] + parts[1]
        grad_s, grad_t, norm, grad_latents = call(
            functools.partial(last_body, sizes, scale, Z),
            [
                shape((width, shard_s), F32),
                shape((width, shard_t), F32),
                shape((2, width), F32),
                shape((rows, channels), BF16),
            ],
            moved=1_000_000,
        )(*terms, *operands)
        grad_s, grad_t = grad_s.T, grad_t.T
    else:
        sums = lax.all_to_all(
            grads_t[1], ("dp", "wide"), split_axis=0, concat_axis=0, tiled=True
        )
        norm, grad_latents = call(
            functools.partial(apart_body, sizes, scale),
            [shape((2, width), F32), shape((rows, channels), BF16)],
        )(sums, *operands)
        outs = []
        for full in (grads_s[0], grads_t[0]):
            part = lax.psum_scatter(
                full.astype(F32), "wide", scatter_dimension=0, tiled=True
            ).T.astype(BF16)
            part = lax.psum_scatter(part, "dp", scatter_dimension=0, tiled=True)
            outs.append(part.astype(F32) * scale)
        grad_s, grad_t = outs
    return (
        block_out.reshape(latents.shape),
        grad_latents.reshape(latents.shape),
        grad_s,
        grad_t,
        norm,
    )


def solution(mesh):
    return jax.shard_map(
        local,
        mesh=mesh,
        in_specs=(
            P("dp", "wide", None, None, None),
            P("dp", "wide", None, None, None),
            P(),
            P(),
            P("dp", None),
            P("dp", None),
        ),
        out_specs=(
            P("dp", "wide", None, None, None),
            P("dp", "wide", None, None, None),
            P("dp", "wide"),
            P("dp", "wide"),
            P(None, "wide"),
        ),
        check_vma=False,
    )
```

```python
import functools
import math

import jax
import jax.numpy as jnp
from jax import lax
from jax.experimental import pallas as pl
from jax.experimental.pallas import tpu as pltpu
from jax.sharding import PartitionSpec as P

GROUPS = 32
EPSILON = 1e-05
F32 = jnp.float32
BF16 = jnp.bfloat16
VMEM = pl.BlockSpec(memory_space=pltpu.VMEM)
HBM = pl.BlockSpec(memory_space=pltpu.HBM)
FIRST_VMEM = 60 << 20
NT = (((1,), (1,)), ((), ()))
NN = (((1,), (0,)), ((), ()))


def call(body, out_shapes, scratch=(), flops=0, moved=0, in_specs=None, vmem=40 << 20):
    many = isinstance(out_shapes, (tuple, list))

    def run(*operands):
        return pl.pallas_call(
            body,
            out_shape=out_shapes,
            in_specs=in_specs or [VMEM] * len(operands),
            out_specs=[VMEM] * len(out_shapes) if many else VMEM,
            scratch_shapes=list(scratch),
            compiler_params=pltpu.CompilerParams(vmem_limit_bytes=vmem),
            cost_estimate=pl.CostEstimate(
                flops=flops, bytes_accessed=moved, transcendentals=0
            ),
        )(*operands)

    return run


def shape(dims, kind):
    return jax.ShapeDtypeStruct(dims, kind)


def mm(left, right, dims=NN):
    return lax.dot_general(left, right, dims, preferred_element_type=F32)


def group_total(rows, per_group):
    channels = rows.shape[-1]
    first = lax.broadcasted_iota(jnp.int32, (channels, channels), 0) // per_group
    second = lax.broadcasted_iota(jnp.int32, (channels, channels), 1) // per_group
    same = (first == second).astype(F32)
    return lax.dot_general(
        rows, same, NN, precision=lax.Precision.HIGHEST, preferred_element_type=F32
    )


def stats_body(lat_ref, gain_ref, bias_ref, ws_ref, wt_ref, out_ref, affine_ref, half_ref, *scratch):
    lat_here, gain_here, bias_here, sems = scratch
    core = lax.rem(lax.axis_index("wide"), 2)
    moves, place = [(lat_ref, lat_here), (gain_ref, gain_here), (bias_ref, bias_here)], 0
    for source in (ws_ref, wt_ref):
        half = source.shape[0] // 2
        start = pl.multiple_of(core * half, 16)
        moves.append((source.at[pl.ds(start, half)], half_ref.at[pl.ds(place, half)]))
        place += half
    copies = [pltpu.make_async_copy(*move, sems.at[at]) for at, move in enumerate(moves)]
    for copy in copies:
        copy.start()
    for copy in copies[:3]:
        copy.wait()
    affine_ref[0:1] = gain_here[...]
    affine_ref[1:2] = bias_here[...]
    x = lat_here[...].astype(F32)
    both = jnp.concatenate(
        [jnp.sum(x, axis=0, keepdims=True), jnp.sum(x * x, axis=0, keepdims=True)], axis=0
    )
    out_ref[...] = jnp.broadcast_to(both[None], out_ref.shape)
    for copy in copies[3:]:
        copy.wait()


def transpose_body(cot_ref, out_ref):
    out_ref[...] = cot_ref[...].astype(F32).T.astype(BF16)


def fill_weights(full, shard_ref, pieces, offset, D):
    d = lax.axis_index("dp")
    core = lax.rem(lax.axis_index("wide"), 2)
    n = shard_ref.shape[0]
    half = n // 2
    full[pl.ds(pl.multiple_of(d * n, 16), n)] = shard_ref[...]
    for s in range(1, D):
        source = lax.rem(d + D - s, D)
        for which in range(2):
            holder = core if which == 0 else 1 - core
            start = pl.multiple_of(source * n + holder * half, 16)
            full[pl.ds(start, half)] = pieces[2 * (s - 1) + which][offset : offset + half]


def group_params(stats, count, per_group):
    total = group_total(jnp.sum(stats, axis=0), per_group) / count
    mean = total[0:1]
    return jnp.concatenate(
        [mean, 1.0 / jnp.sqrt(total[1:2] - mean * mean + EPSILON)], axis=0
    )


def whiten(lat, params):
    return (lat.astype(F32) - params[0:1]) * params[1:2]


def store_shifted(pad_ref, values, frames, cells, cols):
    total = frames * cells
    column = lax.broadcasted_iota(jnp.int32, (total, 1), 0) % cols
    left = jnp.where(column == 0, 0.0, pltpu.roll(values, 1, 0))
    right = jnp.where(column == cols - 1, 0.0, pltpu.roll(values, total - 1, 0))
    edge = jnp.zeros((cols, values.shape[1]), BF16)
    for at, form in enumerate((left, values, right)):
        low = form.astype(BF16)
        for f in range(frames):
            pad_ref[at, f, 0:cols] = edge
            pad_ref[at, f, cols : cols + cells] = low[f * cells : (f + 1) * cells]
            pad_ref[at, f, cols + cells :] = edge


def window(pad_ref, dy, dx, frames, cells, cols):
    return jnp.concatenate(
        [pad_ref[dx, f, dy * cols : dy * cols + cells] for f in range(frames)], axis=0
    )


def in_parts(total):
    high = total.astype(BF16).astype(F32)
    return jnp.concatenate([high, total - high], axis=0).astype(BF16)


def from_parts(terms):
    total = 0.0
    for term in terms:
        wide = term.astype(F32)
        total = total + (wide[0:8] + wide[8:16])
    return total


def add(terms):
    total = terms[0].astype(F32)
    for term in terms[1:]:
        total += term.astype(F32)
    return total


def core_order(transposed_ref, W, core):
    step = transposed_ref.shape[0] // W
    order = [(2 * j + core) * step for j in range(W // 2)]
    order += [(2 * j + 1 - core) * step for j in range(W // 2)]
    return jnp.concatenate(
        [transposed_ref[pl.ds(pl.multiple_of(at, 16), step)] for at in order], axis=0
    )


def put(block, column, shard, keep_ref, send_ref):
    low = block.astype(BF16)
    if send_ref is None:
        keep_ref[:, column : column + block.shape[1]] = low
        return
    half = block.shape[0] // 2
    for at in range(0, block.shape[1], 128):
        owner, place = (column + at) // shard, (column + at) % shard
        keep_ref[owner, :, place : place + 128] = low[:half, at : at + 128]
        send_ref[owner, :, place : place + 128] = low[half:, at : at + 128]


def normalise(lat_ref, params, affine_ref):
    white = whiten(lat_ref[...], params)
    normed = white * affine_ref[0:1] + affine_ref[1:2]
    return white, normed, jax.nn.sigmoid(normed)


def pick_halo(near_ref, next_ref):
    core = lax.rem(lax.axis_index("wide"), 2)
    return jnp.where(core == 0, near_ref[...].astype(F32), next_ref[...].astype(F32))


def first_body(sizes, lat_ref, cot_ref, near_ref, next_ref, stats_ref, affine_ref, wt_ref, *rest):
    D, W, frames, cells, cols, count, per_group, aligned = sizes
    pieces, rest = rest[: 2 * (D - 1)], rest[2 * (D - 1) :]
    full_wt, act_pad, gsa_t = rest[-3:]
    gsa_ref, params_ref, seen_ref, keep_ref = rest[:4]
    send_ref = rest[4] if aligned else None
    channels = lat_ref.shape[1]
    core = lax.rem(lax.axis_index("wide"), 2)
    fill_weights(full_wt, wt_ref, pieces, pieces[0].shape[0] - wt_ref.shape[0] // 2, D)
    rows = frames * cells
    halo = pick_halo(near_ref, next_ref).astype(BF16)
    extended = jnp.concatenate([cot_ref[...], halo], axis=0)
    gsa = jnp.zeros((rows, channels), F32)
    for k in range(3):
        gsa += mm(
            extended[k * cells : k * cells + rows],
            full_wt[k * channels : (k + 1) * channels],
            NT,
        )
    gsa_ref[...] = gsa.astype(BF16)
    gsa_t[...] = gsa.astype(BF16).astype(F32).T.astype(BF16)
    params = group_params(stats_ref[...], count, per_group)
    params_ref[...] = params
    _, normed, sig = normalise(lat_ref, params, affine_ref)
    act = (normed * sig).astype(BF16).astype(F32)
    store_shifted(act_pad, act, frames, cells, cols)
    left = core_order(gsa_t, W, core) if aligned else gsa_t[...]
    shard = wt_ref.shape[0] * 3
    for dy in range(3):
        for dx in range(3):
            at = (3 * dy + dx) * channels
            seen = window(act_pad, dy, dx, frames, cells, cols)
            seen_ref[:, at : at + channels] = seen
            put(mm(left, seen), at, shard, keep_ref, send_ref)


def second_body(
    sizes,
    lat_ref,
    cot_t_ref,
    near_ref,
    next_ref,
    params_ref,
    affine_ref,
    gsa_ref,
    seen_ref,
    ws_ref,
    *rest,
):
    D, W, frames, cells, cols, count, per_group, aligned = sizes
    pieces, rest = rest[: 2 * (D - 1)], rest[2 * (D - 1) :]
    full_ws, side_ws, gsa_pad, gsa_seen, cot_t = rest[-5:]
    spatial_ref, grad_ref, keep_ref, other_ref = rest[:4]
    send_ref = other_ref if aligned else None
    channels = lat_ref.shape[1]
    core = lax.rem(lax.axis_index("wide"), 2)
    fill_weights(full_ws, ws_ref, pieces, 0, D)
    rows = frames * cells
    store_shifted(gsa_pad, gsa_ref[...].astype(F32), frames, cells, cols)
    cot_t[:, :rows] = cot_t_ref[...]
    cot_t[:, rows : rows + 2 * cells] = (
        pick_halo(near_ref, next_ref)[: 2 * cells].T.astype(BF16)
    )
    left = core_order(cot_t, W, core) if aligned else cot_t[...]
    spatial = mm(seen_ref[...], full_ws[...]).astype(BF16)
    spatial_ref[...] = spatial
    shard = ws_ref.shape[0] // 3
    for k in range(3):
        block = mm(left[:, k * cells : k * cells + rows], spatial)
        put(block, k * channels, shard, keep_ref, send_ref)

    for dy in range(3):
        for dx in range(3):
            at = (3 * dy + dx) * channels
            gsa_seen[:, at : at + channels] = window(
                gsa_pad, 2 - dy, 2 - dx, frames, cells, cols
            )
            side_ws[:, at : at + channels] = full_ws[at : at + channels]
    grad = mm(gsa_seen[...], side_ws[...], NT)
    white, normed, sig = normalise(lat_ref, params_ref[...], affine_ref)
    grad = grad * (sig * (1.0 + normed * (1.0 - sig)))
    grad_ref[...] = grad
    gain_term = jnp.sum(grad * white, axis=0, keepdims=True)
    bias_term = jnp.sum(grad, axis=0, keepdims=True)
    if not aligned:
        both = jnp.concatenate([gain_term, bias_term], axis=0)
        other_ref[...] = jnp.broadcast_to(both[None], other_ref.shape)
        return
    d = lax.axis_index("dp")
    quarter = jnp.concatenate(
        [term[:, at : at + 128] for term in (gain_term, bias_term) for at in (0, 128)], axis=0
    )
    low = in_parts(
        jnp.concatenate([jnp.where(d == s, quarter, 0.0) for s in range(2)], axis=0)
    )
    for target in (keep_ref, send_ref):
        for owner in range(D):
            for at in range(0, channels // 2, 16):
                target[owner, at : at + 16, shard:] = low


def block_body(sizes, lat_ref, spatial_ref, before_ref, wt_ref, *rest):
    D, W, frames, cells, cols, count, per_group, aligned = sizes
    pieces = rest[: 2 * (D - 1)]
    block_ref, full_wt = rest[2 * (D - 1) :]
    channels = lat_ref.shape[1]
    fill_weights(full_wt, wt_ref, pieces, pieces[0].shape[0] - wt_ref.shape[0] // 2, D)
    extended = jnp.concatenate([before_ref[...], spatial_ref[...]], axis=0)
    rows = frames * cells
    temporal = jnp.zeros((rows, channels), F32)
    for k in range(3):
        start = (2 - k) * cells
        temporal += mm(
            extended[start : start + rows], full_wt[k * channels : (k + 1) * channels]
        )
    block_ref[...] = (lat_ref[...].astype(F32) + temporal).astype(BF16)


def latent_gradient(sizes, total, lat_ref, cot_ref, params_ref, affine_ref, grad_ref):
    count, per_group = sizes[5:7]
    white, inv_std = whiten(lat_ref[...], params_ref[...]), params_ref[1:2]
    gain = affine_ref[0:1]
    means = group_total(total * gain, per_group) / count
    inner = inv_std * (grad_ref[...] * gain - means[1:2] - white * means[0:1])
    return (cot_ref[...].astype(F32) + inner).astype(BF16)


def plane_body(keep_s, got_s, keep_t, got_t, *outs):
    d = lax.axis_index("dp")
    y = lax.rem(lax.axis_index("wide") // 2, 2)
    split = keep_s.shape[-1]
    ride = outs[0].shape[-1] - 128
    for a in range(2):
        for b in range(2):
            owner, side = lax.rem(d + a, 2), lax.rem(y + b, 2)
            out = outs[2 * a + b]
            for z in range(out.shape[0]):
                out[z, :, :split] = add([keep_s[owner, z, side], got_s[owner, z, side]]).astype(
                    BF16
                )
                both = [keep_t[owner, z, side], got_t[owner, z, side]]
                out[z, :, split:ride] = add([t[:, : ride - split] for t in both]).astype(BF16)
                out[z, :, ride:] = in_parts(from_parts([t[:, ride - split :] for t in both]))


def line_body(depth, *refs):
    terms, outs = refs[:4], refs[4:]
    z = lax.axis_index("wide") // 4
    ride = outs[0].shape[-1] - 128
    for s in range(depth):
        owner = lax.rem(z + s, depth)
        seen = [term[owner] for term in terms]
        outs[s][:, :ride] = add([t[:, :ride] for t in seen]).astype(BF16)
        outs[s][:, ride:] = in_parts(from_parts([t[:, ride:] for t in seen]))


def last_body(sizes, scale, depth, *refs):
    terms, operands, outs = refs[:depth], refs[depth:-4], refs[-4:]
    spatial_ref, temporal_ref, norm_ref, glat_ref = outs
    split = spatial_ref.shape[1]
    ride = terms[0].shape[1] - 128
    sums = from_parts([term[:, ride:] for term in terms])

    def rows_of(part):
        return jnp.concatenate(
            [jnp.concatenate([part[at : at + 1], part[at + 1 : at + 2]], axis=1) for at in (0, 2)],
            axis=0,
        )

    first, second = rows_of(sums[0:4]), rows_of(sums[4:8])
    own = jnp.where(lax.axis_index("dp") == 0, first, second)
    glat_ref[...] = latent_gradient(sizes, own, *operands)
    norm_columns(scale, first + second, norm_ref)
    total = add([term[:, :ride] for term in terms]) * scale
    spatial_ref[...] = total[:, :split]
    temporal_ref[...] = total[:, split:]


def apart_body(sizes, scale, sums_ref, *refs):
    norm_ref, glat_ref = refs[-2:]
    W = sizes[1]
    own = jnp.sum(sums_ref[pl.ds(lax.axis_index("dp") * W, W)], axis=0)
    norm_columns(scale, jnp.sum(sums_ref[...], axis=0), norm_ref)
    glat_ref[...] = latent_gradient(sizes, own, *refs[:-2])


def norm_columns(scale, norm, norm_ref):
    channels, width = norm.shape[1], norm_ref.shape[1]
    row = lax.broadcasted_iota(jnp.int32, (channels, width), 0)
    column = lax.broadcasted_iota(jnp.int32, (channels, width), 1)
    pick = (row == column + lax.axis_index("wide") * width).astype(F32)
    norm_ref[...] = (
        lax.dot_general(
            norm, pick, NN, precision=lax.Precision.HIGHEST, preferred_element_type=F32
        )
        * scale
    )


def local(latents, cotangent, norm_gain, norm_bias, w_spatial, w_temporal):
    D, W = lax.axis_size("dp"), lax.axis_size("wide")
    _, frames, rows_here, cols, channels = latents.shape
    cells = rows_here * cols
    rows = frames * cells
    per_group = channels // GROUPS
    count = W * frames * cells * per_group
    shard_s, shard_t = w_spatial.shape[0], w_temporal.shape[0]
    aligned = (channels // W) % 16 == 0 and shard_s % 128 == 0 and shard_t % 128 == 0
    aligned = aligned and W % 4 == 0 and D == 2 and channels == 256
    sizes = (D, W, frames, cells, cols, count, per_group, aligned)
    scale = 1.0 / math.sqrt(D * W * frames * cells)

    lat, cot = latents.reshape(rows, channels), cotangent.reshape(rows, channels)
    gain, bias = norm_gain.reshape(1, channels), norm_bias.reshape(1, channels)

    def over_all(moves):
        pairs = []
        for d in range(D):
            for w in range(W):
                to = moves(d, w)
                pairs.append((d * W + w, to[0] * W + to[1]))
        return pairs

    def send(value, moves):
        return lax.ppermute(value, ("dp", "wide"), over_all(moves))

    R = shard_s + shard_t
    stats, affine, half = call(
        stats_body,
        [
            shape((W, 2, channels), F32),
            shape((2, channels), F32),
            shape((R // 2, channels), BF16),
        ],
        [
            pltpu.VMEM((rows, channels), BF16),
            pltpu.VMEM((1, channels), F32),
            pltpu.VMEM((1, channels), F32),
            pltpu.SemaphoreType.DMA((5,)),
        ],
        in_specs=[HBM] * 5,
        vmem=FIRST_VMEM,
    )(lat, gain, bias, w_spatial, w_temporal)
    cot_t = call(transpose_body, shape((channels, rows), BF16), moved=300_000)(cot)
    firsts = [send(half, lambda d, w: ((d + s) % D, w)) for s in range(1, D)]

    next_cot = lax.ppermute(cot, "wide", [(w + 1, w) for w in range(1, W - 1, 2)])
    near_cot = send(cot, lambda d, w: (d, w ^ 1))
    stats = lax.all_to_all(stats, "wide", split_axis=0, concat_axis=0, tiled=True)
    firsts, stats, next_cot, cot_t = lax.optimization_barrier((firsts, stats, next_cot, cot_t))
    pieces = []
    for first in firsts:
        pieces += [first, send(first, lambda d, w: (d, w ^ 1))]

    ride = 128 if aligned else 0
    if aligned:
        terms_s = [shape((D, channels // 2, shard_s), BF16)] * 2
        terms_t = [shape((D, channels // 2, shard_t + ride), BF16)] * 2
    else:
        terms_s = [shape((channels, D * shard_s), BF16)]
        terms_t = [shape((channels, D * shard_t), BF16), shape((D * W, 2, channels), F32)]
    pad = pltpu.VMEM((3, frames, cells + 2 * cols, channels), BF16)
    taps = D * shard_s
    gsa, params, seen, *grads_s = call(
        functools.partial(first_body, sizes),
        [
            shape((rows, channels), BF16),
            shape((2, channels), F32),
            shape((rows, taps), BF16),
        ]
        + terms_s,
        [pltpu.VMEM((D * shard_t, channels), BF16), pad, pltpu.VMEM((channels, rows), BF16)],
        flops=2 * 12 * rows * channels * channels,
        moved=3_000_000,
    )(lat, cot, near_cot, next_cot, stats, affine, w_temporal, *pieces)
    spatial, grad, *grads_t = call(
        functools.partial(second_body, sizes),
        [shape((rows, channels), BF16), shape((rows, channels), F32)] + terms_t,
        [
            pltpu.VMEM((taps, channels), BF16),
            pltpu.VMEM((channels, taps), BF16),
            pad,
            pltpu.VMEM((rows, taps), BF16),
            pltpu.VMEM((channels, rows + 2 * cells), BF16),
        ],
        flops=2 * 21 * rows * channels * channels,
        moved=3_000_000,
    )(lat, cot_t, near_cot, next_cot, params, affine, gsa, seen, w_spatial, *pieces)
    before = lax.ppermute(spatial, "wide", [(w, w + 1) for w in range(W - 1)])
    block_out = call(
        functools.partial(block_body, sizes),
        shape((rows, channels), BF16),
        [pltpu.VMEM((D * shard_t, channels), BF16)],
        flops=2 * 3 * rows * channels * channels,
        moved=1_000_000,
    )(lat, spatial, before, w_temporal, *pieces)

    width = channels // W
    operands = (lat, cot, params, affine, grad)
    if aligned:
        Z = W // 4

        def over_core(away):
            return send(away, lambda d, w: (d, w ^ 1))

        pairs = []
        for keep, away in (grads_s, grads_t):
            view = (D, Z, 2, width, keep.shape[-1])
            pairs += [keep.reshape(view), over_core(away).reshape(view)]
        plane = call(
            plane_body, [shape((Z, width, R + ride), BF16)] * (2 * D), moved=3_000_000
        )(*pairs)
        seen = [plane[0]] + [
            send(plane[2 * a + b], lambda d, w: ((d + a) % D, w ^ (2 * b)))
            for a, b in ((0, 1), (1, 0), (1, 1))
        ]
        line = call(
            functools.partial(line_body, Z),
            [shape((width, R + ride), BF16)] * Z,
            moved=1_000_000,
        )(*seen)
        terms = [line[0]]
        for s in range(1, Z):
            terms.append(send(line[s], lambda d, w: (d, (w + 4 * s) % W)))
        grad_s, grad_t, norm, grad_latents = call(
            functools.partial(last_body, sizes, scale, Z),
            [
                shape((width, shard_s), F32),
                shape((width, shard_t), F32),
                shape((2, width), F32),
                shape((rows, channels), BF16),
            ],
            moved=1_000_000,
        )(*terms, *operands)
        grad_s, grad_t = grad_s.T, grad_t.T
    else:
        sums = lax.all_to_all(
            grads_t[1], ("dp", "wide"), split_axis=0, concat_axis=0, tiled=True
        )
        norm, grad_latents = call(
            functools.partial(apart_body, sizes, scale),
            [shape((2, width), F32), shape((rows, channels), BF16)],
        )(sums, *operands)
        outs = []
        for full in (grads_s[0], grads_t[0]):
            part = lax.psum_scatter(
                full.astype(F32), "wide", scatter_dimension=0, tiled=True
            ).T.astype(BF16)
            part = lax.psum_scatter(part, "dp", scatter_dimension=0, tiled=True)
            outs.append(part.astype(F32) * scale)
        grad_s, grad_t = outs
    return (
        block_out.reshape(latents.shape),
        grad_latents.reshape(latents.shape),
        grad_s,
        grad_t,
        norm,
    )


def solution(mesh):
    return jax.shard_map(
        local,
        mesh=mesh,
        in_specs=(
            P("dp", "wide", None, None, None),
            P("dp", "wide", None, None, None),
            P(),
            P(),
            P("dp", None),
            P("dp", None),
        ),
        out_specs=(
            P("dp", "wide", None, None, None),
            P("dp", "wide", None, None, None),
            P("dp", "wide"),
            P("dp", "wide"),
            P(None, "wide"),
        ),
        check_vma=False,
    )
```

```python
import functools
import math

import jax
import jax.numpy as jnp
from jax import lax
from jax.experimental import pallas as pl
from jax.experimental.pallas import tpu as pltpu
from jax.sharding import PartitionSpec as P

GROUPS = 32
EPSILON = 1e-05
F32 = jnp.float32
BF16 = jnp.bfloat16
VMEM = pl.BlockSpec(memory_space=pltpu.VMEM)
HBM = pl.BlockSpec(memory_space=pltpu.HBM)
FIRST_VMEM = 60 << 20
NT = (((1,), (1,)), ((), ()))
NN = (((1,), (0,)), ((), ()))


def call(body, out_shapes, scratch=(), flops=0, moved=0, in_specs=None, vmem=40 << 20):
    many = isinstance(out_shapes, (tuple, list))

    def run(*operands):
        return pl.pallas_call(
            body,
            out_shape=out_shapes,
            in_specs=in_specs or [VMEM] * len(operands),
            out_specs=[VMEM] * len(out_shapes) if many else VMEM,
            scratch_shapes=list(scratch),
            compiler_params=pltpu.CompilerParams(vmem_limit_bytes=vmem),
            cost_estimate=pl.CostEstimate(
                flops=flops, bytes_accessed=moved, transcendentals=0
            ),
        )(*operands)

    return run


def shape(dims, kind):
    return jax.ShapeDtypeStruct(dims, kind)


def mm(left, right, dims=NN):
    return lax.dot_general(left, right, dims, preferred_element_type=F32)


def group_total(rows, per_group):
    channels = rows.shape[-1]
    first = lax.broadcasted_iota(jnp.int32, (channels, channels), 0) // per_group
    second = lax.broadcasted_iota(jnp.int32, (channels, channels), 1) // per_group
    same = (first == second).astype(F32)
    return lax.dot_general(
        rows, same, NN, precision=lax.Precision.HIGHEST, preferred_element_type=F32
    )


def stats_body(lat_ref, gain_ref, bias_ref, ws_ref, wt_ref, out_ref, half_s_ref, half_t_ref, *scratch):
    lat_here, gain_here, bias_here, sems = scratch
    core = lax.rem(lax.axis_index("wide"), 2)
    moves = [(lat_ref, lat_here), (gain_ref, gain_here), (bias_ref, bias_here)]
    for source, target in ((wt_ref, half_t_ref), (ws_ref, half_s_ref)):
        half = target.shape[0]
        start = pl.multiple_of(core * half, 16)
        moves.append((source.at[pl.ds(start, half)], target))
    copies = [pltpu.make_async_copy(*move, sems.at[at]) for at, move in enumerate(moves)]
    for copy in copies:
        copy.start()
    for copy in copies[:3]:
        copy.wait()
    x = lat_here[...].astype(F32)
    both = jnp.concatenate(
        [
            jnp.sum(x, axis=0, keepdims=True),
            jnp.sum(x * x, axis=0, keepdims=True),
            gain_here[...],
            bias_here[...],
        ],
        axis=0,
    )
    out_ref[...] = jnp.broadcast_to(both[None], out_ref.shape)
    for copy in copies[3:]:
        copy.wait()


def fill_weights(full, shard_ref, pieces, D):
    d = lax.axis_index("dp")
    core = lax.rem(lax.axis_index("wide"), 2)
    n = shard_ref.shape[0]
    half = n // 2
    full[pl.ds(pl.multiple_of(d * n, 16), n)] = shard_ref[...]
    for s in range(1, D):
        source = lax.rem(d + D - s, D)
        for which in range(2):
            holder = core if which == 0 else 1 - core
            start = pl.multiple_of(source * n + holder * half, 16)
            full[pl.ds(start, half)] = pieces[2 * (s - 1) + which][...]


def group_params(stats, count, per_group):
    total = group_total(jnp.sum(stats, axis=0), per_group) / count
    mean = total[0:1]
    return jnp.concatenate(
        [mean, 1.0 / jnp.sqrt(total[1:2] - mean * mean + EPSILON)], axis=0
    )


def whiten(lat, params):
    return (lat.astype(F32) - params[0:1]) * params[1:2]


def store_shifted(pad_ref, values, frames, cells, cols):
    total = frames * cells
    column = lax.broadcasted_iota(jnp.int32, (total, 1), 0) % cols
    left = jnp.where(column == 0, 0.0, pltpu.roll(values, 1, 0))
    right = jnp.where(column == cols - 1, 0.0, pltpu.roll(values, total - 1, 0))
    edge = jnp.zeros((cols, values.shape[1]), BF16)
    for at, form in enumerate((left, values, right)):
        low = form.astype(BF16)
        for f in range(frames):
            pad_ref[at, f, 0:cols] = edge
            pad_ref[at, f, cols : cols + cells] = low[f * cells : (f + 1) * cells]
            pad_ref[at, f, cols + cells :] = edge


def window(pad_ref, dy, dx, frames, cells, cols):
    return jnp.concatenate(
        [pad_ref[dx, f, dy * cols : dy * cols + cells] for f in range(frames)], axis=0
    )


def in_parts(total):
    high = total.astype(BF16).astype(F32)
    return jnp.concatenate([high, total - high], axis=0).astype(BF16)


def from_parts(terms):
    total = 0.0
    for term in terms:
        wide = term.astype(F32)
        total = total + (wide[0:8] + wide[8:16])
    return total


def add(terms):
    total = terms[0].astype(F32)
    for term in terms[1:]:
        total += term.astype(F32)
    return total


def core_order(transposed_ref, W, core):
    step = transposed_ref.shape[0] // W
    order = [(2 * j + core) * step for j in range(W // 2)]
    order += [(2 * j + 1 - core) * step for j in range(W // 2)]
    return jnp.concatenate(
        [transposed_ref[pl.ds(pl.multiple_of(at, 16), step)] for at in order], axis=0
    )


def put(block, column, shard, keep_ref, send_ref):
    low = block.astype(BF16)
    if send_ref is None:
        keep_ref[:, column : column + block.shape[1]] = low
        return
    half = block.shape[0] // 2
    for at in range(0, block.shape[1], 128):
        owner, place = (column + at) // shard, (column + at) % shard
        keep_ref[owner, :, place : place + 128] = low[:half, at : at + 128]
        send_ref[owner, :, place : place + 128] = low[half:, at : at + 128]


def normalise(lat_ref, params):
    white = whiten(lat_ref[...], params)
    normed = white * params[2:3] + params[3:4]
    return white, normed, jax.nn.sigmoid(normed)


def pick_halo(near_ref, next_ref):
    core = lax.rem(lax.axis_index("wide"), 2)
    return jnp.where(core == 0, near_ref[...].astype(F32), next_ref[...].astype(F32))


def ready_body(sizes, lat_ref, cot_ref, near_ref, next_ref, wt_ref, *rest):
    D, W, frames, cells, cols, count, per_group, aligned = sizes
    pieces, rest = rest[: 2 * (D - 1)], rest[2 * (D - 1) :]
    lat_copy, cot_copy, left_t_ref, left_s_ref, gsa_seen, full_wt = rest[:6]
    gsa_pad, gsa_t, cot_t = rest[6:]
    channels = lat_ref.shape[1]
    core = lax.rem(lax.axis_index("wide"), 2)
    rows = frames * cells
    fill_weights(full_wt, wt_ref, pieces, D)
    lat_copy[...] = lat_ref[...]
    cot = cot_ref[...]
    cot_copy[...] = cot
    halo = pick_halo(near_ref, next_ref)
    extended = jnp.concatenate([cot, halo.astype(BF16)], axis=0)
    gsa = jnp.zeros((rows, channels), F32)
    for k in range(3):
        gsa += mm(
            extended[k * cells : k * cells + rows],
            full_wt[k * channels : (k + 1) * channels],
            NT,
        )
    gsa = gsa.astype(BF16).astype(F32)
    store_shifted(gsa_pad, gsa, frames, cells, cols)
    for dy in range(3):
        for dx in range(3):
            at = (3 * dy + dx) * channels
            gsa_seen[:, at : at + channels] = window(
                gsa_pad, 2 - dy, 2 - dx, frames, cells, cols
            )
    gsa_t[...] = gsa.T.astype(BF16)
    cot_t[:, :rows] = cot.astype(F32).T.astype(BF16)
    cot_t[:, rows : rows + 2 * cells] = halo[: 2 * cells].T.astype(BF16)
    left_s_ref[...] = core_order(gsa_t, W, core) if aligned else gsa_t[...]
    left_t_ref[...] = core_order(cot_t, W, core) if aligned else cot_t[...]


def first_body(sizes, lat_ref, stats_ref, left_s_ref, *rest):
    D, W, frames, cells, cols, count, per_group, aligned = sizes
    params_ref, seen_ref, keep_ref = rest[:3]
    send_ref = rest[3] if aligned else None
    act_pad = rest[-1]
    channels = lat_ref.shape[1]
    params = jnp.concatenate(
        [group_params(stats_ref[:, 0:2], count, per_group), stats_ref[0, 2:4]], axis=0
    )
    params_ref[...] = params
    _, normed, sig = normalise(lat_ref, params)
    act = (normed * sig).astype(BF16).astype(F32)
    store_shifted(act_pad, act, frames, cells, cols)
    left = left_s_ref[...]
    for dy in range(3):
        for dx in range(3):
            at = (3 * dy + dx) * channels
            seen = window(act_pad, dy, dx, frames, cells, cols)
            seen_ref[:, at : at + channels] = seen
            put(mm(left, seen), at, keep_ref.shape[-1], keep_ref, send_ref)


def second_body(
    sizes, lat_ref, left_t_ref, params_ref, gsa_seen_ref, seen_ref, ws_ref, *rest
):
    D, W, frames, cells, cols, count, per_group, aligned = sizes
    pieces, rest = rest[: 2 * (D - 1)], rest[2 * (D - 1) :]
    full_ws, side_ws = rest[-2:]
    spatial_ref, grad_ref, keep_ref, other_ref = rest[:4]
    send_ref = other_ref if aligned else None
    channels = lat_ref.shape[1]
    fill_weights(full_ws, ws_ref, pieces, D)
    rows = frames * cells
    left = left_t_ref[...]
    spatial = mm(seen_ref[...], full_ws[...]).astype(BF16)
    spatial_ref[...] = spatial
    shard = ws_ref.shape[0] // 3
    for k in range(3):
        block = mm(left[:, k * cells : k * cells + rows], spatial)
        put(block, k * channels, shard, keep_ref, send_ref)

    for tap in range(9):
        at = tap * channels
        side_ws[:, at : at + channels] = full_ws[at : at + channels]
    grad = mm(gsa_seen_ref[...], side_ws[...], NT)
    white, normed, sig = normalise(lat_ref, params_ref[...])
    grad = grad * (sig * (1.0 + normed * (1.0 - sig)))
    grad_ref[...] = grad
    gain_term = jnp.sum(grad * white, axis=0, keepdims=True)
    bias_term = jnp.sum(grad, axis=0, keepdims=True)
    if not aligned:
        both = jnp.concatenate([gain_term, bias_term], axis=0)
        other_ref[...] = jnp.broadcast_to(both[None], other_ref.shape)
        return
    d = lax.axis_index("dp")
    quarter = jnp.concatenate(
        [term[:, at : at + 128] for term in (gain_term, bias_term) for at in (0, 128)], axis=0
    )
    low = in_parts(
        jnp.concatenate([jnp.where(d == s, quarter, 0.0) for s in range(2)], axis=0)
    )
    for target in (keep_ref, send_ref):
        for owner in range(D):
            for at in range(0, channels // 2, 16):
                target[owner, at : at + 16, shard:] = low


def block_body(sizes, lat_ref, spatial_ref, before_ref, full_wt, block_ref):
    D, W, frames, cells, cols, count, per_group, aligned = sizes
    channels = lat_ref.shape[1]
    extended = jnp.concatenate([before_ref[...], spatial_ref[...]], axis=0)
    rows = frames * cells
    temporal = jnp.zeros((rows, channels), F32)
    for k in range(3):
        start = (2 - k) * cells
        temporal += mm(
            extended[start : start + rows], full_wt[k * channels : (k + 1) * channels]
        )
    block_ref[...] = (lat_ref[...].astype(F32) + temporal).astype(BF16)


def latent_gradient(sizes, total, lat_ref, cot_ref, params_ref, grad_ref):
    count, per_group = sizes[5:7]
    white, inv_std = whiten(lat_ref[...], params_ref[...]), params_ref[1:2]
    gain = params_ref[2:3]
    means = group_total(total * gain, per_group) / count
    inner = inv_std * (grad_ref[...] * gain - means[1:2] - white * means[0:1])
    return (cot_ref[...].astype(F32) + inner).astype(BF16)


def plane_body(keep_s, got_s, keep_t, got_t, *outs):
    d = lax.axis_index("dp")
    y = lax.rem(lax.axis_index("wide") // 2, 2)
    split = keep_s.shape[-1]
    ride = outs[0].shape[-1] - 128
    for a in range(2):
        for b in range(2):
            owner, side = lax.rem(d + a, 2), lax.rem(y + b, 2)
            out = outs[2 * a + b]
            for z in range(out.shape[0]):
                out[z, :, :split] = add([keep_s[owner, z, side], got_s[owner, z, side]]).astype(
                    BF16
                )
                both = [keep_t[owner, z, side], got_t[owner, z, side]]
                out[z, :, split:ride] = add([t[:, : ride - split] for t in both]).astype(BF16)
                out[z, :, ride:] = in_parts(from_parts([t[:, ride - split :] for t in both]))


def line_body(depth, *refs):
    terms, outs = refs[:4], refs[4:]
    z = lax.axis_index("wide") // 4
    ride = outs[0].shape[-1] - 128
    for s in range(depth):
        owner = lax.rem(z + s, depth)
        seen = [term[owner] for term in terms]
        outs[s][:, :ride] = add([t[:, :ride] for t in seen]).astype(BF16)
        outs[s][:, ride:] = in_parts(from_parts([t[:, ride:] for t in seen]))


def last_body(sizes, scale, depth, *refs):
    terms, operands, outs = refs[:depth], refs[depth:-4], refs[-4:]
    spatial_ref, temporal_ref, norm_ref, glat_ref = outs
    split = spatial_ref.shape[1]
    ride = terms[0].shape[1] - 128
    sums = from_parts([term[:, ride:] for term in terms])

    def rows_of(part):
        return jnp.concatenate(
            [jnp.concatenate([part[at : at + 1], part[at + 1 : at + 2]], axis=1) for at in (0, 2)],
            axis=0,
        )

    first, second = rows_of(sums[0:4]), rows_of(sums[4:8])
    own = jnp.where(lax.axis_index("dp") == 0, first, second)
    glat_ref[...] = latent_gradient(sizes, own, *operands)
    norm_columns(scale, first + second, norm_ref)
    total = add([term[:, :ride] for term in terms]) * scale
    spatial_ref[...] = total[:, :split]
    temporal_ref[...] = total[:, split:]


def apart_body(sizes, scale, sums_ref, *refs):
    norm_ref, glat_ref = refs[-2:]
    W = sizes[1]
    own = jnp.sum(sums_ref[pl.ds(lax.axis_index("dp") * W, W)], axis=0)
    norm_columns(scale, jnp.sum(sums_ref[...], axis=0), norm_ref)
    glat_ref[...] = latent_gradient(sizes, own, *refs[:-2])


def norm_columns(scale, norm, norm_ref):
    channels, width = norm.shape[1], norm_ref.shape[1]
    row = lax.broadcasted_iota(jnp.int32, (channels, width), 0)
    column = lax.broadcasted_iota(jnp.int32, (channels, width), 1)
    pick = (row == column + lax.axis_index("wide") * width).astype(F32)
    norm_ref[...] = (
        lax.dot_general(
            norm, pick, NN, precision=lax.Precision.HIGHEST, preferred_element_type=F32
        )
        * scale
    )


def local(latents, cotangent, norm_gain, norm_bias, w_spatial, w_temporal):
    D, W = lax.axis_size("dp"), lax.axis_size("wide")
    _, frames, rows_here, cols, channels = latents.shape
    cells = rows_here * cols
    rows = frames * cells
    per_group = channels // GROUPS
    count = W * frames * cells * per_group
    shard_s, shard_t = w_spatial.shape[0], w_temporal.shape[0]
    aligned = (channels // W) % 16 == 0 and shard_s % 128 == 0 and shard_t % 128 == 0
    aligned = aligned and W % 4 == 0 and D == 2 and channels == 256
    sizes = (D, W, frames, cells, cols, count, per_group, aligned)
    scale = 1.0 / math.sqrt(D * W * frames * cells)

    lat, cot = latents.reshape(rows, channels), cotangent.reshape(rows, channels)
    gain, bias = norm_gain.reshape(1, channels), norm_bias.reshape(1, channels)

    def over_all(moves):
        pairs = []
        for d in range(D):
            for w in range(W):
                to = moves(d, w)
                pairs.append((d * W + w, to[0] * W + to[1]))
        return pairs

    def send(value, moves):
        return lax.ppermute(value, ("dp", "wide"), over_all(moves))

    R = shard_s + shard_t
    stats, half_s, half_t = call(
        stats_body,
        [
            shape((W, 4, channels), F32),
            shape((shard_s // 2, channels), BF16),
            shape((shard_t // 2, channels), BF16),
        ],
        [
            pltpu.VMEM((rows, channels), BF16),
            pltpu.VMEM((1, channels), F32),
            pltpu.VMEM((1, channels), F32),
            pltpu.SemaphoreType.DMA((5,)),
        ],
        in_specs=[HBM] * 5,
        vmem=FIRST_VMEM,
    )(lat, gain, bias, w_spatial, w_temporal)
    firsts_t = [send(half_t, lambda d, w: ((d + s) % D, w)) for s in range(1, D)]
    half_s, firsts_t = lax.optimization_barrier((half_s, firsts_t))
    firsts_s = [send(half_s, lambda d, w: ((d + s) % D, w)) for s in range(1, D)]

    next_cot = lax.ppermute(cot, "wide", [(w + 1, w) for w in range(1, W - 1, 2)])
    near_cot = send(cot, lambda d, w: (d, w ^ 1))
    pieces_t, pieces_s = [], []
    for first in firsts_t:
        pieces_t += [first, send(first, lambda d, w: (d, w ^ 1))]
    stats, pieces_t, near_cot, cot = lax.optimization_barrier(
        (stats, pieces_t, near_cot, cot)
    )
    stats = lax.all_to_all(stats, "wide", split_axis=0, concat_axis=0, tiled=True)
    taps = D * shard_s
    pad = pltpu.VMEM((3, frames, cells + 2 * cols, channels), BF16)
    ready = call(
        functools.partial(ready_body, sizes),
        [
            shape((rows, channels), BF16),
            shape((rows, channels), BF16),
            shape((channels, rows + 2 * cells), BF16),
            shape((channels, rows), BF16),
            shape((rows, taps), BF16),
            shape((D * shard_t, channels), BF16),
        ],
        [
            pad,
            pltpu.VMEM((channels, rows), BF16),
            pltpu.VMEM((channels, rows + 2 * cells), BF16),
        ],
        flops=2 * 3 * rows * channels * channels,
        moved=2_000_000,
    )(lat, cot, near_cot, next_cot, w_temporal, *pieces_t)
    firsts_s, stats, ready = lax.optimization_barrier((firsts_s, stats, ready))
    lat, cot, left_t, left_s, gsa_seen, full_wt = ready
    for first in firsts_s:
        pieces_s += [first, send(first, lambda d, w: (d, w ^ 1))]

    ride = 128 if aligned else 0
    if aligned:
        terms_s = [shape((D, channels // 2, shard_s), BF16)] * 2
        terms_t = [shape((D, channels // 2, shard_t + ride), BF16)] * 2
    else:
        terms_s = [shape((channels, D * shard_s), BF16)]
        terms_t = [shape((channels, D * shard_t), BF16), shape((D * W, 2, channels), F32)]
    params, seen, *grads_s = call(
        functools.partial(first_body, sizes),
        [shape((4, channels), F32), shape((rows, taps), BF16)] + terms_s,
        [pad],
        flops=2 * 9 * rows * channels * channels,
        moved=3_000_000,
    )(lat, stats, left_s)
    spatial, grad, *grads_t = call(
        functools.partial(second_body, sizes),
        [shape((rows, channels), BF16), shape((rows, channels), F32)] + terms_t,
        [pltpu.VMEM((taps, channels), BF16), pltpu.VMEM((channels, taps), BF16)],
        flops=2 * 21 * rows * channels * channels,
        moved=3_000_000,
    )(lat, left_t, params, gsa_seen, seen, w_spatial, *pieces_s)
    before = lax.ppermute(spatial, "wide", [(w, w + 1) for w in range(W - 1)])
    block_out = call(
        functools.partial(block_body, sizes),
        shape((rows, channels), BF16),
        flops=2 * 3 * rows * channels * channels,
        moved=1_000_000,
    )(lat, spatial, before, full_wt)

    width = channels // W

    operands = (lat, cot, params, grad)
    if aligned:
        Z = W // 4

        def over_core(away):
            return send(away, lambda d, w: (d, w ^ 1))

        pairs = []
        for keep, away in (grads_s, grads_t):
            view = (D, Z, 2, width, keep.shape[-1])
            pairs += [keep.reshape(view), over_core(away).reshape(view)]
        plane = call(
            plane_body, [shape((Z, width, R + ride), BF16)] * (2 * D), moved=3_000_000
        )(*pairs)
        seen = [plane[0]] + [
            send(plane[2 * a + b], lambda d, w: ((d + a) % D, w ^ (2 * b)))
            for a, b in ((0, 1), (1, 0), (1, 1))
        ]
        line = call(
            functools.partial(line_body, Z),
            [shape((width, R + ride), BF16)] * Z,
            moved=1_000_000,
        )(*seen)
        terms = [line[0]]
        for s in range(1, Z):
            terms.append(send(line[s], lambda d, w: (d, (w + 4 * s) % W)))
        grad_s, grad_t, norm, grad_latents = call(
            functools.partial(last_body, sizes, scale, Z),
            [
                shape((width, shard_s), F32),
                shape((width, shard_t), F32),
                shape((2, width), F32),
                shape((rows, channels), BF16),
            ],
            moved=1_000_000,
        )(*terms, *operands)
        grad_s, grad_t = grad_s.T, grad_t.T
    else:
        sums = lax.all_to_all(
            grads_t[1], ("dp", "wide"), split_axis=0, concat_axis=0, tiled=True
        )
        norm, grad_latents = call(
            functools.partial(apart_body, sizes, scale),
            [shape((2, width), F32), shape((rows, channels), BF16)],
        )(sums, *operands)
        outs = []
        for full in (grads_s[0], grads_t[0]):
            part = lax.psum_scatter(
                full.astype(F32), "wide", scatter_dimension=0, tiled=True
            ).T.astype(BF16)
            part = lax.psum_scatter(part, "dp", scatter_dimension=0, tiled=True)
            outs.append(part.astype(F32) * scale)
        grad_s, grad_t = outs
    return (
        block_out.reshape(latents.shape),
        grad_latents.reshape(latents.shape),
        grad_s,
        grad_t,
        norm,
    )


def solution(mesh):
    return jax.shard_map(
        local,
        mesh=mesh,
        in_specs=(
            P("dp", "wide", None, None, None),
            P("dp", "wide", None, None, None),
            P(),
            P(),
            P("dp", None),
            P("dp", None),
        ),
        out_specs=(
            P("dp", "wide", None, None, None),
            P("dp", "wide", None, None, None),
            P("dp", "wide"),
            P("dp", "wide"),
            P(None, "wide"),
        ),
        check_vma=False,
    )
```

```python
import functools
import math

import jax
import jax.numpy as jnp
from jax import lax
from jax.experimental import pallas as pl
from jax.experimental.pallas import tpu as pltpu
from jax.sharding import PartitionSpec as P

GROUPS = 32
EPSILON = 1e-05
F32 = jnp.float32
BF16 = jnp.bfloat16
VMEM = pl.BlockSpec(memory_space=pltpu.VMEM)
HBM = pl.BlockSpec(memory_space=pltpu.HBM)
FIRST_VMEM = 60 << 20
NT = (((1,), (1,)), ((), ()))
NN = (((1,), (0,)), ((), ()))


def call(body, out_shapes, scratch=(), flops=0, moved=0, in_specs=None, vmem=40 << 20):
    many = isinstance(out_shapes, (tuple, list))

    def run(*operands):
        return pl.pallas_call(
            body,
            out_shape=out_shapes,
            in_specs=in_specs or [VMEM] * len(operands),
            out_specs=[VMEM] * len(out_shapes) if many else VMEM,
            scratch_shapes=list(scratch),
            compiler_params=pltpu.CompilerParams(vmem_limit_bytes=vmem),
            cost_estimate=pl.CostEstimate(
                flops=flops, bytes_accessed=moved, transcendentals=0
            ),
        )(*operands)

    return run


def shape(dims, kind):
    return jax.ShapeDtypeStruct(dims, kind)


def mm(left, right, dims=NN):
    return lax.dot_general(left, right, dims, preferred_element_type=F32)


def group_total(rows, per_group):
    channels = rows.shape[-1]
    first = lax.broadcasted_iota(jnp.int32, (channels, channels), 0) // per_group
    second = lax.broadcasted_iota(jnp.int32, (channels, channels), 1) // per_group
    same = (first == second).astype(F32)
    return lax.dot_general(
        rows, same, NN, precision=lax.Precision.HIGHEST, preferred_element_type=F32
    )


def stats_body(lat_ref, gain_ref, bias_ref, ws_ref, wt_ref, out_ref, affine_ref, half_ref, *scratch):
    lat_here, gain_here, bias_here, sems = scratch
    core = lax.rem(lax.axis_index("wide"), 2)
    moves, place = [(lat_ref, lat_here), (gain_ref, gain_here), (bias_ref, bias_here)], 0
    for source in (ws_ref, wt_ref):
        half = source.shape[0] // 2
        start = pl.multiple_of(core * half, 16)
        moves.append((source.at[pl.ds(start, half)], half_ref.at[pl.ds(place, half)]))
        place += half
    copies = [pltpu.make_async_copy(*move, sems.at[at]) for at, move in enumerate(moves)]
    for copy in copies:
        copy.start()
    for copy in copies[:3]:
        copy.wait()
    affine_ref[0:1] = gain_here[...]
    affine_ref[1:2] = bias_here[...]
    x = lat_here[...].astype(F32)
    both = jnp.concatenate(
        [jnp.sum(x, axis=0, keepdims=True), jnp.sum(x * x, axis=0, keepdims=True)], axis=0
    )
    out_ref[...] = both
    for copy in copies[3:]:
        copy.wait()


def add_body(left_ref, right_ref, out_ref):
    out_ref[...] = left_ref[...] + right_ref[...]


def transpose_body(cot_ref, out_ref):
    out_ref[...] = cot_ref[...].astype(F32).T.astype(BF16)


def fill_weights(full, shard_ref, pieces, offset, D):
    d = lax.axis_index("dp")
    core = lax.rem(lax.axis_index("wide"), 2)
    n = shard_ref.shape[0]
    half = n // 2
    full[pl.ds(pl.multiple_of(d * n, 16), n)] = shard_ref[...]
    for s in range(1, D):
        source = lax.rem(d + D - s, D)
        for which in range(2):
            holder = core if which == 0 else 1 - core
            start = pl.multiple_of(source * n + holder * half, 16)
            full[pl.ds(start, half)] = pieces[2 * (s - 1) + which][offset : offset + half]


def whiten(lat, stats, count, per_group):
    total = group_total(stats, per_group) / count
    mean = total[0:1]
    inv_std = 1.0 / jnp.sqrt(total[1:2] - mean * mean + EPSILON)
    return (lat.astype(F32) - mean) * inv_std, inv_std


def store_shifted(pad_ref, values, frames, cells, cols):
    total = frames * cells
    column = lax.broadcasted_iota(jnp.int32, (total, 1), 0) % cols
    left = jnp.where(column == 0, 0.0, pltpu.roll(values, 1, 0))
    right = jnp.where(column == cols - 1, 0.0, pltpu.roll(values, total - 1, 0))
    edge = jnp.zeros((cols, values.shape[1]), BF16)
    for at, form in enumerate((left, values, right)):
        low = form.astype(BF16)
        for f in range(frames):
            pad_ref[at, f, 0:cols] = edge
            pad_ref[at, f, cols : cols + cells] = low[f * cells : (f + 1) * cells]
            pad_ref[at, f, cols + cells :] = edge


def window(pad_ref, dy, dx, frames, cells, cols):
    return jnp.concatenate(
        [pad_ref[dx, f, dy * cols : dy * cols + cells] for f in range(frames)], axis=0
    )


def in_parts(total):
    high = total.astype(BF16).astype(F32)
    return jnp.concatenate([high, total - high], axis=0).astype(BF16)


def from_parts(terms):
    total = 0.0
    for term in terms:
        wide = term.astype(F32)
        total = total + (wide[0:8] + wide[8:16])
    return total


def add(terms):
    total = terms[0].astype(F32)
    for term in terms[1:]:
        total += term.astype(F32)
    return total


def core_order(transposed_ref, W, core):
    step = transposed_ref.shape[0] // W
    order = [(2 * j + core) * step for j in range(W // 2)]
    order += [(2 * j + 1 - core) * step for j in range(W // 2)]
    return jnp.concatenate(
        [transposed_ref[pl.ds(pl.multiple_of(at, 16), step)] for at in order], axis=0
    )


def put(block, column, shard, keep_ref, send_ref):
    low = block.astype(BF16)
    if send_ref is None:
        keep_ref[:, column : column + block.shape[1]] = low
        return
    half = block.shape[0] // 2
    for at in range(0, block.shape[1], 128):
        owner, place = (column + at) // shard, (column + at) % shard
        keep_ref[owner, :, place : place + 128] = low[:half, at : at + 128]
        send_ref[owner, :, place : place + 128] = low[half:, at : at + 128]


def normalise(lat_ref, stats, affine_ref, count, per_group):
    white, inv_std = whiten(lat_ref[...], stats, count, per_group)
    normed = white * affine_ref[0:1] + affine_ref[1:2]
    return white, normed, jax.nn.sigmoid(normed)


def first_body(sizes, lat_ref, cot_ref, halo_ref, affine_ref, wt_ref, *rest):
    D, W, frames, cells, cols, count, per_group, aligned = sizes
    pieces, rest = rest[: 2 * (D - 1)], rest[2 * (D - 1) :]
    full_wt, act_pad, gsa_t = rest[-3:]
    outs = rest[-7:-3] if aligned else rest[-6:-3]
    stats = add([ref[...] for ref in rest[: -3 - len(outs)]])
    gsa_ref, total_ref, keep_ref = outs[:3]
    send_ref = outs[3] if aligned else None
    total_ref[...] = stats
    channels = lat_ref.shape[1]
    core = lax.rem(lax.axis_index("wide"), 2)
    fill_weights(full_wt, wt_ref, pieces, pieces[0].shape[0] - wt_ref.shape[0] // 2, D)
    rows = frames * cells
    extended = jnp.concatenate([cot_ref[...], halo_ref[...]], axis=0)
    gsa = jnp.zeros((rows, channels), F32)
    for k in range(3):
        gsa += mm(
            extended[k * cells : k * cells + rows],
            full_wt[k * channels : (k + 1) * channels],
            NT,
        )
    gsa_ref[...] = gsa.astype(BF16)
    gsa_t[...] = gsa.astype(BF16).astype(F32).T.astype(BF16)
    _, normed, sig = normalise(lat_ref, stats, affine_ref, count, per_group)
    act = (normed * sig).astype(BF16).astype(F32)
    store_shifted(act_pad, act, frames, cells, cols)
    left = core_order(gsa_t, W, core) if aligned else gsa_t[...]
    shard = wt_ref.shape[0] * 3
    for dy in range(3):
        for dx in range(3):
            seen = window(act_pad, dy, dx, frames, cells, cols)
            put(mm(left, seen), (3 * dy + dx) * channels, shard, keep_ref, send_ref)


def second_body(
    sizes, lat_ref, cot_t_ref, halo_ref, stats_ref, affine_ref, gsa_ref, ws_ref, *rest
):
    D, W, frames, cells, cols, count, per_group, aligned = sizes
    pieces, rest = rest[: 2 * (D - 1)], rest[2 * (D - 1) :]
    full_ws, act_pad, gsa_pad, cot_t = rest[-4:]
    spatial_ref, grad_ref, keep_ref, other_ref = rest[:4]
    send_ref = other_ref if aligned else None
    channels = lat_ref.shape[1]
    core = lax.rem(lax.axis_index("wide"), 2)
    fill_weights(full_ws, ws_ref, pieces, 0, D)
    rows = frames * cells
    white, normed, sig = normalise(lat_ref, stats_ref[...], affine_ref, count, per_group)
    act = (normed * sig).astype(BF16).astype(F32)
    store_shifted(act_pad, act, frames, cells, cols)
    store_shifted(gsa_pad, gsa_ref[...].astype(F32), frames, cells, cols)
    cot_t[:, :rows] = cot_t_ref[...]
    for f in range(2):
        cot_t[:, rows + f * cells : rows + (f + 1) * cells] = (
            halo_ref[f * cells : (f + 1) * cells].astype(F32).T.astype(BF16)
        )
    left = core_order(cot_t, W, core) if aligned else cot_t[...]
    out = jnp.zeros((rows, channels), F32)
    for dy in range(3):
        for dx in range(3):
            tap = 3 * dy + dx
            seen = window(act_pad, dy, dx, frames, cells, cols)
            out += mm(seen, full_ws[tap * channels : (tap + 1) * channels])
    spatial = out.astype(BF16)
    spatial_ref[...] = spatial
    shard = ws_ref.shape[0] // 3
    for k in range(3):
        block = mm(left[:, k * cells : k * cells + rows], spatial)
        put(block, k * channels, shard, keep_ref, send_ref)

    grad = jnp.zeros((rows, channels), F32)
    for dy in range(3):
        for dx in range(3):
            tap = 3 * dy + dx
            seen = window(gsa_pad, 2 - dy, 2 - dx, frames, cells, cols)
            grad += mm(seen, full_ws[tap * channels : (tap + 1) * channels], NT)
    grad = grad * (sig * (1.0 + normed * (1.0 - sig)))
    grad_ref[...] = grad
    gain_term = jnp.sum(grad * white, axis=0, keepdims=True)
    bias_term = jnp.sum(grad, axis=0, keepdims=True)
    if not aligned:
        both = jnp.concatenate([gain_term, bias_term], axis=0)
        other_ref[...] = jnp.broadcast_to(both[None], other_ref.shape)
        return
    d = lax.axis_index("dp")
    quarter = jnp.concatenate(
        [term[:, at : at + 128] for term in (gain_term, bias_term) for at in (0, 128)], axis=0
    )
    low = in_parts(
        jnp.concatenate([jnp.where(d == s, quarter, 0.0) for s in range(2)], axis=0)
    )
    for target in (keep_ref, send_ref):
        for owner in range(D):
            for at in range(0, channels // 2, 16):
                target[owner, at : at + 16, shard:] = low


def block_body(sizes, lat_ref, spatial_ref, before_ref, wt_ref, *rest):
    D, W, frames, cells, cols, count, per_group, aligned = sizes
    pieces = rest[: 2 * (D - 1)]
    block_ref, full_wt = rest[2 * (D - 1) :]
    channels = lat_ref.shape[1]
    fill_weights(full_wt, wt_ref, pieces, pieces[0].shape[0] - wt_ref.shape[0] // 2, D)
    extended = jnp.concatenate([before_ref[...], spatial_ref[...]], axis=0)
    rows = frames * cells
    temporal = jnp.zeros((rows, channels), F32)
    for k in range(3):
        start = (2 - k) * cells
        temporal += mm(
            extended[start : start + rows], full_wt[k * channels : (k + 1) * channels]
        )
    block_ref[...] = (lat_ref[...].astype(F32) + temporal).astype(BF16)


def latent_gradient(sizes, total, lat_ref, cot_ref, stats_ref, affine_ref, grad_ref):
    D, W, frames, cells, cols, count, per_group, aligned = sizes
    white, inv_std = whiten(lat_ref[...], stats_ref[...], count, per_group)
    gain = affine_ref[0:1]
    means = group_total(total * gain, per_group) / count
    inner = inv_std * (grad_ref[...] * gain - means[1:2] - white * means[0:1])
    return (cot_ref[...].astype(F32) + inner).astype(BF16)


def plane_body(keep_s, got_s, keep_t, got_t, *outs):
    d = lax.axis_index("dp")
    y = lax.rem(lax.axis_index("wide") // 2, 2)
    split = keep_s.shape[-1]
    ride = outs[0].shape[-1] - 128
    for a in range(2):
        for b in range(2):
            owner, side = lax.rem(d + a, 2), lax.rem(y + b, 2)
            out = outs[2 * a + b]
            for z in range(out.shape[0]):
                out[z, :, :split] = add([keep_s[owner, z, side], got_s[owner, z, side]]).astype(
                    BF16
                )
                both = [keep_t[owner, z, side], got_t[owner, z, side]]
                out[z, :, split:ride] = add([t[:, : ride - split] for t in both]).astype(BF16)
                out[z, :, ride:] = in_parts(from_parts([t[:, ride - split :] for t in both]))


def line_body(depth, *refs):
    terms, outs = refs[:4], refs[4:]
    z = lax.axis_index("wide") // 4
    ride = outs[0].shape[-1] - 128
    for s in range(depth):
        owner = lax.rem(z + s, depth)
        seen = [term[owner] for term in terms]
        outs[s][:, :ride] = add([t[:, :ride] for t in seen]).astype(BF16)
        outs[s][:, ride:] = in_parts(from_parts([t[:, ride:] for t in seen]))


def last_body(sizes, scale, depth, *refs):
    terms, operands, outs = refs[:depth], refs[depth:-4], refs[-4:]
    spatial_ref, temporal_ref, norm_ref, glat_ref = outs
    split = spatial_ref.shape[1]
    ride = terms[0].shape[1] - 128
    sums = from_parts([term[:, ride:] for term in terms])

    def rows_of(part):
        return jnp.concatenate(
            [jnp.concatenate([part[at : at + 1], part[at + 1 : at + 2]], axis=1) for at in (0, 2)],
            axis=0,
        )

    first, second = rows_of(sums[0:4]), rows_of(sums[4:8])
    own = jnp.where(lax.axis_index("dp") == 0, first, second)
    glat_ref[...] = latent_gradient(sizes, own, *operands)
    norm_columns(scale, first + second, norm_ref)
    total = add([term[:, :ride] for term in terms]) * scale
    spatial_ref[...] = total[:, :split]
    temporal_ref[...] = total[:, split:]


def apart_body(sizes, scale, sums_ref, *refs):
    norm_ref, glat_ref = refs[-2:]
    W = sizes[1]
    own = jnp.sum(sums_ref[pl.ds(lax.axis_index("dp") * W, W)], axis=0)
    norm_columns(scale, jnp.sum(sums_ref[...], axis=0), norm_ref)
    glat_ref[...] = latent_gradient(sizes, own, *refs[:-2])


def norm_columns(scale, norm, norm_ref):
    channels, width = norm.shape[1], norm_ref.shape[1]
    row = lax.broadcasted_iota(jnp.int32, (channels, width), 0)
    column = lax.broadcasted_iota(jnp.int32, (channels, width), 1)
    pick = (row == column + lax.axis_index("wide") * width).astype(F32)
    norm_ref[...] = (
        lax.dot_general(
            norm, pick, NN, precision=lax.Precision.HIGHEST, preferred_element_type=F32
        )
        * scale
    )


def local(latents, cotangent, norm_gain, norm_bias, w_spatial, w_temporal):
    D, W = lax.axis_size("dp"), lax.axis_size("wide")
    _, frames, rows_here, cols, channels = latents.shape
    cells = rows_here * cols
    rows = frames * cells
    per_group = channels // GROUPS
    count = W * frames * cells * per_group
    shard_s, shard_t = w_spatial.shape[0], w_temporal.shape[0]
    aligned = (channels // W) % 16 == 0 and shard_s % 128 == 0 and shard_t % 128 == 0
    aligned = aligned and W % 4 == 0 and D == 2 and channels == 256
    sizes = (D, W, frames, cells, cols, count, per_group, aligned)
    scale = 1.0 / math.sqrt(D * W * frames * cells)

    lat, cot = latents.reshape(rows, channels), cotangent.reshape(rows, channels)
    gain, bias = norm_gain.reshape(1, channels), norm_bias.reshape(1, channels)

    def over_all(moves):
        pairs = []
        for d in range(D):
            for w in range(W):
                to = moves(d, w)
                pairs.append((d * W + w, to[0] * W + to[1]))
        return pairs

    def send(value, moves):
        return lax.ppermute(value, ("dp", "wide"), over_all(moves))

    R = shard_s + shard_t
    stats, affine, half = call(
        stats_body,
        [
            shape((2, channels), F32),
            shape((2, channels), F32),
            shape((R // 2, channels), BF16),
        ],
        [
            pltpu.VMEM((rows, channels), BF16),
            pltpu.VMEM((1, channels), F32),
            pltpu.VMEM((1, channels), F32),
            pltpu.SemaphoreType.DMA((5,)),
        ],
        in_specs=[HBM] * 5,
        vmem=FIRST_VMEM,
    )(lat, gain, bias, w_spatial, w_temporal)
    cot_t = call(transpose_body, shape((channels, rows), BF16), moved=300_000)(cot)
    firsts = [send(half, lambda d, w: ((d + s) % D, w)) for s in range(1, D)]

    halo = lax.ppermute(cot, "wide", [(w + 1, w) for w in range(W - 1)])
    steps = [1, 2] if W % 4 == 0 else [1]
    for step in steps:
        other = send(stats, lambda d, w: (d, w ^ step))
        stats = call(add_body, shape((2, channels), F32))(stats, other)
    block = 2 * steps[-1]
    stats = [stats] + [
        send(stats, lambda d, w: (d, (w + block * s) % W)) for s in range(1, W // block)
    ]
    firsts, stats, halo, cot_t = lax.optimization_barrier((firsts, stats, halo, cot_t))
    pieces = []
    for first in firsts:
        pieces += [first, send(first, lambda d, w: (d, w ^ 1))]

    ride = 128 if aligned else 0
    if aligned:
        terms_s = [shape((D, channels // 2, shard_s), BF16)] * 2
        terms_t = [shape((D, channels // 2, shard_t + ride), BF16)] * 2
    else:
        terms_s = [shape((channels, D * shard_s), BF16)]
        terms_t = [shape((channels, D * shard_t), BF16), shape((D * W, 2, channels), F32)]
    pad = pltpu.VMEM((3, frames, cells + 2 * cols, channels), BF16)
    gsa, stats, *grads_s = call(
        functools.partial(first_body, sizes),
        [shape((rows, channels), BF16), shape((2, channels), F32)] + terms_s,
        [pltpu.VMEM((D * shard_t, channels), BF16), pad, pltpu.VMEM((channels, rows), BF16)],
        flops=2 * 12 * rows * channels * channels,
        moved=3_000_000,
    )(lat, cot, halo, affine, w_temporal, *pieces, *stats)
    spatial, grad, *grads_t = call(
        functools.partial(second_body, sizes),
        [shape((rows, channels), BF16), shape((rows, channels), F32)] + terms_t,
        [
            pltpu.VMEM((D * shard_s, channels), BF16),
            pad,
            pad,
            pltpu.VMEM((channels, rows + 2 * cells), BF16),
        ],
        flops=2 * 21 * rows * channels * channels,
        moved=3_000_000,
    )(lat, cot_t, halo, stats, affine, gsa, w_spatial, *pieces)
    before = lax.ppermute(spatial, "wide", [(w, w + 1) for w in range(W - 1)])
    block_out = call(
        functools.partial(block_body, sizes),
        shape((rows, channels), BF16),
        [pltpu.VMEM((D * shard_t, channels), BF16)],
        flops=2 * 3 * rows * channels * channels,
        moved=1_000_000,
    )(lat, spatial, before, w_temporal, *pieces)

    width = channels // W
    operands = (lat, cot, stats, affine, grad)
    if aligned:
        Z = W // 4

        def over_core(away):
            return send(away, lambda d, w: (d, w ^ 1))

        pairs = []
        for keep, away in (grads_s, grads_t):
            view = (D, Z, 2, width, keep.shape[-1])
            pairs += [keep.reshape(view), over_core(away).reshape(view)]
        plane = call(
            plane_body, [shape((Z, width, R + ride), BF16)] * (2 * D), moved=3_000_000
        )(*pairs)
        seen = [plane[0]] + [
            send(plane[2 * a + b], lambda d, w: ((d + a) % D, w ^ (2 * b)))
            for a, b in ((0, 1), (1, 0), (1, 1))
        ]
        line = call(
            functools.partial(line_body, Z),
            [shape((width, R + ride), BF16)] * Z,
            moved=1_000_000,
        )(*seen)
        terms = [line[0]]
        for s in range(1, Z):
            terms.append(send(line[s], lambda d, w: (d, (w + 4 * s) % W)))
        grad_s, grad_t, norm, grad_latents = call(
            functools.partial(last_body, sizes, scale, Z),
            [
                shape((width, shard_s), F32),
                shape((width, shard_t), F32),
                shape((2, width), F32),
                shape((rows, channels), BF16),
            ],
            moved=1_000_000,
        )(*terms, *operands)
        grad_s, grad_t = grad_s.T, grad_t.T
    else:
        sums = lax.all_to_all(
            grads_t[1], ("dp", "wide"), split_axis=0, concat_axis=0, tiled=True
        )
        norm, grad_latents = call(
            functools.partial(apart_body, sizes, scale),
            [shape((2, width), F32), shape((rows, channels), BF16)],
        )(sums, *operands)
        outs = []
        for full in (grads_s[0], grads_t[0]):
            part = lax.psum_scatter(
                full.astype(F32), "wide", scatter_dimension=0, tiled=True
            ).T.astype(BF16)
            part = lax.psum_scatter(part, "dp", scatter_dimension=0, tiled=True)
            outs.append(part.astype(F32) * scale)
        grad_s, grad_t = outs
    return (
        block_out.reshape(latents.shape),
        grad_latents.reshape(latents.shape),
        grad_s,
        grad_t,
        norm,
    )


def solution(mesh):
    return jax.shard_map(
        local,
        mesh=mesh,
        in_specs=(
            P("dp", "wide", None, None, None),
            P("dp", "wide", None, None, None),
            P(),
            P(),
            P("dp", None),
            P("dp", None),
        ),
        out_specs=(
            P("dp", "wide", None, None, None),
            P("dp", "wide", None, None, None),
            P("dp", "wide"),
            P("dp", "wide"),
            P(None, "wide"),
        ),
        check_vma=False,
    )
```

```python
import functools
import math

import jax
import jax.numpy as jnp
from jax import lax
from jax.experimental import pallas as pl
from jax.experimental.pallas import tpu as pltpu
from jax.sharding import PartitionSpec as P

GROUPS = 32
EPSILON = 1e-05
F32 = jnp.float32
BF16 = jnp.bfloat16
VMEM = pl.BlockSpec(memory_space=pltpu.VMEM)
HBM = pl.BlockSpec(memory_space=pltpu.HBM)
FIRST_VMEM = 60 << 20
NT = (((1,), (1,)), ((), ()))
NN = (((1,), (0,)), ((), ()))


def call(body, out_shapes, scratch=(), flops=0, moved=0, in_specs=None, vmem=40 << 20):
    many = isinstance(out_shapes, (tuple, list))

    def run(*operands):
        return pl.pallas_call(
            body,
            out_shape=out_shapes,
            in_specs=in_specs or [VMEM] * len(operands),
            out_specs=[VMEM] * len(out_shapes) if many else VMEM,
            scratch_shapes=list(scratch),
            compiler_params=pltpu.CompilerParams(vmem_limit_bytes=vmem),
            cost_estimate=pl.CostEstimate(
                flops=flops, bytes_accessed=moved, transcendentals=0
            ),
        )(*operands)

    return run


def shape(dims, kind):
    return jax.ShapeDtypeStruct(dims, kind)


def mm(left, right, dims=NN):
    return lax.dot_general(left, right, dims, preferred_element_type=F32)


def group_total(rows, per_group):
    channels = rows.shape[-1]
    first = lax.broadcasted_iota(jnp.int32, (channels, channels), 0) // per_group
    second = lax.broadcasted_iota(jnp.int32, (channels, channels), 1) // per_group
    same = (first == second).astype(F32)
    return lax.dot_general(
        rows, same, NN, precision=lax.Precision.HIGHEST, preferred_element_type=F32
    )


def stats_body(lat_ref, gain_ref, bias_ref, ws_ref, wt_ref, out_ref, half_ref, *scratch):
    lat_here, gain_here, bias_here, sems = scratch
    core = lax.rem(lax.axis_index("wide"), 2)
    moves = [(lat_ref, lat_here), (gain_ref, gain_here), (bias_ref, bias_here)]
    half = ws_ref.shape[0] // 2
    start = pl.multiple_of(core * half, 16)
    moves.append((ws_ref.at[pl.ds(start, half)], half_ref.at[pl.ds(0, half)]))
    moves.append((wt_ref, half_ref.at[pl.ds(half, wt_ref.shape[0])]))
    copies = [pltpu.make_async_copy(*move, sems.at[at]) for at, move in enumerate(moves)]
    for copy in copies:
        copy.start()
    for copy in copies[:3]:
        copy.wait()
    x = lat_here[...].astype(F32)
    sums = [jnp.sum(x, axis=0, keepdims=True), jnp.sum(x * x, axis=0, keepdims=True)]
    both = jnp.concatenate(
        [
            jnp.concatenate([sums[0], gain_here[...]], axis=1),
            jnp.concatenate([sums[1], bias_here[...]], axis=1),
        ],
        axis=0,
    )
    out_ref[...] = jnp.broadcast_to(both[None], out_ref.shape)
    for copy in copies[3:]:
        copy.wait()


def transpose_body(cot_ref, out_ref):
    out_ref[...] = cot_ref[...].astype(F32).T.astype(BF16)


def fill_spatial(full, shard_ref, pieces, D):
    d = lax.axis_index("dp")
    core = lax.rem(lax.axis_index("wide"), 2)
    n = shard_ref.shape[0]
    half = n // 2
    full[pl.ds(pl.multiple_of(d * n, 16), n)] = shard_ref[...]
    for s in range(1, D):
        source = lax.rem(d + D - s, D)
        for which in range(2):
            holder = core if which == 0 else 1 - core
            start = pl.multiple_of(source * n + holder * half, 16)
            full[pl.ds(start, half)] = pieces[2 * (s - 1) + which][0:half]


def fill_temporal(full, shard_ref, firsts, D):
    d = lax.axis_index("dp")
    n = shard_ref.shape[0]
    full[pl.ds(pl.multiple_of(d * n, 16), n)] = shard_ref[...]
    for s in range(1, D):
        start = pl.multiple_of(lax.rem(d + D - s, D) * n, 16)
        full[pl.ds(start, n)] = firsts[s - 1][firsts[s - 1].shape[0] - n :]


def whiten(lat, stats, count, per_group):
    total = group_total(jnp.sum(stats[:, :, : lat.shape[1]], axis=0), per_group) / count
    mean = total[0:1]
    inv_std = 1.0 / jnp.sqrt(total[1:2] - mean * mean + EPSILON)
    return (lat.astype(F32) - mean) * inv_std, inv_std


def store_shifted(pad_ref, values, frames, cells, cols):
    total = frames * cells
    column = lax.broadcasted_iota(jnp.int32, (total, 1), 0) % cols
    left = jnp.where(column == 0, 0.0, pltpu.roll(values, 1, 0))
    right = jnp.where(column == cols - 1, 0.0, pltpu.roll(values, total - 1, 0))
    edge = jnp.zeros((cols, values.shape[1]), BF16)
    for at, form in enumerate((left, values, right)):
        low = form.astype(BF16)
        for f in range(frames):
            pad_ref[at, f, 0:cols] = edge
            pad_ref[at, f, cols : cols + cells] = low[f * cells : (f + 1) * cells]
            pad_ref[at, f, cols + cells :] = edge


def window(pad_ref, dy, dx, frames, cells, cols):
    return jnp.concatenate(
        [pad_ref[dx, f, dy * cols : dy * cols + cells] for f in range(frames)], axis=0
    )


def in_parts(total):
    high = total.astype(BF16).astype(F32)
    return jnp.concatenate([high, total - high], axis=0).astype(BF16)


def from_parts(terms):
    total = 0.0
    for term in terms:
        wide = term.astype(F32)
        total = total + (wide[0:8] + wide[8:16])
    return total


def add(terms):
    total = terms[0].astype(F32)
    for term in terms[1:]:
        total += term.astype(F32)
    return total


def core_order(transposed_ref, W, core):
    step = transposed_ref.shape[0] // W
    order = [(2 * j + core) * step for j in range(W // 2)]
    order += [(2 * j + 1 - core) * step for j in range(W // 2)]
    return jnp.concatenate(
        [transposed_ref[pl.ds(pl.multiple_of(at, 16), step)] for at in order], axis=0
    )


def put(block, column, shard, keep_ref, send_ref):
    low = block.astype(BF16)
    if send_ref is None:
        keep_ref[:, column : column + block.shape[1]] = low
        return
    half = block.shape[0] // 2
    for at in range(0, block.shape[1], 128):
        owner, place = (column + at) // shard, (column + at) % shard
        keep_ref[owner, :, place : place + 128] = low[:half, at : at + 128]
        send_ref[owner, :, place : place + 128] = low[half:, at : at + 128]


def affine_of(stats_ref):
    return stats_ref[0, :, stats_ref.shape[2] // 2 :]


def normalise(lat_ref, stats_ref, count, per_group):
    white, inv_std = whiten(lat_ref[...], stats_ref[...], count, per_group)
    affine = affine_of(stats_ref)
    normed = white * affine[0:1] + affine[1:2]
    return white, normed, jax.nn.sigmoid(normed)


def first_body(sizes, lat_ref, cot_ref, halo_ref, stats_ref, wt_ref, *rest):
    D, W, frames, cells, cols, count, per_group, aligned = sizes
    firsts, rest = rest[: D - 1], rest[D - 1 :]
    full_wt, act_pad, gsa_t = rest[-3:]
    gsa_ref, seen_ref, keep_ref = rest[:3]
    send_ref = rest[3] if aligned else None
    channels = lat_ref.shape[1]
    core = lax.rem(lax.axis_index("wide"), 2)
    fill_temporal(full_wt, wt_ref, firsts, D)
    rows = frames * cells
    extended = jnp.concatenate([cot_ref[...], halo_ref[...]], axis=0)
    gsa = jnp.zeros((rows, channels), F32)
    for k in range(3):
        gsa += mm(
            extended[k * cells : k * cells + rows],
            full_wt[k * channels : (k + 1) * channels],
            NT,
        )
    gsa_ref[...] = gsa.astype(BF16)
    gsa_t[...] = gsa.astype(BF16).astype(F32).T.astype(BF16)
    _, normed, sig = normalise(lat_ref, stats_ref, count, per_group)
    act = (normed * sig).astype(BF16).astype(F32)
    store_shifted(act_pad, act, frames, cells, cols)
    left = core_order(gsa_t, W, core) if aligned else gsa_t[...]
    shard = wt_ref.shape[0] * 3
    for dy in range(3):
        for dx in range(3):
            at = (3 * dy + dx) * channels
            seen = window(act_pad, dy, dx, frames, cells, cols)
            seen_ref[:, at : at + channels] = seen
            put(mm(left, seen), at, shard, keep_ref, send_ref)


def second_body(
    sizes, lat_ref, cot_t_ref, halo_ref, stats_ref, gsa_ref, seen_ref, ws_ref, *rest
):
    D, W, frames, cells, cols, count, per_group, aligned = sizes
    pieces, rest = rest[: 2 * (D - 1)], rest[2 * (D - 1) :]
    full_ws, side_ws, gsa_pad, gsa_seen, cot_t = rest[-5:]
    spatial_ref, grad_ref, keep_ref, other_ref = rest[:4]
    send_ref = other_ref if aligned else None
    channels = lat_ref.shape[1]
    core = lax.rem(lax.axis_index("wide"), 2)
    fill_spatial(full_ws, ws_ref, pieces, D)
    rows = frames * cells
    white, normed, sig = normalise(lat_ref, stats_ref, count, per_group)
    store_shifted(gsa_pad, gsa_ref[...].astype(F32), frames, cells, cols)
    cot_t[:, :rows] = cot_t_ref[...]
    for f in range(2):
        cot_t[:, rows + f * cells : rows + (f + 1) * cells] = (
            halo_ref[f * cells : (f + 1) * cells].astype(F32).T.astype(BF16)
        )
    left = core_order(cot_t, W, core) if aligned else cot_t[...]
    spatial = mm(seen_ref[...], full_ws[...]).astype(BF16)
    spatial_ref[...] = spatial
    shard = ws_ref.shape[0] // 3
    for k in range(3):
        block = mm(left[:, k * cells : k * cells + rows], spatial)
        put(block, k * channels, shard, keep_ref, send_ref)

    for dy in range(3):
        for dx in range(3):
            at = (3 * dy + dx) * channels
            gsa_seen[:, at : at + channels] = window(
                gsa_pad, 2 - dy, 2 - dx, frames, cells, cols
            )
            side_ws[:, at : at + channels] = full_ws[at : at + channels]
    grad = mm(gsa_seen[...], side_ws[...], NT)
    grad = grad * (sig * (1.0 + normed * (1.0 - sig)))
    grad_ref[...] = grad
    gain_term = jnp.sum(grad * white, axis=0, keepdims=True)
    bias_term = jnp.sum(grad, axis=0, keepdims=True)
    if not aligned:
        both = jnp.concatenate([gain_term, bias_term], axis=0)
        other_ref[...] = jnp.broadcast_to(both[None], other_ref.shape)
        return
    d = lax.axis_index("dp")
    quarter = jnp.concatenate(
        [term[:, at : at + 128] for term in (gain_term, bias_term) for at in (0, 128)], axis=0
    )
    low = in_parts(
        jnp.concatenate([jnp.where(d == s, quarter, 0.0) for s in range(2)], axis=0)
    )
    for target in (keep_ref, send_ref):
        for owner in range(D):
            for at in range(0, channels // 2, 16):
                target[owner, at : at + 16, shard:] = low


def block_body(sizes, lat_ref, spatial_ref, before_ref, wt_ref, *rest):
    D, W, frames, cells, cols, count, per_group, aligned = sizes
    firsts = rest[: D - 1]
    block_ref, full_wt = rest[D - 1 :]
    channels = lat_ref.shape[1]
    fill_temporal(full_wt, wt_ref, firsts, D)
    extended = jnp.concatenate([before_ref[...], spatial_ref[...]], axis=0)
    rows = frames * cells
    temporal = jnp.zeros((rows, channels), F32)
    for k in range(3):
        start = (2 - k) * cells
        temporal += mm(
            extended[start : start + rows], full_wt[k * channels : (k + 1) * channels]
        )
    block_ref[...] = (lat_ref[...].astype(F32) + temporal).astype(BF16)


def latent_gradient(sizes, total, lat_ref, cot_ref, stats_ref, grad_ref):
    D, W, frames, cells, cols, count, per_group, aligned = sizes
    white, inv_std = whiten(lat_ref[...], stats_ref[...], count, per_group)
    gain = affine_of(stats_ref)[0:1]
    means = group_total(total * gain, per_group) / count
    inner = inv_std * (grad_ref[...] * gain - means[1:2] - white * means[0:1])
    return (cot_ref[...].astype(F32) + inner).astype(BF16)


def plane_body(keep_s, got_s, keep_t, got_t, *outs):
    d = lax.axis_index("dp")
    y = lax.rem(lax.axis_index("wide") // 2, 2)
    split = keep_s.shape[-1]
    ride = outs[0].shape[-1] - 128
    for a in range(2):
        for b in range(2):
            owner, side = lax.rem(d + a, 2), lax.rem(y + b, 2)
            out = outs[2 * a + b]
            for z in range(out.shape[0]):
                out[z, :, :split] = add([keep_s[owner, z, side], got_s[owner, z, side]]).astype(
                    BF16
                )
                both = [keep_t[owner, z, side], got_t[owner, z, side]]
                out[z, :, split:ride] = add([t[:, : ride - split] for t in both]).astype(BF16)
                out[z, :, ride:] = in_parts(from_parts([t[:, ride - split :] for t in both]))


def line_body(depth, *refs):
    terms, outs = refs[:4], refs[4:]
    z = lax.axis_index("wide") // 4
    ride = outs[0].shape[-1] - 128
    for s in range(depth):
        owner = lax.rem(z + s, depth)
        seen = [term[owner] for term in terms]
        outs[s][:, :ride] = add([t[:, :ride] for t in seen]).astype(BF16)
        outs[s][:, ride:] = in_parts(from_parts([t[:, ride:] for t in seen]))


def last_body(sizes, scale, depth, *refs):
    terms, operands, outs = refs[:depth], refs[depth:-4], refs[-4:]
    spatial_ref, temporal_ref, norm_ref, glat_ref = outs
    split = spatial_ref.shape[1]
    ride = terms[0].shape[1] - 128
    sums = from_parts([term[:, ride:] for term in terms])

    def rows_of(part):
        return jnp.concatenate(
            [jnp.concatenate([part[at : at + 1], part[at + 1 : at + 2]], axis=1) for at in (0, 2)],
            axis=0,
        )

    first, second = rows_of(sums[0:4]), rows_of(sums[4:8])
    own = jnp.where(lax.axis_index("dp") == 0, first, second)
    glat_ref[...] = latent_gradient(sizes, own, *operands)
    norm_columns(scale, first + second, norm_ref)
    total = add([term[:, :ride] for term in terms]) * scale
    spatial_ref[...] = total[:, :split]
    temporal_ref[...] = total[:, split:]


def apart_body(sizes, scale, sums_ref, *refs):
    norm_ref, glat_ref = refs[-2:]
    W = sizes[1]
    own = jnp.sum(sums_ref[pl.ds(lax.axis_index("dp") * W, W)], axis=0)
    norm_columns(scale, jnp.sum(sums_ref[...], axis=0), norm_ref)
    glat_ref[...] = latent_gradient(sizes, own, *refs[:-2])


def norm_columns(scale, norm, norm_ref):
    channels, width = norm.shape[1], norm_ref.shape[1]
    row = lax.broadcasted_iota(jnp.int32, (channels, width), 0)
    column = lax.broadcasted_iota(jnp.int32, (channels, width), 1)
    pick = (row == column + lax.axis_index("wide") * width).astype(F32)
    norm_ref[...] = (
        lax.dot_general(
            norm, pick, NN, precision=lax.Precision.HIGHEST, preferred_element_type=F32
        )
        * scale
    )


def local(latents, cotangent, norm_gain, norm_bias, w_spatial, w_temporal):
    D, W = lax.axis_size("dp"), lax.axis_size("wide")
    _, frames, rows_here, cols, channels = latents.shape
    cells = rows_here * cols
    rows = frames * cells
    per_group = channels // GROUPS
    count = W * frames * cells * per_group
    shard_s, shard_t = w_spatial.shape[0], w_temporal.shape[0]
    aligned = (channels // W) % 16 == 0 and shard_s % 128 == 0 and shard_t % 128 == 0
    aligned = aligned and W % 4 == 0 and D == 2 and channels == 256
    sizes = (D, W, frames, cells, cols, count, per_group, aligned)
    scale = 1.0 / math.sqrt(D * W * frames * cells)

    lat, cot = latents.reshape(rows, channels), cotangent.reshape(rows, channels)
    gain, bias = norm_gain.reshape(1, channels), norm_bias.reshape(1, channels)

    def over_all(moves):
        pairs = []
        for d in range(D):
            for w in range(W):
                to = moves(d, w)
                pairs.append((d * W + w, to[0] * W + to[1]))
        return pairs

    def send(value, moves):
        return lax.ppermute(value, ("dp", "wide"), over_all(moves))

    R = shard_s + shard_t
    stats, half = call(
        stats_body,
        [
            shape((W, 2, 2 * channels), F32),
            shape((shard_s // 2 + shard_t, channels), BF16),
        ],
        [
            pltpu.VMEM((rows, channels), BF16),
            pltpu.VMEM((1, channels), F32),
            pltpu.VMEM((1, channels), F32),
            pltpu.SemaphoreType.DMA((5,)),
        ],
        in_specs=[HBM] * 5,
        vmem=FIRST_VMEM,
    )(lat, gain, bias, w_spatial, w_temporal)
    cot_t = call(transpose_body, shape((channels, rows), BF16), moved=300_000)(cot)
    firsts = [send(half, lambda d, w: ((d + s) % D, w)) for s in range(1, D)]

    halo = lax.ppermute(cot, "wide", [(w + 1, w) for w in range(W - 1)])
    stats = lax.all_to_all(stats, "wide", split_axis=0, concat_axis=0, tiled=True)
    firsts, stats, halo, cot_t = lax.optimization_barrier((firsts, stats, halo, cot_t))
    pieces = []
    for first in firsts:
        pieces += [first, send(first, lambda d, w: (d, w ^ 1))]

    ride = 128 if aligned else 0
    if aligned:
        terms_s = [shape((D, channels // 2, shard_s), BF16)] * 2
        terms_t = [shape((D, channels // 2, shard_t + ride), BF16)] * 2
    else:
        terms_s = [shape((channels, D * shard_s), BF16)]
        terms_t = [shape((channels, D * shard_t), BF16), shape((D * W, 2, channels), F32)]
    pad = pltpu.VMEM((3, frames, cells + 2 * cols, channels), BF16)
    taps = D * shard_s
    gsa, seen, *grads_s = call(
        functools.partial(first_body, sizes),
        [shape((rows, channels), BF16), shape((rows, taps), BF16)] + terms_s,
        [pltpu.VMEM((D * shard_t, channels), BF16), pad, pltpu.VMEM((channels, rows), BF16)],
        flops=2 * 12 * rows * channels * channels,
        moved=3_000_000,
    )(lat, cot, halo, stats, w_temporal, *firsts)
    spatial, grad, *grads_t = call(
        functools.partial(second_body, sizes),
        [shape((rows, channels), BF16), shape((rows, channels), F32)] + terms_t,
        [
            pltpu.VMEM((taps, channels), BF16),
            pltpu.VMEM((channels, taps), BF16),
            pad,
            pltpu.VMEM((rows, taps), BF16),
            pltpu.VMEM((channels, rows + 2 * cells), BF16),
        ],
        flops=2 * 21 * rows * channels * channels,
        moved=3_000_000,
    )(lat, cot_t, halo, stats, gsa, seen, w_spatial, *pieces)
    before = lax.ppermute(spatial, "wide", [(w, w + 1) for w in range(W - 1)])
    block_out = call(
        functools.partial(block_body, sizes),
        shape((rows, channels), BF16),
        [pltpu.VMEM((D * shard_t, channels), BF16)],
        flops=2 * 3 * rows * channels * channels,
        moved=1_000_000,
    )(lat, spatial, before, w_temporal, *firsts)

    width = channels // W
    operands = (lat, cot, stats, grad)
    if aligned:
        Z = W // 4

        def over_core(away):
            return send(away, lambda d, w: (d, w ^ 1))

        pairs = []
        for keep, away in (grads_s, grads_t):
            view = (D, Z, 2, width, keep.shape[-1])
            pairs += [keep.reshape(view), over_core(away).reshape(view)]
        plane = call(
            plane_body, [shape((Z, width, R + ride), BF16)] * (2 * D), moved=3_000_000
        )(*pairs)
        parts = [plane[0]] + [
            send(plane[2 * a + b], lambda d, w: ((d + a) % D, w ^ (2 * b)))
            for a, b in ((0, 1), (1, 0), (1, 1))
        ]
        line = call(
            functools.partial(line_body, Z),
            [shape((width, R + ride), BF16)] * Z,
            moved=1_000_000,
        )(*parts)
        terms = [line[0]]
        for s in range(1, Z):
            terms.append(send(line[s], lambda d, w: (d, (w + 4 * s) % W)))
        grad_s, grad_t, norm, grad_latents = call(
            functools.partial(last_body, sizes, scale, Z),
            [
                shape((width, shard_s), F32),
                shape((width, shard_t), F32),
                shape((2, width), F32),
                shape((rows, channels), BF16),
            ],
            moved=1_000_000,
        )(*terms, *operands)
        grad_s, grad_t = grad_s.T, grad_t.T
    else:
        sums = lax.all_to_all(
            grads_t[1], ("dp", "wide"), split_axis=0, concat_axis=0, tiled=True
        )
        norm, grad_latents = call(
            functools.partial(apart_body, sizes, scale),
            [shape((2, width), F32), shape((rows, channels), BF16)],
        )(sums, *operands)
        outs = []
        for full in (grads_s[0], grads_t[0]):
            part = lax.psum_scatter(
                full.astype(F32), "wide", scatter_dimension=0, tiled=True
            ).T.astype(BF16)
            part = lax.psum_scatter(part, "dp", scatter_dimension=0, tiled=True)
            outs.append(part.astype(F32) * scale)
        grad_s, grad_t = outs
    return (
        block_out.reshape(latents.shape),
        grad_latents.reshape(latents.shape),
        grad_s,
        grad_t,
        norm,
    )


def solution(mesh):
    return jax.shard_map(
        local,
        mesh=mesh,
        in_specs=(
            P("dp", "wide", None, None, None),
            P("dp", "wide", None, None, None),
            P(),
            P(),
            P("dp", None),
            P("dp", None),
        ),
        out_specs=(
            P("dp", "wide", None, None, None),
            P("dp", "wide", None, None, None),
            P("dp", "wide"),
            P("dp", "wide"),
            P(None, "wide"),
        ),
        check_vma=False,
    )
```

```python
import functools
import math

import jax
import jax.numpy as jnp
from jax import lax
from jax.experimental import pallas as pl
from jax.experimental.pallas import tpu as pltpu
from jax.sharding import PartitionSpec as P

GROUPS = 32
EPSILON = 1e-05
F32 = jnp.float32
BF16 = jnp.bfloat16
VMEM = pl.BlockSpec(memory_space=pltpu.VMEM)
HBM = pl.BlockSpec(memory_space=pltpu.HBM)
FIRST_VMEM = 60 << 20
NT = (((1,), (1,)), ((), ()))
NN = (((1,), (0,)), ((), ()))


def call(body, out_shapes, scratch=(), flops=0, moved=0, in_specs=None, vmem=40 << 20):
    many = isinstance(out_shapes, (tuple, list))

    def run(*operands):
        return pl.pallas_call(
            body,
            out_shape=out_shapes,
            in_specs=in_specs or [VMEM] * len(operands),
            out_specs=[VMEM] * len(out_shapes) if many else VMEM,
            scratch_shapes=list(scratch),
            compiler_params=pltpu.CompilerParams(vmem_limit_bytes=vmem),
            cost_estimate=pl.CostEstimate(
                flops=flops, bytes_accessed=moved, transcendentals=0
            ),
        )(*operands)

    return run


def shape(dims, kind):
    return jax.ShapeDtypeStruct(dims, kind)


def mm(left, right, dims=NN):
    return lax.dot_general(left, right, dims, preferred_element_type=F32)


def group_total(rows, per_group):
    channels = rows.shape[-1]
    first = lax.broadcasted_iota(jnp.int32, (channels, channels), 0) // per_group
    second = lax.broadcasted_iota(jnp.int32, (channels, channels), 1) // per_group
    same = (first == second).astype(F32)
    return lax.dot_general(
        rows, same, NN, precision=lax.Precision.HIGHEST, preferred_element_type=F32
    )


def cut_body(ws_ref, wt_ref, half_ref, sems):
    core = lax.rem(lax.axis_index("wide"), 2)
    half = ws_ref.shape[0] // 2
    start = pl.multiple_of(core * half, 16)
    moves = (
        (ws_ref.at[pl.ds(start, half)], half_ref.at[pl.ds(0, half)]),
        (wt_ref, half_ref.at[pl.ds(half, wt_ref.shape[0])]),
    )
    copies = [pltpu.make_async_copy(*move, sems.at[at]) for at, move in enumerate(moves)]
    for copy in copies:
        copy.start()
    for copy in copies:
        copy.wait()


def stats_body(lat_ref, gain_ref, bias_ref, out_ref):
    x = lat_ref[...].astype(F32)
    sums = [jnp.sum(x, axis=0, keepdims=True), jnp.sum(x * x, axis=0, keepdims=True)]
    both = jnp.concatenate(
        [
            jnp.concatenate([sums[0], gain_ref[...]], axis=1),
            jnp.concatenate([sums[1], bias_ref[...]], axis=1),
        ],
        axis=0,
    )
    out_ref[...] = jnp.broadcast_to(both[None], out_ref.shape)


def transpose_body(cot_ref, out_ref):
    out_ref[...] = cot_ref[...].astype(F32).T.astype(BF16)


def fill_spatial(full, shard_ref, pieces, D):
    d = lax.axis_index("dp")
    core = lax.rem(lax.axis_index("wide"), 2)
    n = shard_ref.shape[0]
    half = n // 2
    full[pl.ds(pl.multiple_of(d * n, 16), n)] = shard_ref[...]
    for s in range(1, D):
        source = lax.rem(d + D - s, D)
        for which in range(2):
            holder = core if which == 0 else 1 - core
            start = pl.multiple_of(source * n + holder * half, 16)
            full[pl.ds(start, half)] = pieces[2 * (s - 1) + which][0:half]


def fill_temporal(full, shard_ref, firsts, D):
    d = lax.axis_index("dp")
    n = shard_ref.shape[0]
    full[pl.ds(pl.multiple_of(d * n, 16), n)] = shard_ref[...]
    for s in range(1, D):
        start = pl.multiple_of(lax.rem(d + D - s, D) * n, 16)
        full[pl.ds(start, n)] = firsts[s - 1][firsts[s - 1].shape[0] - n :]


def whiten(lat, stats, count, per_group):
    total = group_total(jnp.sum(stats[:, :, : lat.shape[1]], axis=0), per_group) / count
    mean = total[0:1]
    inv_std = 1.0 / jnp.sqrt(total[1:2] - mean * mean + EPSILON)
    return (lat.astype(F32) - mean) * inv_std, inv_std


def store_shifted(pad_ref, values, frames, cells, cols):
    total = frames * cells
    column = lax.broadcasted_iota(jnp.int32, (total, 1), 0) % cols
    left = jnp.where(column == 0, 0.0, pltpu.roll(values, 1, 0))
    right = jnp.where(column == cols - 1, 0.0, pltpu.roll(values, total - 1, 0))
    edge = jnp.zeros((cols, values.shape[1]), BF16)
    for at, form in enumerate((left, values, right)):
        low = form.astype(BF16)
        for f in range(frames):
            pad_ref[at, f, 0:cols] = edge
            pad_ref[at, f, cols : cols + cells] = low[f * cells : (f + 1) * cells]
            pad_ref[at, f, cols + cells :] = edge


def window(pad_ref, dy, dx, frames, cells, cols):
    return jnp.concatenate(
        [pad_ref[dx, f, dy * cols : dy * cols + cells] for f in range(frames)], axis=0
    )


def in_parts(total):
    high = total.astype(BF16).astype(F32)
    return jnp.concatenate([high, total - high], axis=0).astype(BF16)


def from_parts(terms):
    total = 0.0
    for term in terms:
        wide = term.astype(F32)
        total = total + (wide[0:8] + wide[8:16])
    return total


def add(terms):
    total = terms[0].astype(F32)
    for term in terms[1:]:
        total += term.astype(F32)
    return total


def core_order(transposed_ref, W, core):
    step = transposed_ref.shape[0] // W
    order = [(2 * j + core) * step for j in range(W // 2)]
    order += [(2 * j + 1 - core) * step for j in range(W // 2)]
    return jnp.concatenate(
        [transposed_ref[pl.ds(pl.multiple_of(at, 16), step)] for at in order], axis=0
    )


def put(block, column, shard, keep_ref, send_ref):
    low = block.astype(BF16)
    if send_ref is None:
        keep_ref[:, column : column + block.shape[1]] = low
        return
    half = block.shape[0] // 2
    for at in range(0, block.shape[1], 128):
        owner, place = (column + at) // shard, (column + at) % shard
        keep_ref[owner, :, place : place + 128] = low[:half, at : at + 128]
        send_ref[owner, :, place : place + 128] = low[half:, at : at + 128]


def affine_of(stats_ref):
    return stats_ref[0, :, stats_ref.shape[2] // 2 :]


def normalise(lat_ref, stats_ref, count, per_group):
    white, inv_std = whiten(lat_ref[...], stats_ref[...], count, per_group)
    affine = affine_of(stats_ref)
    normed = white * affine[0:1] + affine[1:2]
    return white, normed, jax.nn.sigmoid(normed)


def first_body(sizes, lat_ref, cot_ref, halo_ref, stats_ref, wt_ref, *rest):
    D, W, frames, cells, cols, count, per_group, aligned = sizes
    firsts, rest = rest[: D - 1], rest[D - 1 :]
    full_wt, act_pad, gsa_t = rest[-3:]
    gsa_ref, seen_ref, keep_ref = rest[:3]
    send_ref = rest[3] if aligned else None
    channels = lat_ref.shape[1]
    core = lax.rem(lax.axis_index("wide"), 2)
    fill_temporal(full_wt, wt_ref, firsts, D)
    rows = frames * cells
    extended = jnp.concatenate([cot_ref[...], halo_ref[...]], axis=0)
    gsa = jnp.zeros((rows, channels), F32)
    for k in range(3):
        gsa += mm(
            extended[k * cells : k * cells + rows],
            full_wt[k * channels : (k + 1) * channels],
            NT,
        )
    gsa_ref[...] = gsa.astype(BF16)
    gsa_t[...] = gsa.astype(BF16).astype(F32).T.astype(BF16)
    _, normed, sig = normalise(lat_ref, stats_ref, count, per_group)
    act = (normed * sig).astype(BF16).astype(F32)
    store_shifted(act_pad, act, frames, cells, cols)
    left = core_order(gsa_t, W, core) if aligned else gsa_t[...]
    shard = wt_ref.shape[0] * 3
    for dy in range(3):
        for dx in range(3):
            at = (3 * dy + dx) * channels
            seen = window(act_pad, dy, dx, frames, cells, cols)
            seen_ref[:, at : at + channels] = seen
            put(mm(left, seen), at, shard, keep_ref, send_ref)


def second_body(
    sizes, lat_ref, cot_t_ref, halo_ref, stats_ref, gsa_ref, seen_ref, ws_ref, *rest
):
    D, W, frames, cells, cols, count, per_group, aligned = sizes
    pieces, rest = rest[: 2 * (D - 1)], rest[2 * (D - 1) :]
    full_ws, side_ws, gsa_pad, gsa_seen, cot_t = rest[-5:]
    spatial_ref, grad_ref, keep_ref, other_ref = rest[:4]
    send_ref = other_ref if aligned else None
    channels = lat_ref.shape[1]
    core = lax.rem(lax.axis_index("wide"), 2)
    fill_spatial(full_ws, ws_ref, pieces, D)
    rows = frames * cells
    white, normed, sig = normalise(lat_ref, stats_ref, count, per_group)
    store_shifted(gsa_pad, gsa_ref[...].astype(F32), frames, cells, cols)
    cot_t[:, :rows] = cot_t_ref[...]
    for f in range(2):
        cot_t[:, rows + f * cells : rows + (f + 1) * cells] = (
            halo_ref[f * cells : (f + 1) * cells].astype(F32).T.astype(BF16)
        )
    left = core_order(cot_t, W, core) if aligned else cot_t[...]
    spatial = mm(seen_ref[...], full_ws[...]).astype(BF16)
    spatial_ref[...] = spatial
    shard = ws_ref.shape[0] // 3
    for k in range(3):
        block = mm(left[:, k * cells : k * cells + rows], spatial)
        put(block, k * channels, shard, keep_ref, send_ref)

    for dy in range(3):
        for dx in range(3):
            at = (3 * dy + dx) * channels
            gsa_seen[:, at : at + channels] = window(
                gsa_pad, 2 - dy, 2 - dx, frames, cells, cols
            )
            side_ws[:, at : at + channels] = full_ws[at : at + channels]
    grad = mm(gsa_seen[...], side_ws[...], NT)
    grad = grad * (sig * (1.0 + normed * (1.0 - sig)))
    grad_ref[...] = grad
    gain_term = jnp.sum(grad * white, axis=0, keepdims=True)
    bias_term = jnp.sum(grad, axis=0, keepdims=True)
    if not aligned:
        both = jnp.concatenate([gain_term, bias_term], axis=0)
        other_ref[...] = jnp.broadcast_to(both[None], other_ref.shape)
        return
    d = lax.axis_index("dp")
    quarter = jnp.concatenate(
        [term[:, at : at + 128] for term in (gain_term, bias_term) for at in (0, 128)], axis=0
    )
    low = in_parts(
        jnp.concatenate([jnp.where(d == s, quarter, 0.0) for s in range(2)], axis=0)
    )
    for target in (keep_ref, send_ref):
        for owner in range(D):
            for at in range(0, channels // 2, 16):
                target[owner, at : at + 16, shard:] = low


def block_body(sizes, lat_ref, spatial_ref, before_ref, wt_ref, *rest):
    D, W, frames, cells, cols, count, per_group, aligned = sizes
    firsts = rest[: D - 1]
    block_ref, full_wt = rest[D - 1 :]
    channels = lat_ref.shape[1]
    fill_temporal(full_wt, wt_ref, firsts, D)
    extended = jnp.concatenate([before_ref[...], spatial_ref[...]], axis=0)
    rows = frames * cells
    temporal = jnp.zeros((rows, channels), F32)
    for k in range(3):
        start = (2 - k) * cells
        temporal += mm(
            extended[start : start + rows], full_wt[k * channels : (k + 1) * channels]
        )
    block_ref[...] = (lat_ref[...].astype(F32) + temporal).astype(BF16)


def latent_gradient(sizes, total, lat_ref, cot_ref, stats_ref, grad_ref):
    D, W, frames, cells, cols, count, per_group, aligned = sizes
    white, inv_std = whiten(lat_ref[...], stats_ref[...], count, per_group)
    gain = affine_of(stats_ref)[0:1]
    means = group_total(total * gain, per_group) / count
    inner = inv_std * (grad_ref[...] * gain - means[1:2] - white * means[0:1])
    return (cot_ref[...].astype(F32) + inner).astype(BF16)


def plane_body(keep_s, got_s, keep_t, got_t, *outs):
    d = lax.axis_index("dp")
    y = lax.rem(lax.axis_index("wide") // 2, 2)
    split = keep_s.shape[-1]
    ride = outs[0].shape[-1] - 128
    for a in range(2):
        for b in range(2):
            owner, side = lax.rem(d + a, 2), lax.rem(y + b, 2)
            out = outs[2 * a + b]
            for z in range(out.shape[0]):
                out[z, :, :split] = add([keep_s[owner, z, side], got_s[owner, z, side]]).astype(
                    BF16
                )
                both = [keep_t[owner, z, side], got_t[owner, z, side]]
                out[z, :, split:ride] = add([t[:, : ride - split] for t in both]).astype(BF16)
                out[z, :, ride:] = in_parts(from_parts([t[:, ride - split :] for t in both]))


def line_body(depth, *refs):
    terms, outs = refs[:4], refs[4:]
    z = lax.axis_index("wide") // 4
    ride = outs[0].shape[-1] - 128
    for s in range(depth):
        owner = lax.rem(z + s, depth)
        seen = [term[owner] for term in terms]
        outs[s][:, :ride] = add([t[:, :ride] for t in seen]).astype(BF16)
        outs[s][:, ride:] = in_parts(from_parts([t[:, ride:] for t in seen]))


def last_body(sizes, scale, depth, *refs):
    terms, operands, outs = refs[:depth], refs[depth:-4], refs[-4:]
    spatial_ref, temporal_ref, norm_ref, glat_ref = outs
    split = spatial_ref.shape[1]
    ride = terms[0].shape[1] - 128
    sums = from_parts([term[:, ride:] for term in terms])

    def rows_of(part):
        return jnp.concatenate(
            [jnp.concatenate([part[at : at + 1], part[at + 1 : at + 2]], axis=1) for at in (0, 2)],
            axis=0,
        )

    first, second = rows_of(sums[0:4]), rows_of(sums[4:8])
    own = jnp.where(lax.axis_index("dp") == 0, first, second)
    glat_ref[...] = latent_gradient(sizes, own, *operands)
    norm_columns(scale, first + second, norm_ref)
    total = add([term[:, :ride] for term in terms]) * scale
    spatial_ref[...] = total[:, :split]
    temporal_ref[...] = total[:, split:]


def apart_body(sizes, scale, sums_ref, *refs):
    norm_ref, glat_ref = refs[-2:]
    W = sizes[1]
    own = jnp.sum(sums_ref[pl.ds(lax.axis_index("dp") * W, W)], axis=0)
    norm_columns(scale, jnp.sum(sums_ref[...], axis=0), norm_ref)
    glat_ref[...] = latent_gradient(sizes, own, *refs[:-2])


def norm_columns(scale, norm, norm_ref):
    channels, width = norm.shape[1], norm_ref.shape[1]
    row = lax.broadcasted_iota(jnp.int32, (channels, width), 0)
    column = lax.broadcasted_iota(jnp.int32, (channels, width), 1)
    pick = (row == column + lax.axis_index("wide") * width).astype(F32)
    norm_ref[...] = (
        lax.dot_general(
            norm, pick, NN, precision=lax.Precision.HIGHEST, preferred_element_type=F32
        )
        * scale
    )


def local(latents, cotangent, norm_gain, norm_bias, w_spatial, w_temporal):
    D, W = lax.axis_size("dp"), lax.axis_size("wide")
    _, frames, rows_here, cols, channels = latents.shape
    cells = rows_here * cols
    rows = frames * cells
    per_group = channels // GROUPS
    count = W * frames * cells * per_group
    shard_s, shard_t = w_spatial.shape[0], w_temporal.shape[0]
    aligned = (channels // W) % 16 == 0 and shard_s % 128 == 0 and shard_t % 128 == 0
    aligned = aligned and W % 4 == 0 and D == 2 and channels == 256
    sizes = (D, W, frames, cells, cols, count, per_group, aligned)
    scale = 1.0 / math.sqrt(D * W * frames * cells)

    lat, cot = latents.reshape(rows, channels), cotangent.reshape(rows, channels)
    gain, bias = norm_gain.reshape(1, channels), norm_bias.reshape(1, channels)

    def over_all(moves):
        pairs = []
        for d in range(D):
            for w in range(W):
                to = moves(d, w)
                pairs.append((d * W + w, to[0] * W + to[1]))
        return pairs

    def send(value, moves):
        return lax.ppermute(value, ("dp", "wide"), over_all(moves))

    R = shard_s + shard_t
    half = call(
        cut_body,
        shape((shard_s // 2 + shard_t, channels), BF16),
        [pltpu.SemaphoreType.DMA((2,))],
        in_specs=[HBM] * 2,
        vmem=FIRST_VMEM,
    )(w_spatial, w_temporal)
    stats = call(stats_body, shape((W, 2, 2 * channels), F32))(lat, gain, bias)
    cot_t = call(transpose_body, shape((channels, rows), BF16), moved=300_000)(cot)
    firsts = [send(half, lambda d, w: ((d + s) % D, w)) for s in range(1, D)]

    halo = lax.ppermute(cot, "wide", [(w + 1, w) for w in range(W - 1)])
    stats = lax.all_to_all(stats, "wide", split_axis=0, concat_axis=0, tiled=True)
    firsts, stats, halo, cot_t = lax.optimization_barrier((firsts, stats, halo, cot_t))
    pieces = []
    for first in firsts:
        pieces += [first, send(first, lambda d, w: (d, w ^ 1))]

    ride = 128 if aligned else 0
    if aligned:
        terms_s = [shape((D, channels // 2, shard_s), BF16)] * 2
        terms_t = [shape((D, channels // 2, shard_t + ride), BF16)] * 2
    else:
        terms_s = [shape((channels, D * shard_s), BF16)]
        terms_t = [shape((channels, D * shard_t), BF16), shape((D * W, 2, channels), F32)]
    pad = pltpu.VMEM((3, frames, cells + 2 * cols, channels), BF16)
    taps = D * shard_s
    gsa, seen, *grads_s = call(
        functools.partial(first_body, sizes),
        [shape((rows, channels), BF16), shape((rows, taps), BF16)] + terms_s,
        [pltpu.VMEM((D * shard_t, channels), BF16), pad, pltpu.VMEM((channels, rows), BF16)],
        flops=2 * 12 * rows * channels * channels,
        moved=3_000_000,
    )(lat, cot, halo, stats, w_temporal, *firsts)
    spatial, grad, *grads_t = call(
        functools.partial(second_body, sizes),
        [shape((rows, channels), BF16), shape((rows, channels), F32)] + terms_t,
        [
            pltpu.VMEM((taps, channels), BF16),
            pltpu.VMEM((channels, taps), BF16),
            pad,
            pltpu.VMEM((rows, taps), BF16),
            pltpu.VMEM((channels, rows + 2 * cells), BF16),
        ],
        flops=2 * 21 * rows * channels * channels,
        moved=3_000_000,
    )(lat, cot_t, halo, stats, gsa, seen, w_spatial, *pieces)
    before = lax.ppermute(spatial, "wide", [(w, w + 1) for w in range(W - 1)])
    block_out = call(
        functools.partial(block_body, sizes),
        shape((rows, channels), BF16),
        [pltpu.VMEM((D * shard_t, channels), BF16)],
        flops=2 * 3 * rows * channels * channels,
        moved=1_000_000,
    )(lat, spatial, before, w_temporal, *firsts)

    width = channels // W
    operands = (lat, cot, stats, grad)
    if aligned:
        Z = W // 4

        def over_core(away):
            return send(away, lambda d, w: (d, w ^ 1))

        pairs = []
        for keep, away in (grads_s, grads_t):
            view = (D, Z, 2, width, keep.shape[-1])
            pairs += [keep.reshape(view), over_core(away).reshape(view)]
        plane = call(
            plane_body, [shape((Z, width, R + ride), BF16)] * (2 * D), moved=3_000_000
        )(*pairs)
        parts = [plane[0]] + [
            send(plane[2 * a + b], lambda d, w: ((d + a) % D, w ^ (2 * b)))
            for a, b in ((0, 1), (1, 0), (1, 1))
        ]
        line = call(
            functools.partial(line_body, Z),
            [shape((width, R + ride), BF16)] * Z,
            moved=1_000_000,
        )(*parts)
        terms = [line[0]]
        for s in range(1, Z):
            terms.append(send(line[s], lambda d, w: (d, (w + 4 * s) % W)))
        grad_s, grad_t, norm, grad_latents = call(
            functools.partial(last_body, sizes, scale, Z),
            [
                shape((width, shard_s), F32),
                shape((width, shard_t), F32),
                shape((2, width), F32),
                shape((rows, channels), BF16),
            ],
            moved=1_000_000,
        )(*terms, *operands)
        grad_s, grad_t = grad_s.T, grad_t.T
    else:
        sums = lax.all_to_all(
            grads_t[1], ("dp", "wide"), split_axis=0, concat_axis=0, tiled=True
        )
        norm, grad_latents = call(
            functools.partial(apart_body, sizes, scale),
            [shape((2, width), F32), shape((rows, channels), BF16)],
        )(sums, *operands)
        outs = []
        for full in (grads_s[0], grads_t[0]):
            part = lax.psum_scatter(
                full.astype(F32), "wide", scatter_dimension=0, tiled=True
            ).T.astype(BF16)
            part = lax.psum_scatter(part, "dp", scatter_dimension=0, tiled=True)
            outs.append(part.astype(F32) * scale)
        grad_s, grad_t = outs
    return (
        block_out.reshape(latents.shape),
        grad_latents.reshape(latents.shape),
        grad_s,
        grad_t,
        norm,
    )


def solution(mesh):
    return jax.shard_map(
        local,
        mesh=mesh,
        in_specs=(
            P("dp", "wide", None, None, None),
            P("dp", "wide", None, None, None),
            P(),
            P(),
            P("dp", None),
            P("dp", None),
        ),
        out_specs=(
            P("dp", "wide", None, None, None),
            P("dp", "wide", None, None, None),
            P("dp", "wide"),
            P("dp", "wide"),
            P(None, "wide"),
        ),
        check_vma=False,
    )
```

```python
import functools
import math

import jax
import jax.numpy as jnp
from jax import lax
from jax.experimental import pallas as pl
from jax.experimental.pallas import tpu as pltpu
from jax.sharding import PartitionSpec as P

GROUPS = 32
EPSILON = 1e-05
F32 = jnp.float32
BF16 = jnp.bfloat16
VMEM = pl.BlockSpec(memory_space=pltpu.VMEM)
HBM = pl.BlockSpec(memory_space=pltpu.HBM)
FIRST_VMEM = 60 << 20
NT = (((1,), (1,)), ((), ()))
NN = (((1,), (0,)), ((), ()))


def call(body, out_shapes, scratch=(), flops=0, moved=0, in_specs=None, vmem=40 << 20):
    many = isinstance(out_shapes, (tuple, list))

    def run(*operands):
        return pl.pallas_call(
            body,
            out_shape=out_shapes,
            in_specs=in_specs or [VMEM] * len(operands),
            out_specs=[VMEM] * len(out_shapes) if many else VMEM,
            scratch_shapes=list(scratch),
            compiler_params=pltpu.CompilerParams(vmem_limit_bytes=vmem),
            cost_estimate=pl.CostEstimate(
                flops=flops, bytes_accessed=moved, transcendentals=0
            ),
        )(*operands)

    return run


def shape(dims, kind):
    return jax.ShapeDtypeStruct(dims, kind)


def mm(left, right, dims=NN):
    return lax.dot_general(left, right, dims, preferred_element_type=F32)


def group_total(rows, per_group):
    channels = rows.shape[-1]
    first = lax.broadcasted_iota(jnp.int32, (channels, channels), 0) // per_group
    second = lax.broadcasted_iota(jnp.int32, (channels, channels), 1) // per_group
    same = (first == second).astype(F32)
    return lax.dot_general(
        rows, same, NN, precision=lax.Precision.HIGHEST, preferred_element_type=F32
    )


def stats_body(lat_ref, gain_ref, bias_ref, out_ref, lat_here, gain_here, bias_here, sems):
    moves = ((lat_ref, lat_here), (gain_ref, gain_here), (bias_ref, bias_here))
    copies = [pltpu.make_async_copy(*move, sems.at[at]) for at, move in enumerate(moves)]
    for copy in copies:
        copy.start()
    for copy in copies:
        copy.wait()
    x = lat_here[...].astype(F32)
    sums = [jnp.sum(x, axis=0, keepdims=True), jnp.sum(x * x, axis=0, keepdims=True)]
    both = jnp.concatenate(
        [
            jnp.concatenate([sums[0], gain_here[...]], axis=1),
            jnp.concatenate([sums[1], bias_here[...]], axis=1),
        ],
        axis=0,
    )
    out_ref[...] = jnp.broadcast_to(both[None], out_ref.shape)


def ready_body(cot_ref, lat_ref, wt_ref, cot_t_ref, *copies):
    for source, target in zip((cot_ref, lat_ref, wt_ref), copies):
        target[...] = source[...]
    cot_t_ref[...] = cot_ref[...].astype(F32).T.astype(BF16)


def fill_weights(full, shard_ref, pieces, fetcher, D):
    d = lax.axis_index("dp")
    core = lax.rem(lax.axis_index("wide"), 2)
    n = shard_ref.shape[0]
    full[pl.ds(pl.multiple_of(d * n, 16), n)] = shard_ref[...]
    for s in range(1, D):
        start = pl.multiple_of(lax.rem(d + D - s, D) * n, 16)
        fetched, passed_on = pieces[2 * (s - 1) : 2 * s]

        @pl.when(core == fetcher)
        def _(start=start, fetched=fetched):
            full[pl.ds(start, n)] = fetched[...]

        @pl.when(core != fetcher)
        def _(start=start, passed_on=passed_on):
            full[pl.ds(start, n)] = passed_on[...]


def whiten(lat, stats, count, per_group):
    total = group_total(jnp.sum(stats[:, :, : lat.shape[1]], axis=0), per_group) / count
    mean = total[0:1]
    inv_std = 1.0 / jnp.sqrt(total[1:2] - mean * mean + EPSILON)
    return (lat.astype(F32) - mean) * inv_std, inv_std


def store_shifted(pad_ref, values, frames, cells, cols):
    total = frames * cells
    column = lax.broadcasted_iota(jnp.int32, (total, 1), 0) % cols
    left = jnp.where(column == 0, 0.0, pltpu.roll(values, 1, 0))
    right = jnp.where(column == cols - 1, 0.0, pltpu.roll(values, total - 1, 0))
    edge = jnp.zeros((cols, values.shape[1]), BF16)
    for at, form in enumerate((left, values, right)):
        low = form.astype(BF16)
        for f in range(frames):
            pad_ref[at, f, 0:cols] = edge
            pad_ref[at, f, cols : cols + cells] = low[f * cells : (f + 1) * cells]
            pad_ref[at, f, cols + cells :] = edge


def window(pad_ref, dy, dx, frames, cells, cols):
    return jnp.concatenate(
        [pad_ref[dx, f, dy * cols : dy * cols + cells] for f in range(frames)], axis=0
    )


def in_parts(total):
    high = total.astype(BF16).astype(F32)
    return jnp.concatenate([high, total - high], axis=0).astype(BF16)


def from_parts(terms):
    total = 0.0
    for term in terms:
        wide = term.astype(F32)
        total = total + (wide[0:8] + wide[8:16])
    return total


def add(terms):
    total = terms[0].astype(F32)
    for term in terms[1:]:
        total += term.astype(F32)
    return total


def core_order(transposed_ref, W, core):
    step = transposed_ref.shape[0] // W
    order = [(2 * j + core) * step for j in range(W // 2)]
    order += [(2 * j + 1 - core) * step for j in range(W // 2)]
    return jnp.concatenate(
        [transposed_ref[pl.ds(pl.multiple_of(at, 16), step)] for at in order], axis=0
    )


def put(block, column, shard, keep_ref, send_ref):
    low = block.astype(BF16)
    if send_ref is None:
        keep_ref[:, column : column + block.shape[1]] = low
        return
    half = block.shape[0] // 2
    for at in range(0, block.shape[1], 128):
        owner, place = (column + at) // shard, (column + at) % shard
        keep_ref[owner, :, place : place + 128] = low[:half, at : at + 128]
        send_ref[owner, :, place : place + 128] = low[half:, at : at + 128]


def affine_of(stats_ref):
    return stats_ref[0, :, stats_ref.shape[2] // 2 :]


def normalise(lat_ref, stats_ref, count, per_group):
    white, inv_std = whiten(lat_ref[...], stats_ref[...], count, per_group)
    affine = affine_of(stats_ref)
    normed = white * affine[0:1] + affine[1:2]
    return white, normed, jax.nn.sigmoid(normed)


def first_body(sizes, lat_ref, cot_ref, halo_ref, stats_ref, wt_ref, *rest):
    D, W, frames, cells, cols, count, per_group, aligned = sizes
    pieces, rest = rest[: 2 * (D - 1)], rest[2 * (D - 1) :]
    full_wt, act_pad, gsa_t = rest[-3:]
    gsa_ref, seen_ref, keep_ref = rest[:3]
    send_ref = rest[3] if aligned else None
    channels = lat_ref.shape[1]
    core = lax.rem(lax.axis_index("wide"), 2)
    fill_weights(full_wt, wt_ref, pieces, 0, D)
    rows = frames * cells
    extended = jnp.concatenate([cot_ref[...], halo_ref[...]], axis=0)
    gsa = jnp.zeros((rows, channels), F32)
    for k in range(3):
        gsa += mm(
            extended[k * cells : k * cells + rows],
            full_wt[k * channels : (k + 1) * channels],
            NT,
        )
    gsa_ref[...] = gsa.astype(BF16)
    gsa_t[...] = gsa.astype(BF16).astype(F32).T.astype(BF16)
    _, normed, sig = normalise(lat_ref, stats_ref, count, per_group)
    act = (normed * sig).astype(BF16).astype(F32)
    store_shifted(act_pad, act, frames, cells, cols)
    left = core_order(gsa_t, W, core) if aligned else gsa_t[...]
    shard = wt_ref.shape[0] * 3
    for dy in range(3):
        for dx in range(3):
            at = (3 * dy + dx) * channels
            seen = window(act_pad, dy, dx, frames, cells, cols)
            seen_ref[:, at : at + channels] = seen
            put(mm(left, seen), at, shard, keep_ref, send_ref)


def second_body(
    sizes, lat_ref, cot_t_ref, halo_ref, stats_ref, gsa_ref, seen_ref, ws_ref, *rest
):
    D, W, frames, cells, cols, count, per_group, aligned = sizes
    pieces, rest = rest[: 2 * (D - 1)], rest[2 * (D - 1) :]
    full_ws, side_ws, gsa_pad, gsa_seen, cot_t = rest[-5:]
    spatial_ref, grad_ref, keep_ref, other_ref = rest[:4]
    send_ref = other_ref if aligned else None
    channels = lat_ref.shape[1]
    core = lax.rem(lax.axis_index("wide"), 2)
    fill_weights(full_ws, ws_ref, pieces, 1, D)
    rows = frames * cells
    white, normed, sig = normalise(lat_ref, stats_ref, count, per_group)
    store_shifted(gsa_pad, gsa_ref[...].astype(F32), frames, cells, cols)
    cot_t[:, :rows] = cot_t_ref[...]
    for f in range(2):
        cot_t[:, rows + f * cells : rows + (f + 1) * cells] = (
            halo_ref[f * cells : (f + 1) * cells].astype(F32).T.astype(BF16)
        )
    left = core_order(cot_t, W, core) if aligned else cot_t[...]
    spatial = mm(seen_ref[...], full_ws[...]).astype(BF16)
    spatial_ref[...] = spatial
    shard = ws_ref.shape[0] // 3
    for k in range(3):
        block = mm(left[:, k * cells : k * cells + rows], spatial)
        put(block, k * channels, shard, keep_ref, send_ref)

    for dy in range(3):
        for dx in range(3):
            at = (3 * dy + dx) * channels
            gsa_seen[:, at : at + channels] = window(
                gsa_pad, 2 - dy, 2 - dx, frames, cells, cols
            )
            side_ws[:, at : at + channels] = full_ws[at : at + channels]
    grad = mm(gsa_seen[...], side_ws[...], NT)
    grad = grad * (sig * (1.0 + normed * (1.0 - sig)))
    grad_ref[...] = grad
    gain_term = jnp.sum(grad * white, axis=0, keepdims=True)
    bias_term = jnp.sum(grad, axis=0, keepdims=True)
    if not aligned:
        both = jnp.concatenate([gain_term, bias_term], axis=0)
        other_ref[...] = jnp.broadcast_to(both[None], other_ref.shape)
        return
    d = lax.axis_index("dp")
    quarter = jnp.concatenate(
        [term[:, at : at + 128] for term in (gain_term, bias_term) for at in (0, 128)], axis=0
    )
    low = in_parts(
        jnp.concatenate([jnp.where(d == s, quarter, 0.0) for s in range(2)], axis=0)
    )
    for target in (keep_ref, send_ref):
        for owner in range(D):
            for at in range(0, channels // 2, 16):
                target[owner, at : at + 16, shard:] = low


def block_body(sizes, lat_ref, spatial_ref, before_ref, wt_ref, *rest):
    D, W, frames, cells, cols, count, per_group, aligned = sizes
    pieces = rest[: 2 * (D - 1)]
    block_ref, full_wt = rest[2 * (D - 1) :]
    channels = lat_ref.shape[1]
    fill_weights(full_wt, wt_ref, pieces, 0, D)
    extended = jnp.concatenate([before_ref[...], spatial_ref[...]], axis=0)
    rows = frames * cells
    temporal = jnp.zeros((rows, channels), F32)
    for k in range(3):
        start = (2 - k) * cells
        temporal += mm(
            extended[start : start + rows], full_wt[k * channels : (k + 1) * channels]
        )
    block_ref[...] = (lat_ref[...].astype(F32) + temporal).astype(BF16)


def latent_gradient(sizes, total, lat_ref, cot_ref, stats_ref, grad_ref):
    D, W, frames, cells, cols, count, per_group, aligned = sizes
    white, inv_std = whiten(lat_ref[...], stats_ref[...], count, per_group)
    gain = affine_of(stats_ref)[0:1]
    means = group_total(total * gain, per_group) / count
    inner = inv_std * (grad_ref[...] * gain - means[1:2] - white * means[0:1])
    return (cot_ref[...].astype(F32) + inner).astype(BF16)


def plane_body(keep_s, got_s, keep_t, got_t, *outs):
    d = lax.axis_index("dp")
    y = lax.rem(lax.axis_index("wide") // 2, 2)
    split = keep_s.shape[-1]
    ride = outs[0].shape[-1] - 128
    for a in range(2):
        for b in range(2):
            owner, side = lax.rem(d + a, 2), lax.rem(y + b, 2)
            out = outs[2 * a + b]
            for z in range(out.shape[0]):
                out[z, :, :split] = add([keep_s[owner, z, side], got_s[owner, z, side]]).astype(
                    BF16
                )
                both = [keep_t[owner, z, side], got_t[owner, z, side]]
                out[z, :, split:ride] = add([t[:, : ride - split] for t in both]).astype(BF16)
                out[z, :, ride:] = in_parts(from_parts([t[:, ride - split :] for t in both]))


def line_body(depth, *refs):
    terms, outs = refs[:4], refs[4:]
    z = lax.axis_index("wide") // 4
    ride = outs[0].shape[-1] - 128
    for s in range(depth):
        owner = lax.rem(z + s, depth)
        seen = [term[owner] for term in terms]
        outs[s][:, :ride] = add([t[:, :ride] for t in seen]).astype(BF16)
        outs[s][:, ride:] = in_parts(from_parts([t[:, ride:] for t in seen]))


def last_body(sizes, scale, depth, *refs):
    terms, operands, outs = refs[:depth], refs[depth:-4], refs[-4:]
    spatial_ref, temporal_ref, norm_ref, glat_ref = outs
    split = spatial_ref.shape[1]
    ride = terms[0].shape[1] - 128
    sums = from_parts([term[:, ride:] for term in terms])

    def rows_of(part):
        return jnp.concatenate(
            [jnp.concatenate([part[at : at + 1], part[at + 1 : at + 2]], axis=1) for at in (0, 2)],
            axis=0,
        )

    first, second = rows_of(sums[0:4]), rows_of(sums[4:8])
    own = jnp.where(lax.axis_index("dp") == 0, first, second)
    glat_ref[...] = latent_gradient(sizes, own, *operands)
    norm_columns(scale, first + second, norm_ref)
    total = add([term[:, :ride] for term in terms]) * scale
    spatial_ref[...] = total[:, :split]
    temporal_ref[...] = total[:, split:]


def apart_body(sizes, scale, sums_ref, *refs):
    norm_ref, glat_ref = refs[-2:]
    W = sizes[1]
    own = jnp.sum(sums_ref[pl.ds(lax.axis_index("dp") * W, W)], axis=0)
    norm_columns(scale, jnp.sum(sums_ref[...], axis=0), norm_ref)
    glat_ref[...] = latent_gradient(sizes, own, *refs[:-2])


def norm_columns(scale, norm, norm_ref):
    channels, width = norm.shape[1], norm_ref.shape[1]
    row = lax.broadcasted_iota(jnp.int32, (channels, width), 0)
    column = lax.broadcasted_iota(jnp.int32, (channels, width), 1)
    pick = (row == column + lax.axis_index("wide") * width).astype(F32)
    norm_ref[...] = (
        lax.dot_general(
            norm, pick, NN, precision=lax.Precision.HIGHEST, preferred_element_type=F32
        )
        * scale
    )


def local(latents, cotangent, norm_gain, norm_bias, w_spatial, w_temporal):
    D, W = lax.axis_size("dp"), lax.axis_size("wide")
    _, frames, rows_here, cols, channels = latents.shape
    cells = rows_here * cols
    rows = frames * cells
    per_group = channels // GROUPS
    count = W * frames * cells * per_group
    shard_s, shard_t = w_spatial.shape[0], w_temporal.shape[0]
    aligned = (channels // W) % 16 == 0 and shard_s % 128 == 0 and shard_t % 128 == 0
    aligned = aligned and W % 4 == 0 and D == 2 and channels == 256
    sizes = (D, W, frames, cells, cols, count, per_group, aligned)
    scale = 1.0 / math.sqrt(D * W * frames * cells)

    lat, cot = latents.reshape(rows, channels), cotangent.reshape(rows, channels)
    gain, bias = norm_gain.reshape(1, channels), norm_bias.reshape(1, channels)

    def over_all(moves):
        pairs = []
        for d in range(D):
            for w in range(W):
                to = moves(d, w)
                pairs.append((d * W + w, to[0] * W + to[1]))
        return pairs

    def send(value, moves):
        return lax.ppermute(value, ("dp", "wide"), over_all(moves))

    R = shard_s + shard_t
    def fetch(value, core):
        return [
            lax.ppermute(
                value,
                ("dp", "wide"),
                [
                    (d * W + w, (d + s) % D * W + w)
                    for d in range(D)
                    for w in range(core, W, 2)
                ],
            )
            for s in range(1, D)
        ]

    def pass_on(values, core):
        pairs = [(w, w ^ 1) for w in range(core, W, 2)]
        return [lax.ppermute(value, "wide", pairs) for value in values]

    firsts = (fetch(w_temporal, 0), fetch(w_spatial, 1))
    stats = call(
        stats_body,
        shape((W, 2, 2 * channels), F32),
        [
            pltpu.VMEM((rows, channels), BF16),
            pltpu.VMEM((1, channels), F32),
            pltpu.VMEM((1, channels), F32),
            pltpu.SemaphoreType.DMA((3,)),
        ],
        in_specs=[HBM] * 3,
        vmem=FIRST_VMEM,
    )(lat, gain, bias)
    ready = call(
        ready_body,
        [
            shape((channels, rows), BF16),
            shape((rows, channels), BF16),
            shape((rows, channels), BF16),
            shape((shard_t, channels), BF16),
        ],
        moved=1_000_000,
    )(cot, lat, w_temporal)

    halo = lax.ppermute(cot, "wide", [(w + 1, w) for w in range(W - 1)])
    stats = lax.all_to_all(stats, "wide", split_axis=0, concat_axis=0, tiled=True)
    firsts, stats, halo, ready = lax.optimization_barrier((firsts, stats, halo, ready))
    cot_t, cot, lat, w_temporal = ready
    pieces_t, pieces_s = (
        [piece for pair in zip(values, pass_on(values, core)) for piece in pair]
        for core, values in enumerate(firsts)
    )

    ride = 128 if aligned else 0
    if aligned:
        terms_s = [shape((D, channels // 2, shard_s), BF16)] * 2
        terms_t = [shape((D, channels // 2, shard_t + ride), BF16)] * 2
    else:
        terms_s = [shape((channels, D * shard_s), BF16)]
        terms_t = [shape((channels, D * shard_t), BF16), shape((D * W, 2, channels), F32)]
    pad = pltpu.VMEM((3, frames, cells + 2 * cols, channels), BF16)
    taps = D * shard_s
    gsa, seen, *grads_s = call(
        functools.partial(first_body, sizes),
        [shape((rows, channels), BF16), shape((rows, taps), BF16)] + terms_s,
        [pltpu.VMEM((D * shard_t, channels), BF16), pad, pltpu.VMEM((channels, rows), BF16)],
        flops=2 * 12 * rows * channels * channels,
        moved=3_000_000,
    )(lat, cot, halo, stats, w_temporal, *pieces_t)
    spatial, grad, *grads_t = call(
        functools.partial(second_body, sizes),
        [shape((rows, channels), BF16), shape((rows, channels), F32)] + terms_t,
        [
            pltpu.VMEM((taps, channels), BF16),
            pltpu.VMEM((channels, taps), BF16),
            pad,
            pltpu.VMEM((rows, taps), BF16),
            pltpu.VMEM((channels, rows + 2 * cells), BF16),
        ],
        flops=2 * 21 * rows * channels * channels,
        moved=3_000_000,
    )(lat, cot_t, halo, stats, gsa, seen, w_spatial, *pieces_s)
    before = lax.ppermute(spatial, "wide", [(w, w + 1) for w in range(W - 1)])
    block_out = call(
        functools.partial(block_body, sizes),
        shape((rows, channels), BF16),
        [pltpu.VMEM((D * shard_t, channels), BF16)],
        flops=2 * 3 * rows * channels * channels,
        moved=1_000_000,
    )(lat, spatial, before, w_temporal, *pieces_t)

    width = channels // W
    operands = (lat, cot, stats, grad)
    if aligned:
        Z = W // 4

        def over_core(away):
            return send(away, lambda d, w: (d, w ^ 1))

        pairs = []
        for keep, away in (grads_s, grads_t):
            view = (D, Z, 2, width, keep.shape[-1])
            pairs += [keep.reshape(view), over_core(away).reshape(view)]
        plane = call(
            plane_body, [shape((Z, width, R + ride), BF16)] * (2 * D), moved=3_000_000
        )(*pairs)
        parts = [plane[0]] + [
            send(plane[2 * a + b], lambda d, w: ((d + a) % D, w ^ (2 * b)))
            for a, b in ((0, 1), (1, 0), (1, 1))
        ]
        line = call(
            functools.partial(line_body, Z),
            [shape((width, R + ride), BF16)] * Z,
            moved=1_000_000,
        )(*parts)
        terms = [line[0]]
        for s in range(1, Z):
            terms.append(send(line[s], lambda d, w: (d, (w + 4 * s) % W)))
        grad_s, grad_t, norm, grad_latents = call(
            functools.partial(last_body, sizes, scale, Z),
            [
                shape((width, shard_s), F32),
                shape((width, shard_t), F32),
                shape((2, width), F32),
                shape((rows, channels), BF16),
            ],
            moved=1_000_000,
        )(*terms, *operands)
        grad_s, grad_t = grad_s.T, grad_t.T
    else:
        sums = lax.all_to_all(
            grads_t[1], ("dp", "wide"), split_axis=0, concat_axis=0, tiled=True
        )
        norm, grad_latents = call(
            functools.partial(apart_body, sizes, scale),
            [shape((2, width), F32), shape((rows, channels), BF16)],
        )(sums, *operands)
        outs = []
        for full in (grads_s[0], grads_t[0]):
            part = lax.psum_scatter(
                full.astype(F32), "wide", scatter_dimension=0, tiled=True
            ).T.astype(BF16)
            part = lax.psum_scatter(part, "dp", scatter_dimension=0, tiled=True)
            outs.append(part.astype(F32) * scale)
        grad_s, grad_t = outs
    return (
        block_out.reshape(latents.shape),
        grad_latents.reshape(latents.shape),
        grad_s,
        grad_t,
        norm,
    )


def solution(mesh):
    return jax.shard_map(
        local,
        mesh=mesh,
        in_specs=(
            P("dp", "wide", None, None, None),
            P("dp", "wide", None, None, None),
            P(),
            P(),
            P("dp", None),
            P("dp", None),
        ),
        out_specs=(
            P("dp", "wide", None, None, None),
            P("dp", "wide", None, None, None),
            P("dp", "wide"),
            P("dp", "wide"),
            P(None, "wide"),
        ),
        check_vma=False,
    )
```

```python
import functools
import math

import jax
import jax.numpy as jnp
from jax import lax
from jax.experimental import pallas as pl
from jax.experimental.pallas import tpu as pltpu
from jax.sharding import PartitionSpec as P

GROUPS = 32
EPSILON = 1e-05
F32 = jnp.float32
BF16 = jnp.bfloat16
VMEM = pl.BlockSpec(memory_space=pltpu.VMEM)
HBM = pl.BlockSpec(memory_space=pltpu.HBM)
FIRST_VMEM = 60 << 20
NT = (((1,), (1,)), ((), ()))
NN = (((1,), (0,)), ((), ()))


def call(body, out_shapes, scratch=(), flops=0, moved=0, in_specs=None, out_specs=None, vmem=40 << 20):
    many = isinstance(out_shapes, (tuple, list))

    def run(*operands):
        return pl.pallas_call(
            body,
            out_shape=out_shapes,
            in_specs=in_specs or [VMEM] * len(operands),
            out_specs=out_specs or ([VMEM] * len(out_shapes) if many else VMEM),
            scratch_shapes=list(scratch),
            compiler_params=pltpu.CompilerParams(vmem_limit_bytes=vmem),
            cost_estimate=pl.CostEstimate(
                flops=flops, bytes_accessed=moved, transcendentals=0
            ),
        )(*operands)

    return run


def shape(dims, kind):
    return jax.ShapeDtypeStruct(dims, kind)


def mm(left, right, dims=NN):
    return lax.dot_general(left, right, dims, preferred_element_type=F32)


def group_total(rows, per_group):
    channels = rows.shape[-1]
    first = lax.broadcasted_iota(jnp.int32, (channels, channels), 0) // per_group
    second = lax.broadcasted_iota(jnp.int32, (channels, channels), 1) // per_group
    same = (first == second).astype(F32)
    return lax.dot_general(
        rows, same, NN, precision=lax.Precision.HIGHEST, preferred_element_type=F32
    )


def stats_body(lat_ref, gain_ref, bias_ref, ws_ref, wt_ref, out_ref, half_ref, *scratch):
    lat_here, gain_here, bias_here, half_here, sems = scratch
    core = lax.rem(lax.axis_index("wide"), 2)
    moves = [(lat_ref, lat_here), (gain_ref, gain_here), (bias_ref, bias_here)]
    half = ws_ref.shape[0] // 2
    start = pl.multiple_of(core * half, 16)
    moves.append((ws_ref.at[pl.ds(start, half)], half_here.at[pl.ds(0, half)]))
    moves.append((wt_ref, half_here.at[pl.ds(half, wt_ref.shape[0])]))
    copies = [pltpu.make_async_copy(*move, sems.at[at]) for at, move in enumerate(moves)]
    for copy in copies:
        copy.start()
    parts = (pl.ds(0, half), pl.ds(half, wt_ref.shape[0]))
    leaving = [
        pltpu.make_async_copy(half_here.at[part], half_ref.at[part], sems.at[5 + at])
        for at, part in enumerate(parts)
    ]
    for copy, leave in zip(copies[3:], leaving):
        copy.wait()
        leave.start()
    for copy in copies[:3]:
        copy.wait()
    x = lat_here[...].astype(F32)
    sums = [jnp.sum(x, axis=0, keepdims=True), jnp.sum(x * x, axis=0, keepdims=True)]
    both = jnp.concatenate(
        [
            jnp.concatenate([sums[0], gain_here[...]], axis=1),
            jnp.concatenate([sums[1], bias_here[...]], axis=1),
        ],
        axis=0,
    )
    out_ref[...] = jnp.broadcast_to(both[None], out_ref.shape)
    for copy in leaving:
        copy.wait()


def transpose_body(cot_ref, out_ref):
    out_ref[...] = cot_ref[...].astype(F32).T.astype(BF16)


def fill_spatial(full, shard_ref, pieces, D):
    d = lax.axis_index("dp")
    core = lax.rem(lax.axis_index("wide"), 2)
    n = shard_ref.shape[0]
    half = n // 2
    full[pl.ds(pl.multiple_of(d * n, 16), n)] = shard_ref[...]
    for s in range(1, D):
        source = lax.rem(d + D - s, D)
        for which in range(2):
            holder = core if which == 0 else 1 - core
            start = pl.multiple_of(source * n + holder * half, 16)
            full[pl.ds(start, half)] = pieces[2 * (s - 1) + which][0:half]


def fill_temporal(full, shard_ref, firsts, D):
    d = lax.axis_index("dp")
    n = shard_ref.shape[0]
    full[pl.ds(pl.multiple_of(d * n, 16), n)] = shard_ref[...]
    for s in range(1, D):
        start = pl.multiple_of(lax.rem(d + D - s, D) * n, 16)
        full[pl.ds(start, n)] = firsts[s - 1][firsts[s - 1].shape[0] - n :]


def whiten(lat, stats, count, per_group):
    total = group_total(jnp.sum(stats[:, :, : lat.shape[1]], axis=0), per_group) / count
    mean = total[0:1]
    inv_std = 1.0 / jnp.sqrt(total[1:2] - mean * mean + EPSILON)
    return (lat.astype(F32) - mean) * inv_std, inv_std


def store_shifted(pad_ref, values, frames, cells, cols):
    total = frames * cells
    column = lax.broadcasted_iota(jnp.int32, (total, 1), 0) % cols
    left = jnp.where(column == 0, 0.0, pltpu.roll(values, 1, 0))
    right = jnp.where(column == cols - 1, 0.0, pltpu.roll(values, total - 1, 0))
    edge = jnp.zeros((cols, values.shape[1]), BF16)
    for at, form in enumerate((left, values, right)):
        low = form.astype(BF16)
        for f in range(frames):
            pad_ref[at, f, 0:cols] = edge
            pad_ref[at, f, cols : cols + cells] = low[f * cells : (f + 1) * cells]
            pad_ref[at, f, cols + cells :] = edge


def window(pad_ref, dy, dx, frames, cells, cols):
    return jnp.concatenate(
        [pad_ref[dx, f, dy * cols : dy * cols + cells] for f in range(frames)], axis=0
    )


def in_parts(total):
    high = total.astype(BF16).astype(F32)
    return jnp.concatenate([high, total - high], axis=0).astype(BF16)


def from_parts(terms):
    total = 0.0
    for term in terms:
        wide = term.astype(F32)
        total = total + (wide[0:8] + wide[8:16])
    return total


def add(terms):
    total = terms[0].astype(F32)
    for term in terms[1:]:
        total += term.astype(F32)
    return total


def core_order(transposed_ref, W, core):
    step = transposed_ref.shape[0] // W
    order = [(2 * j + core) * step for j in range(W // 2)]
    order += [(2 * j + 1 - core) * step for j in range(W // 2)]
    return jnp.concatenate(
        [transposed_ref[pl.ds(pl.multiple_of(at, 16), step)] for at in order], axis=0
    )


def put(block, column, shard, keep_ref, send_ref):
    low = block.astype(BF16)
    if send_ref is None:
        keep_ref[:, column : column + block.shape[1]] = low
        return
    half = block.shape[0] // 2
    for at in range(0, block.shape[1], 128):
        owner, place = (column + at) // shard, (column + at) % shard
        keep_ref[owner, :, place : place + 128] = low[:half, at : at + 128]
        send_ref[owner, :, place : place + 128] = low[half:, at : at + 128]


def affine_of(stats_ref):
    return stats_ref[0, :, stats_ref.shape[2] // 2 :]


def normalise(lat_ref, stats_ref, count, per_group):
    white, inv_std = whiten(lat_ref[...], stats_ref[...], count, per_group)
    affine = affine_of(stats_ref)
    normed = white * affine[0:1] + affine[1:2]
    return white, normed, jax.nn.sigmoid(normed)


def first_body(sizes, lat_ref, cot_ref, halo_ref, stats_ref, wt_ref, *rest):
    D, W, frames, cells, cols, count, per_group, aligned = sizes
    firsts, rest = rest[: D - 1], rest[D - 1 :]
    full_wt, act_pad, gsa_t = rest[-3:]
    gsa_ref, seen_ref, keep_ref = rest[:3]
    send_ref = rest[3] if aligned else None
    channels = lat_ref.shape[1]
    core = lax.rem(lax.axis_index("wide"), 2)
    fill_temporal(full_wt, wt_ref, firsts, D)
    rows = frames * cells
    extended = jnp.concatenate([cot_ref[...], halo_ref[...]], axis=0)
    gsa = jnp.zeros((rows, channels), F32)
    for k in range(3):
        gsa += mm(
            extended[k * cells : k * cells + rows],
            full_wt[k * channels : (k + 1) * channels],
            NT,
        )
    gsa_ref[...] = gsa.astype(BF16)
    gsa_t[...] = gsa.astype(BF16).astype(F32).T.astype(BF16)
    _, normed, sig = normalise(lat_ref, stats_ref, count, per_group)
    act = (normed * sig).astype(BF16).astype(F32)
    store_shifted(act_pad, act, frames, cells, cols)
    left = core_order(gsa_t, W, core) if aligned else gsa_t[...]
    shard = wt_ref.shape[0] * 3
    for dy in range(3):
        for dx in range(3):
            at = (3 * dy + dx) * channels
            seen = window(act_pad, dy, dx, frames, cells, cols)
            seen_ref[:, at : at + channels] = seen
            put(mm(left, seen), at, shard, keep_ref, send_ref)


def second_body(
    sizes, lat_ref, cot_t_ref, halo_ref, stats_ref, gsa_ref, seen_ref, ws_ref, *rest
):
    D, W, frames, cells, cols, count, per_group, aligned = sizes
    pieces, rest = rest[: 2 * (D - 1)], rest[2 * (D - 1) :]
    full_ws, side_ws, gsa_pad, gsa_seen, cot_t = rest[-5:]
    spatial_ref, grad_ref, keep_ref, other_ref = rest[:4]
    send_ref = other_ref if aligned else None
    channels = lat_ref.shape[1]
    core = lax.rem(lax.axis_index("wide"), 2)
    fill_spatial(full_ws, ws_ref, pieces, D)
    rows = frames * cells
    white, normed, sig = normalise(lat_ref, stats_ref, count, per_group)
    store_shifted(gsa_pad, gsa_ref[...].astype(F32), frames, cells, cols)
    cot_t[:, :rows] = cot_t_ref[...]
    for f in range(2):
        cot_t[:, rows + f * cells : rows + (f + 1) * cells] = (
            halo_ref[f * cells : (f + 1) * cells].astype(F32).T.astype(BF16)
        )
    left = core_order(cot_t, W, core) if aligned else cot_t[...]
    spatial = mm(seen_ref[...], full_ws[...]).astype(BF16)
    spatial_ref[...] = spatial
    shard = ws_ref.shape[0] // 3
    for k in range(3):
        block = mm(left[:, k * cells : k * cells + rows], spatial)
        put(block, k * channels, shard, keep_ref, send_ref)

    for dy in range(3):
        for dx in range(3):
            at = (3 * dy + dx) * channels
            gsa_seen[:, at : at + channels] = window(
                gsa_pad, 2 - dy, 2 - dx, frames, cells, cols
            )
            side_ws[:, at : at + channels] = full_ws[at : at + channels]
    grad = mm(gsa_seen[...], side_ws[...], NT)
    grad = grad * (sig * (1.0 + normed * (1.0 - sig)))
    grad_ref[...] = grad
    gain_term = jnp.sum(grad * white, axis=0, keepdims=True)
    bias_term = jnp.sum(grad, axis=0, keepdims=True)
    if not aligned:
        both = jnp.concatenate([gain_term, bias_term], axis=0)
        other_ref[...] = jnp.broadcast_to(both[None], other_ref.shape)
        return
    d = lax.axis_index("dp")
    quarter = jnp.concatenate(
        [term[:, at : at + 128] for term in (gain_term, bias_term) for at in (0, 128)], axis=0
    )
    low = in_parts(
        jnp.concatenate([jnp.where(d == s, quarter, 0.0) for s in range(2)], axis=0)
    )
    for target in (keep_ref, send_ref):
        for owner in range(D):
            for at in range(0, channels // 2, 16):
                target[owner, at : at + 16, shard:] = low


def block_body(sizes, lat_ref, spatial_ref, before_ref, wt_ref, *rest):
    D, W, frames, cells, cols, count, per_group, aligned = sizes
    firsts = rest[: D - 1]
    block_ref, full_wt = rest[D - 1 :]
    channels = lat_ref.shape[1]
    fill_temporal(full_wt, wt_ref, firsts, D)
    extended = jnp.concatenate([before_ref[...], spatial_ref[...]], axis=0)
    rows = frames * cells
    temporal = jnp.zeros((rows, channels), F32)
    for k in range(3):
        start = (2 - k) * cells
        temporal += mm(
            extended[start : start + rows], full_wt[k * channels : (k + 1) * channels]
        )
    block_ref[...] = (lat_ref[...].astype(F32) + temporal).astype(BF16)


def latent_gradient(sizes, total, lat_ref, cot_ref, stats_ref, grad_ref):
    D, W, frames, cells, cols, count, per_group, aligned = sizes
    white, inv_std = whiten(lat_ref[...], stats_ref[...], count, per_group)
    gain = affine_of(stats_ref)[0:1]
    means = group_total(total * gain, per_group) / count
    inner = inv_std * (grad_ref[...] * gain - means[1:2] - white * means[0:1])
    return (cot_ref[...].astype(F32) + inner).astype(BF16)


def plane_body(keep_s, got_s, keep_t, got_t, *outs):
    d = lax.axis_index("dp")
    y = lax.rem(lax.axis_index("wide") // 2, 2)
    split = keep_s.shape[-1]
    ride = outs[0].shape[-1] - 128
    for a in range(2):
        for b in range(2):
            owner, side = lax.rem(d + a, 2), lax.rem(y + b, 2)
            out = outs[2 * a + b]
            for z in range(out.shape[0]):
                out[z, :, :split] = add([keep_s[owner, z, side], got_s[owner, z, side]]).astype(
                    BF16
                )
                both = [keep_t[owner, z, side], got_t[owner, z, side]]
                out[z, :, split:ride] = add([t[:, : ride - split] for t in both]).astype(BF16)
                out[z, :, ride:] = in_parts(from_parts([t[:, ride - split :] for t in both]))


def line_body(depth, *refs):
    terms, outs = refs[:4], refs[4:]
    z = lax.axis_index("wide") // 4
    ride = outs[0].shape[-1] - 128
    for s in range(depth):
        owner = lax.rem(z + s, depth)
        seen = [term[owner] for term in terms]
        outs[s][:, :ride] = add([t[:, :ride] for t in seen]).astype(BF16)
        outs[s][:, ride:] = in_parts(from_parts([t[:, ride:] for t in seen]))


def last_body(sizes, scale, depth, *refs):
    terms, operands, outs = refs[:depth], refs[depth:-4], refs[-4:]
    spatial_ref, temporal_ref, norm_ref, glat_ref = outs
    split = spatial_ref.shape[1]
    ride = terms[0].shape[1] - 128
    sums = from_parts([term[:, ride:] for term in terms])

    def rows_of(part):
        return jnp.concatenate(
            [jnp.concatenate([part[at : at + 1], part[at + 1 : at + 2]], axis=1) for at in (0, 2)],
            axis=0,
        )

    first, second = rows_of(sums[0:4]), rows_of(sums[4:8])
    own = jnp.where(lax.axis_index("dp") == 0, first, second)
    glat_ref[...] = latent_gradient(sizes, own, *operands)
    norm_columns(scale, first + second, norm_ref)
    total = add([term[:, :ride] for term in terms]) * scale
    spatial_ref[...] = total[:, :split]
    temporal_ref[...] = total[:, split:]


def apart_body(sizes, scale, sums_ref, *refs):
    norm_ref, glat_ref = refs[-2:]
    W = sizes[1]
    own = jnp.sum(sums_ref[pl.ds(lax.axis_index("dp") * W, W)], axis=0)
    norm_columns(scale, jnp.sum(sums_ref[...], axis=0), norm_ref)
    glat_ref[...] = latent_gradient(sizes, own, *refs[:-2])


def norm_columns(scale, norm, norm_ref):
    channels, width = norm.shape[1], norm_ref.shape[1]
    row = lax.broadcasted_iota(jnp.int32, (channels, width), 0)
    column = lax.broadcasted_iota(jnp.int32, (channels, width), 1)
    pick = (row == column + lax.axis_index("wide") * width).astype(F32)
    norm_ref[...] = (
        lax.dot_general(
            norm, pick, NN, precision=lax.Precision.HIGHEST, preferred_element_type=F32
        )
        * scale
    )


def local(latents, cotangent, norm_gain, norm_bias, w_spatial, w_temporal):
    D, W = lax.axis_size("dp"), lax.axis_size("wide")
    _, frames, rows_here, cols, channels = latents.shape
    cells = rows_here * cols
    rows = frames * cells
    per_group = channels // GROUPS
    count = W * frames * cells * per_group
    shard_s, shard_t = w_spatial.shape[0], w_temporal.shape[0]
    aligned = (channels // W) % 16 == 0 and shard_s % 128 == 0 and shard_t % 128 == 0
    aligned = aligned and W % 4 == 0 and D == 2 and channels == 256
    sizes = (D, W, frames, cells, cols, count, per_group, aligned)
    scale = 1.0 / math.sqrt(D * W * frames * cells)

    lat, cot = latents.reshape(rows, channels), cotangent.reshape(rows, channels)
    gain, bias = norm_gain.reshape(1, channels), norm_bias.reshape(1, channels)

    def over_all(moves):
        pairs = []
        for d in range(D):
            for w in range(W):
                to = moves(d, w)
                pairs.append((d * W + w, to[0] * W + to[1]))
        return pairs

    def send(value, moves):
        return lax.ppermute(value, ("dp", "wide"), over_all(moves))

    R = shard_s + shard_t
    stats, half = call(
        stats_body,
        [
            shape((W, 2, 2 * channels), F32),
            shape((shard_s // 2 + shard_t, channels), BF16),
        ],
        [
            pltpu.VMEM((rows, channels), BF16),
            pltpu.VMEM((1, channels), F32),
            pltpu.VMEM((1, channels), F32),
            pltpu.VMEM((shard_s // 2 + shard_t, channels), BF16),
            pltpu.SemaphoreType.DMA((7,)),
        ],
        in_specs=[HBM] * 5,
        out_specs=[VMEM, HBM],
        vmem=FIRST_VMEM,
    )(lat, gain, bias, w_spatial, w_temporal)
    cot_t = call(transpose_body, shape((channels, rows), BF16), moved=300_000)(cot)
    firsts = [send(half, lambda d, w: ((d + s) % D, w)) for s in range(1, D)]

    halo = lax.ppermute(cot, "wide", [(w + 1, w) for w in range(W - 1)])
    stats = lax.all_to_all(stats, "wide", split_axis=0, concat_axis=0, tiled=True)
    firsts, stats, halo, cot_t = lax.optimization_barrier((firsts, stats, halo, cot_t))
    pieces = []
    for first in firsts:
        pieces += [first, send(first, lambda d, w: (d, w ^ 1))]

    ride = 128 if aligned else 0
    if aligned:
        terms_s = [shape((D, channels // 2, shard_s), BF16)] * 2
        terms_t = [shape((D, channels // 2, shard_t + ride), BF16)] * 2
    else:
        terms_s = [shape((channels, D * shard_s), BF16)]
        terms_t = [shape((channels, D * shard_t), BF16), shape((D * W, 2, channels), F32)]
    pad = pltpu.VMEM((3, frames, cells + 2 * cols, channels), BF16)
    taps = D * shard_s
    gsa, seen, *grads_s = call(
        functools.partial(first_body, sizes),
        [shape((rows, channels), BF16), shape((rows, taps), BF16)] + terms_s,
        [pltpu.VMEM((D * shard_t, channels), BF16), pad, pltpu.VMEM((channels, rows), BF16)],
        flops=2 * 12 * rows * channels * channels,
        moved=3_000_000,
    )(lat, cot, halo, stats, w_temporal, *firsts)
    spatial, grad, *grads_t = call(
        functools.partial(second_body, sizes),
        [shape((rows, channels), BF16), shape((rows, channels), F32)] + terms_t,
        [
            pltpu.VMEM((taps, channels), BF16),
            pltpu.VMEM((channels, taps), BF16),
            pad,
            pltpu.VMEM((rows, taps), BF16),
            pltpu.VMEM((channels, rows + 2 * cells), BF16),
        ],
        flops=2 * 21 * rows * channels * channels,
        moved=3_000_000,
    )(lat, cot_t, halo, stats, gsa, seen, w_spatial, *pieces)
    before = lax.ppermute(spatial, "wide", [(w, w + 1) for w in range(W - 1)])
    block_out = call(
        functools.partial(block_body, sizes),
        shape((rows, channels), BF16),
        [pltpu.VMEM((D * shard_t, channels), BF16)],
        flops=2 * 3 * rows * channels * channels,
        moved=1_000_000,
    )(lat, spatial, before, w_temporal, *firsts)

    width = channels // W
    operands = (lat, cot, stats, grad)
    if aligned:
        Z = W // 4

        def over_core(away):
            return send(away, lambda d, w: (d, w ^ 1))

        pairs = []
        for keep, away in (grads_s, grads_t):
            view = (D, Z, 2, width, keep.shape[-1])
            pairs += [keep.reshape(view), over_core(away).reshape(view)]
        plane = call(
            plane_body, [shape((Z, width, R + ride), BF16)] * (2 * D), moved=3_000_000
        )(*pairs)
        parts = [plane[0]] + [
            send(plane[2 * a + b], lambda d, w: ((d + a) % D, w ^ (2 * b)))
            for a, b in ((0, 1), (1, 0), (1, 1))
        ]
        line = call(
            functools.partial(line_body, Z),
            [shape((width, R + ride), BF16)] * Z,
            moved=1_000_000,
        )(*parts)
        terms = [line[0]]
        for s in range(1, Z):
            terms.append(send(line[s], lambda d, w: (d, (w + 4 * s) % W)))
        grad_s, grad_t, norm, grad_latents = call(
            functools.partial(last_body, sizes, scale, Z),
            [
                shape((width, shard_s), F32),
                shape((width, shard_t), F32),
                shape((2, width), F32),
                shape((rows, channels), BF16),
            ],
            moved=1_000_000,
        )(*terms, *operands)
        grad_s, grad_t = grad_s.T, grad_t.T
    else:
        sums = lax.all_to_all(
            grads_t[1], ("dp", "wide"), split_axis=0, concat_axis=0, tiled=True
        )
        norm, grad_latents = call(
            functools.partial(apart_body, sizes, scale),
            [shape((2, width), F32), shape((rows, channels), BF16)],
        )(sums, *operands)
        outs = []
        for full in (grads_s[0], grads_t[0]):
            part = lax.psum_scatter(
                full.astype(F32), "wide", scatter_dimension=0, tiled=True
            ).T.astype(BF16)
            part = lax.psum_scatter(part, "dp", scatter_dimension=0, tiled=True)
            outs.append(part.astype(F32) * scale)
        grad_s, grad_t = outs
    return (
        block_out.reshape(latents.shape),
        grad_latents.reshape(latents.shape),
        grad_s,
        grad_t,
        norm,
    )


def solution(mesh):
    return jax.shard_map(
        local,
        mesh=mesh,
        in_specs=(
            P("dp", "wide", None, None, None),
            P("dp", "wide", None, None, None),
            P(),
            P(),
            P("dp", None),
            P("dp", None),
        ),
        out_specs=(
            P("dp", "wide", None, None, None),
            P("dp", "wide", None, None, None),
            P("dp", "wide"),
            P("dp", "wide"),
            P(None, "wide"),
        ),
        check_vma=False,
    )
```

```python
import functools
import math

import jax
import jax.numpy as jnp
from jax import lax
from jax.experimental import pallas as pl
from jax.experimental.pallas import tpu as pltpu
from jax.sharding import PartitionSpec as P

GROUPS = 32
EPSILON = 1e-05
F32 = jnp.float32
BF16 = jnp.bfloat16
VMEM = pl.BlockSpec(memory_space=pltpu.VMEM)
HBM = pl.BlockSpec(memory_space=pltpu.HBM)
FIRST_VMEM = 60 << 20
NT = (((1,), (1,)), ((), ()))
NN = (((1,), (0,)), ((), ()))


def call(body, out_shapes, scratch=(), flops=0, moved=0, in_specs=None, vmem=40 << 20):
    many = isinstance(out_shapes, (tuple, list))

    def run(*operands):
        return pl.pallas_call(
            body,
            out_shape=out_shapes,
            in_specs=in_specs or [VMEM] * len(operands),
            out_specs=[VMEM] * len(out_shapes) if many else VMEM,
            scratch_shapes=list(scratch),
            compiler_params=pltpu.CompilerParams(vmem_limit_bytes=vmem),
            cost_estimate=pl.CostEstimate(
                flops=flops, bytes_accessed=moved, transcendentals=0
            ),
        )(*operands)

    return run


def shape(dims, kind):
    return jax.ShapeDtypeStruct(dims, kind)


def mm(left, right, dims=NN):
    return lax.dot_general(left, right, dims, preferred_element_type=F32)


def group_total(rows, per_group):
    channels = rows.shape[-1]
    first = lax.broadcasted_iota(jnp.int32, (channels, channels), 0) // per_group
    second = lax.broadcasted_iota(jnp.int32, (channels, channels), 1) // per_group
    same = (first == second).astype(F32)
    return lax.dot_general(
        rows, same, NN, precision=lax.Precision.HIGHEST, preferred_element_type=F32
    )


def stats_body(lat_ref, gain_ref, bias_ref, ws_ref, wt_ref, out_ref, half_ref, *scratch):
    lat_here, gain_here, bias_here, sems = scratch
    core = lax.rem(lax.axis_index("wide"), 2)
    moves = [(lat_ref, lat_here), (gain_ref, gain_here), (bias_ref, bias_here)]
    half = ws_ref.shape[0] // 2
    start = pl.multiple_of(core * half, 16)
    moves.append((ws_ref.at[pl.ds(start, half)], half_ref.at[pl.ds(0, half)]))
    moves.append((wt_ref, half_ref.at[pl.ds(half, wt_ref.shape[0])]))
    copies = [pltpu.make_async_copy(*move, sems.at[at]) for at, move in enumerate(moves)]
    for copy in copies:
        copy.start()
    for copy in copies[:3]:
        copy.wait()
    x = lat_here[...].astype(F32)
    sums = [jnp.sum(x, axis=0, keepdims=True), jnp.sum(x * x, axis=0, keepdims=True)]
    both = jnp.concatenate(
        [
            jnp.concatenate([sums[0], gain_here[...]], axis=1),
            jnp.concatenate([sums[1], bias_here[...]], axis=1),
        ],
        axis=0,
    )
    out_ref[...] = jnp.broadcast_to(both[None], out_ref.shape)
    for copy in copies[3:]:
        copy.wait()


def transpose_body(cot_ref, out_ref):
    out_ref[...] = cot_ref[...].astype(F32).T.astype(BF16)


def fill_spatial(full, shard_ref, pieces, D):
    d = lax.axis_index("dp")
    core = lax.rem(lax.axis_index("wide"), 2)
    n = shard_ref.shape[0]
    half = n // 2
    full[pl.ds(pl.multiple_of(d * n, 16), n)] = shard_ref[...]
    for s in range(1, D):
        source = lax.rem(d + D - s, D)
        for which in range(2):
            holder = core if which == 0 else 1 - core
            start = pl.multiple_of(source * n + holder * half, 16)
            full[pl.ds(start, half)] = pieces[2 * (s - 1) + which][0:half]


def fill_temporal(full, shard_ref, firsts, D):
    d = lax.axis_index("dp")
    n = shard_ref.shape[0]
    full[pl.ds(pl.multiple_of(d * n, 16), n)] = shard_ref[...]
    for s in range(1, D):
        start = pl.multiple_of(lax.rem(d + D - s, D) * n, 16)
        full[pl.ds(start, n)] = firsts[s - 1][firsts[s - 1].shape[0] - n :]


def whiten(lat, stats, count, per_group):
    total = group_total(jnp.sum(stats[:, :, : lat.shape[1]], axis=0), per_group) / count
    mean = total[0:1]
    inv_std = 1.0 / jnp.sqrt(total[1:2] - mean * mean + EPSILON)
    return (lat.astype(F32) - mean) * inv_std, inv_std


def store_shifted(pad_ref, values, frames, cells, cols):
    total = frames * cells
    column = lax.broadcasted_iota(jnp.int32, (total, 1), 0) % cols
    left = jnp.where(column == 0, 0.0, pltpu.roll(values, 1, 0))
    right = jnp.where(column == cols - 1, 0.0, pltpu.roll(values, total - 1, 0))
    edge = jnp.zeros((cols, values.shape[1]), BF16)
    for at, form in enumerate((left, values, right)):
        low = form.astype(BF16)
        for f in range(frames):
            pad_ref[at, f, 0:cols] = edge
            pad_ref[at, f, cols : cols + cells] = low[f * cells : (f + 1) * cells]
            pad_ref[at, f, cols + cells :] = edge


def window(pad_ref, dy, dx, frames, cells, cols):
    return jnp.concatenate(
        [pad_ref[dx, f, dy * cols : dy * cols + cells] for f in range(frames)], axis=0
    )


def in_parts(total):
    high = total.astype(BF16).astype(F32)
    return jnp.concatenate([high, total - high], axis=0).astype(BF16)


def from_parts(terms):
    total = 0.0
    for term in terms:
        wide = term.astype(F32)
        total = total + (wide[0:8] + wide[8:16])
    return total


def add(terms):
    total = terms[0].astype(F32)
    for term in terms[1:]:
        total += term.astype(F32)
    return total


def core_order(transposed_ref, W, core):
    step = transposed_ref.shape[0] // W
    order = [(2 * j + core) * step for j in range(W // 2)]
    order += [(2 * j + 1 - core) * step for j in range(W // 2)]
    return jnp.concatenate(
        [transposed_ref[pl.ds(pl.multiple_of(at, 16), step)] for at in order], axis=0
    )


def put(block, column, shard, keep_ref, send_ref):
    low = block.astype(BF16)
    if send_ref is None:
        keep_ref[:, column : column + block.shape[1]] = low
        return
    half = block.shape[0] // 2
    for at in range(0, block.shape[1], 128):
        owner, place = (column + at) // shard, (column + at) % shard
        keep_ref[owner, :, place : place + 128] = low[:half, at : at + 128]
        send_ref[owner, :, place : place + 128] = low[half:, at : at + 128]


def affine_of(stats_ref):
    return stats_ref[0, :, stats_ref.shape[2] // 2 :]


def normalise(lat_ref, stats_ref, count, per_group):
    white, inv_std = whiten(lat_ref[...], stats_ref[...], count, per_group)
    affine = affine_of(stats_ref)
    normed = white * affine[0:1] + affine[1:2]
    return white, normed, jax.nn.sigmoid(normed)


def first_body(sizes, lat_ref, cot_ref, halo_ref, stats_ref, wt_ref, *rest):
    D, W, frames, cells, cols, count, per_group, aligned = sizes
    firsts, rest = rest[: D - 1], rest[D - 1 :]
    full_wt, act_pad, gsa_t = rest[-3:]
    gsa_ref, seen_ref, keep_ref = rest[:3]
    send_ref = rest[3] if aligned else None
    channels = lat_ref.shape[1]
    core = lax.rem(lax.axis_index("wide"), 2)
    fill_temporal(full_wt, wt_ref, firsts, D)
    rows = frames * cells
    extended = jnp.concatenate([cot_ref[...], halo_ref[...]], axis=0)
    gsa = jnp.zeros((rows, channels), F32)
    for k in range(3):
        gsa += mm(
            extended[k * cells : k * cells + rows],
            full_wt[k * channels : (k + 1) * channels],
            NT,
        )
    gsa_ref[...] = gsa.astype(BF16)
    gsa_t[...] = gsa.astype(BF16).astype(F32).T.astype(BF16)
    _, normed, sig = normalise(lat_ref, stats_ref, count, per_group)
    act = (normed * sig).astype(BF16).astype(F32)
    store_shifted(act_pad, act, frames, cells, cols)
    left = core_order(gsa_t, W, core) if aligned else gsa_t[...]
    shard = wt_ref.shape[0] * 3
    for dy in range(3):
        for dx in range(3):
            at = (3 * dy + dx) * channels
            seen = window(act_pad, dy, dx, frames, cells, cols)
            seen_ref[:, at : at + channels] = seen
            put(mm(left, seen), at, shard, keep_ref, send_ref)


def second_body(
    sizes, lat_ref, cot_t_ref, halo_ref, stats_ref, gsa_ref, seen_ref, ws_ref, *rest
):
    D, W, frames, cells, cols, count, per_group, aligned = sizes
    pieces, rest = rest[: 2 * (D - 1)], rest[2 * (D - 1) :]
    full_ws, side_ws, gsa_pad, gsa_seen, cot_t = rest[-5:]
    spatial_ref, grad_ref, keep_ref, other_ref = rest[:4]
    send_ref = other_ref if aligned else None
    channels = lat_ref.shape[1]
    core = lax.rem(lax.axis_index("wide"), 2)
    fill_spatial(full_ws, ws_ref, pieces, D)
    rows = frames * cells
    white, normed, sig = normalise(lat_ref, stats_ref, count, per_group)
    store_shifted(gsa_pad, gsa_ref[...].astype(F32), frames, cells, cols)
    cot_t[:, :rows] = cot_t_ref[...]
    for f in range(2):
        cot_t[:, rows + f * cells : rows + (f + 1) * cells] = (
            halo_ref[f * cells : (f + 1) * cells].astype(F32).T.astype(BF16)
        )
    left = core_order(cot_t, W, core) if aligned else cot_t[...]
    spatial = mm(seen_ref[...], full_ws[...]).astype(BF16)
    spatial_ref[...] = spatial
    shard = ws_ref.shape[0] // 3
    for k in range(3):
        block = mm(left[:, k * cells : k * cells + rows], spatial)
        put(block, k * channels, shard, keep_ref, send_ref)

    for dy in range(3):
        for dx in range(3):
            at = (3 * dy + dx) * channels
            gsa_seen[:, at : at + channels] = window(
                gsa_pad, 2 - dy, 2 - dx, frames, cells, cols
            )
            side_ws[:, at : at + channels] = full_ws[at : at + channels]
    grad = mm(gsa_seen[...], side_ws[...], NT)
    grad = grad * (sig * (1.0 + normed * (1.0 - sig)))
    grad_ref[...] = grad
    gain_term = jnp.sum(grad * white, axis=0, keepdims=True)
    bias_term = jnp.sum(grad, axis=0, keepdims=True)
    if not aligned:
        both = jnp.concatenate([gain_term, bias_term], axis=0)
        other_ref[...] = jnp.broadcast_to(both[None], other_ref.shape)
        return
    d = lax.axis_index("dp")
    quarter = jnp.concatenate(
        [term[:, at : at + 128] for term in (gain_term, bias_term) for at in (0, 128)], axis=0
    )
    low = in_parts(
        jnp.concatenate([jnp.where(d == s, quarter, 0.0) for s in range(2)], axis=0)
    )
    for target in (keep_ref, send_ref):
        for owner in range(D):
            for at in range(0, channels // 2, 16):
                target[owner, at : at + 16, shard:] = low


def block_body(sizes, lat_ref, spatial_ref, before_ref, wt_ref, *rest):
    D, W, frames, cells, cols, count, per_group, aligned = sizes
    firsts = rest[: D - 1]
    block_ref, full_wt = rest[D - 1 :]
    channels = lat_ref.shape[1]
    fill_temporal(full_wt, wt_ref, firsts, D)
    extended = jnp.concatenate([before_ref[...], spatial_ref[...]], axis=0)
    rows = frames * cells
    temporal = jnp.zeros((rows, channels), F32)
    for k in range(3):
        start = (2 - k) * cells
        temporal += mm(
            extended[start : start + rows], full_wt[k * channels : (k + 1) * channels]
        )
    block_ref[...] = (lat_ref[...].astype(F32) + temporal).astype(BF16)


def latent_gradient(sizes, total, lat_ref, cot_ref, stats_ref, grad_ref):
    D, W, frames, cells, cols, count, per_group, aligned = sizes
    white, inv_std = whiten(lat_ref[...], stats_ref[...], count, per_group)
    gain = affine_of(stats_ref)[0:1]
    means = group_total(total * gain, per_group) / count
    inner = inv_std * (grad_ref[...] * gain - means[1:2] - white * means[0:1])
    return (cot_ref[...].astype(F32) + inner).astype(BF16)


def plane_body(keep_s, got_s, keep_t, got_t, *outs):
    d = lax.axis_index("dp")
    y = lax.rem(lax.axis_index("wide") // 2, 2)
    split = keep_s.shape[-1]
    ride = outs[0].shape[-1] - 128
    for a in range(2):
        for b in range(2):
            owner, side = lax.rem(d + a, 2), lax.rem(y + b, 2)
            out = outs[2 * a + b]
            for z in range(out.shape[0]):
                out[z, :, :split] = add([keep_s[owner, z, side], got_s[owner, z, side]]).astype(
                    BF16
                )
                both = [keep_t[owner, z, side], got_t[owner, z, side]]
                out[z, :, split:ride] = add([t[:, : ride - split] for t in both]).astype(BF16)
                out[z, :, ride:] = in_parts(from_parts([t[:, ride - split :] for t in both]))


def line_body(depth, *refs):
    terms, outs = refs[:4], refs[4:]
    z = lax.axis_index("wide") // 4
    ride = outs[0].shape[-1] - 128
    for s in range(depth):
        owner = lax.rem(z + s, depth)
        seen = [term[owner] for term in terms]
        outs[s][:, :ride] = add([t[:, :ride] for t in seen]).astype(BF16)
        outs[s][:, ride:] = in_parts(from_parts([t[:, ride:] for t in seen]))


def last_body(sizes, scale, depth, *refs):
    terms, operands, outs = refs[:depth], refs[depth:-4], refs[-4:]
    spatial_ref, temporal_ref, norm_ref, glat_ref = outs
    split = spatial_ref.shape[1]
    ride = terms[0].shape[1] - 128
    sums = from_parts([term[:, ride:] for term in terms])

    def rows_of(part):
        return jnp.concatenate(
            [jnp.concatenate([part[at : at + 1], part[at + 1 : at + 2]], axis=1) for at in (0, 2)],
            axis=0,
        )

    first, second = rows_of(sums[0:4]), rows_of(sums[4:8])
    own = jnp.where(lax.axis_index("dp") == 0, first, second)
    glat_ref[...] = latent_gradient(sizes, own, *operands)
    norm_columns(scale, first + second, norm_ref)
    total = add([term[:, :ride] for term in terms]) * scale
    spatial_ref[...] = total[:, :split]
    temporal_ref[...] = total[:, split:]


def apart_body(sizes, scale, sums_ref, *refs):
    norm_ref, glat_ref = refs[-2:]
    W = sizes[1]
    own = jnp.sum(sums_ref[pl.ds(lax.axis_index("dp") * W, W)], axis=0)
    norm_columns(scale, jnp.sum(sums_ref[...], axis=0), norm_ref)
    glat_ref[...] = latent_gradient(sizes, own, *refs[:-2])


def norm_columns(scale, norm, norm_ref):
    channels, width = norm.shape[1], norm_ref.shape[1]
    row = lax.broadcasted_iota(jnp.int32, (channels, width), 0)
    column = lax.broadcasted_iota(jnp.int32, (channels, width), 1)
    pick = (row == column + lax.axis_index("wide") * width).astype(F32)
    norm_ref[...] = (
        lax.dot_general(
            norm, pick, NN, precision=lax.Precision.HIGHEST, preferred_element_type=F32
        )
        * scale
    )


def local(latents, cotangent, norm_gain, norm_bias, w_spatial, w_temporal):
    D, W = lax.axis_size("dp"), lax.axis_size("wide")
    _, frames, rows_here, cols, channels = latents.shape
    cells = rows_here * cols
    rows = frames * cells
    per_group = channels // GROUPS
    count = W * frames * cells * per_group
    shard_s, shard_t = w_spatial.shape[0], w_temporal.shape[0]
    aligned = (channels // W) % 16 == 0 and shard_s % 128 == 0 and shard_t % 128 == 0
    aligned = aligned and W % 4 == 0 and D == 2 and channels == 256
    sizes = (D, W, frames, cells, cols, count, per_group, aligned)
    scale = 1.0 / math.sqrt(D * W * frames * cells)

    lat, cot = latents.reshape(rows, channels), cotangent.reshape(rows, channels)
    gain, bias = norm_gain.reshape(1, channels), norm_bias.reshape(1, channels)

    def over_all(moves):
        pairs = []
        for d in range(D):
            for w in range(W):
                to = moves(d, w)
                pairs.append((d * W + w, to[0] * W + to[1]))
        return pairs

    def send(value, moves):
        return lax.ppermute(value, ("dp", "wide"), over_all(moves))

    R = shard_s + shard_t
    stats, half = call(
        stats_body,
        [
            shape((W, 2, 2 * channels), F32),
            shape((shard_s // 2 + shard_t, channels), BF16),
        ],
        [
            pltpu.VMEM((rows, channels), BF16),
            pltpu.VMEM((1, channels), F32),
            pltpu.VMEM((1, channels), F32),
            pltpu.SemaphoreType.DMA((5,)),
        ],
        in_specs=[HBM] * 5,
        vmem=FIRST_VMEM,
    )(lat, gain, bias, w_spatial, w_temporal)
    cot_t = call(transpose_body, shape((channels, rows), BF16), moved=300_000)(cot)
    firsts = [send(half, lambda d, w: ((d + s) % D, w)) for s in range(1, D)]

    halo = lax.ppermute(cot, "wide", [(w + 1, w) for w in range(W - 1)])
    stats = lax.all_to_all(stats, "wide", split_axis=0, concat_axis=0, tiled=True)
    firsts, stats, halo, cot_t = lax.optimization_barrier((firsts, stats, halo, cot_t))
    pieces = []
    for first in firsts:
        pieces += [first, send(first, lambda d, w: (d, w ^ 1))]

    ride = 128 if aligned else 0
    if aligned:
        terms_s = [shape((D, channels // 2, shard_s), BF16)] * 2
        terms_t = [shape((D, channels // 2, shard_t + ride), BF16)] * 2
    else:
        terms_s = [shape((channels, D * shard_s), BF16)]
        terms_t = [shape((channels, D * shard_t), BF16), shape((D * W, 2, channels), F32)]
    pad = pltpu.VMEM((3, frames, cells + 2 * cols, channels), BF16)
    taps = D * shard_s
    gsa, seen, *grads_s = call(
        functools.partial(first_body, sizes),
        [shape((rows, channels), BF16), shape((rows, taps), BF16)] + terms_s,
        [pltpu.VMEM((D * shard_t, channels), BF16), pad, pltpu.VMEM((channels, rows), BF16)],
        flops=2 * 12 * rows * channels * channels,
        moved=3_000_000,
    )(lat, cot, halo, stats, w_temporal, *firsts)
    spatial, grad, *grads_t = call(
        functools.partial(second_body, sizes),
        [shape((rows, channels), BF16), shape((rows, channels), F32)] + terms_t,
        [
            pltpu.VMEM((taps, channels), BF16),
            pltpu.VMEM((channels, taps), BF16),
            pad,
            pltpu.VMEM((rows, taps), BF16),
            pltpu.VMEM((channels, rows + 2 * cells), BF16),
        ],
        flops=2 * 21 * rows * channels * channels,
        moved=3_000_000,
    )(lat, cot_t, halo, stats, gsa, seen, w_spatial, *pieces)
    before = lax.ppermute(spatial, "wide", [(w, w + 1) for w in range(W - 1)])
    block_out = call(
        functools.partial(block_body, sizes),
        shape((rows, channels), BF16),
        [pltpu.VMEM((D * shard_t, channels), BF16)],
        flops=2 * 3 * rows * channels * channels,
        moved=1_000_000,
    )(lat, spatial, before, w_temporal, *firsts)

    width = channels // W
    operands = (lat, cot, stats, grad)
    if aligned:
        Z = W // 4

        def over_core(away):
            return send(away, lambda d, w: (d, w ^ 1))

        pairs = []
        for keep, away in (grads_s, grads_t):
            view = (D, Z, 2, width, keep.shape[-1])
            pairs += [keep.reshape(view), over_core(away).reshape(view)]
        plane = call(
            plane_body, [shape((Z, width, R + ride), BF16)] * (2 * D), moved=3_000_000
        )(*pairs)
        parts = [plane[0]] + [
            send(plane[2 * a + b], lambda d, w: ((d + a) % D, w ^ (2 * b)))
            for a, b in ((1, 1), (1, 0), (0, 1))
        ]
        line = call(
            functools.partial(line_body, Z),
            [shape((width, R + ride), BF16)] * Z,
            moved=1_000_000,
        )(*parts)
        terms = [line[0]]
        for s in range(1, Z):
            terms.append(send(line[s], lambda d, w: (d, (w + 4 * s) % W)))
        grad_s, grad_t, norm, grad_latents = call(
            functools.partial(last_body, sizes, scale, Z),
            [
                shape((width, shard_s), F32),
                shape((width, shard_t), F32),
                shape((2, width), F32),
                shape((rows, channels), BF16),
            ],
            moved=1_000_000,
        )(*terms, *operands)
        grad_s, grad_t = grad_s.T, grad_t.T
    else:
        sums = lax.all_to_all(
            grads_t[1], ("dp", "wide"), split_axis=0, concat_axis=0, tiled=True
        )
        norm, grad_latents = call(
            functools.partial(apart_body, sizes, scale),
            [shape((2, width), F32), shape((rows, channels), BF16)],
        )(sums, *operands)
        outs = []
        for full in (grads_s[0], grads_t[0]):
            part = lax.psum_scatter(
                full.astype(F32), "wide", scatter_dimension=0, tiled=True
            ).T.astype(BF16)
            part = lax.psum_scatter(part, "dp", scatter_dimension=0, tiled=True)
            outs.append(part.astype(F32) * scale)
        grad_s, grad_t = outs
    return (
        block_out.reshape(latents.shape),
        grad_latents.reshape(latents.shape),
        grad_s,
        grad_t,
        norm,
    )


def solution(mesh):
    return jax.shard_map(
        local,
        mesh=mesh,
        in_specs=(
            P("dp", "wide", None, None, None),
            P("dp", "wide", None, None, None),
            P(),
            P(),
            P("dp", None),
            P("dp", None),
        ),
        out_specs=(
            P("dp", "wide", None, None, None),
            P("dp", "wide", None, None, None),
            P("dp", "wide"),
            P("dp", "wide"),
            P(None, "wide"),
        ),
        check_vma=False,
    )
```

```python
import functools
import math

import jax
import jax.numpy as jnp
from jax import lax
from jax.experimental import pallas as pl
from jax.experimental.pallas import tpu as pltpu
from jax.sharding import PartitionSpec as P

GROUPS = 32
EPSILON = 1e-05
F32 = jnp.float32
BF16 = jnp.bfloat16
VMEM = pl.BlockSpec(memory_space=pltpu.VMEM)
HBM = pl.BlockSpec(memory_space=pltpu.HBM)
FIRST_VMEM = 60 << 20
NT = (((1,), (1,)), ((), ()))
NN = (((1,), (0,)), ((), ()))


def call(body, out_shapes, scratch=(), flops=0, moved=0, in_specs=None, vmem=40 << 20):
    many = isinstance(out_shapes, (tuple, list))

    def run(*operands):
        return pl.pallas_call(
            body,
            out_shape=out_shapes,
            in_specs=in_specs or [VMEM] * len(operands),
            out_specs=[VMEM] * len(out_shapes) if many else VMEM,
            scratch_shapes=list(scratch),
            compiler_params=pltpu.CompilerParams(vmem_limit_bytes=vmem),
            cost_estimate=pl.CostEstimate(
                flops=flops, bytes_accessed=moved, transcendentals=0
            ),
        )(*operands)

    return run


def shape(dims, kind):
    return jax.ShapeDtypeStruct(dims, kind)


def mm(left, right, dims=NN):
    return lax.dot_general(left, right, dims, preferred_element_type=F32)


def group_total(rows, per_group):
    channels = rows.shape[-1]
    first = lax.broadcasted_iota(jnp.int32, (channels, channels), 0) // per_group
    second = lax.broadcasted_iota(jnp.int32, (channels, channels), 1) // per_group
    same = (first == second).astype(F32)
    return lax.dot_general(
        rows, same, NN, precision=lax.Precision.HIGHEST, preferred_element_type=F32
    )


def stats_body(lat_ref, gain_ref, bias_ref, ws_ref, wt_ref, out_ref, half_ref, *scratch):
    lat_here, gain_here, bias_here, sems = scratch
    core = lax.rem(lax.axis_index("wide"), 2)
    moves = [(lat_ref, lat_here), (gain_ref, gain_here), (bias_ref, bias_here)]
    half = ws_ref.shape[0] // 2
    start = pl.multiple_of(core * half, 16)
    moves.append((ws_ref.at[pl.ds(start, half)], half_ref.at[pl.ds(0, half)]))
    moves.append((wt_ref, half_ref.at[pl.ds(half, wt_ref.shape[0])]))
    copies = [pltpu.make_async_copy(*move, sems.at[at]) for at, move in enumerate(moves)]
    for copy in copies:
        copy.start()
    for copy in copies[:3]:
        copy.wait()
    x = lat_here[...].astype(F32)
    sums = [jnp.sum(x, axis=0, keepdims=True), jnp.sum(x * x, axis=0, keepdims=True)]
    both = jnp.concatenate(
        [
            jnp.concatenate([sums[0], gain_here[...]], axis=1),
            jnp.concatenate([sums[1], bias_here[...]], axis=1),
        ],
        axis=0,
    )
    out_ref[...] = jnp.broadcast_to(both[None], out_ref.shape)
    for copy in copies[3:]:
        copy.wait()


def transpose_body(cot_ref, out_ref):
    out_ref[...] = cot_ref[...].astype(F32).T.astype(BF16)


def fill_spatial(full, shard_ref, pieces, D):
    d = lax.axis_index("dp")
    core = lax.rem(lax.axis_index("wide"), 2)
    n = shard_ref.shape[0]
    half = n // 2
    full[pl.ds(pl.multiple_of(d * n, 16), n)] = shard_ref[...]
    for s in range(1, D):
        source = lax.rem(d + D - s, D)
        for which in range(2):
            holder = core if which == 0 else 1 - core
            start = pl.multiple_of(source * n + holder * half, 16)
            full[pl.ds(start, half)] = pieces[2 * (s - 1) + which][0:half]


def fill_temporal(full, shard_ref, firsts, D):
    d = lax.axis_index("dp")
    n = shard_ref.shape[0]
    full[pl.ds(pl.multiple_of(d * n, 16), n)] = shard_ref[...]
    for s in range(1, D):
        start = pl.multiple_of(lax.rem(d + D - s, D) * n, 16)
        full[pl.ds(start, n)] = firsts[s - 1][firsts[s - 1].shape[0] - n :]


def whiten(lat, stats, count, per_group):
    total = group_total(jnp.sum(stats[:, :, : lat.shape[1]], axis=0), per_group) / count
    mean = total[0:1]
    inv_std = 1.0 / jnp.sqrt(total[1:2] - mean * mean + EPSILON)
    return (lat.astype(F32) - mean) * inv_std, inv_std


def store_shifted(pad_ref, values, frames, cells, cols):
    total = frames * cells
    column = lax.broadcasted_iota(jnp.int32, (total, 1), 0) % cols
    left = jnp.where(column == 0, 0.0, pltpu.roll(values, 1, 0))
    right = jnp.where(column == cols - 1, 0.0, pltpu.roll(values, total - 1, 0))
    edge = jnp.zeros((cols, values.shape[1]), BF16)
    for at, form in enumerate((left, values, right)):
        low = form.astype(BF16)
        for f in range(frames):
            pad_ref[at, f, 0:cols] = edge
            pad_ref[at, f, cols : cols + cells] = low[f * cells : (f + 1) * cells]
            pad_ref[at, f, cols + cells :] = edge


def window(pad_ref, dy, dx, frames, cells, cols):
    return jnp.concatenate(
        [pad_ref[dx, f, dy * cols : dy * cols + cells] for f in range(frames)], axis=0
    )


def in_parts(total):
    high = total.astype(BF16).astype(F32)
    return jnp.concatenate([high, total - high], axis=0).astype(BF16)


def from_parts(terms):
    total = 0.0
    for term in terms:
        wide = term.astype(F32)
        total = total + (wide[0:8] + wide[8:16])
    return total


def add(terms):
    total = terms[0].astype(F32)
    for term in terms[1:]:
        total += term.astype(F32)
    return total


def core_order(transposed_ref, W, core):
    step = transposed_ref.shape[0] // W
    order = [(2 * j + core) * step for j in range(W // 2)]
    order += [(2 * j + 1 - core) * step for j in range(W // 2)]
    return jnp.concatenate(
        [transposed_ref[pl.ds(pl.multiple_of(at, 16), step)] for at in order], axis=0
    )


def put(block, column, shard, keep_ref, send_ref):
    low = block.astype(BF16)
    if send_ref is None:
        keep_ref[:, column : column + block.shape[1]] = low
        return
    half = block.shape[0] // 2
    for at in range(0, block.shape[1], 128):
        owner, place = (column + at) // shard, (column + at) % shard
        keep_ref[owner, :, place : place + 128] = low[:half, at : at + 128]
        send_ref[owner, :, place : place + 128] = low[half:, at : at + 128]


def affine_of(stats_ref):
    return stats_ref[0, :, stats_ref.shape[2] // 2 :]


def normalise(lat_ref, stats_ref, count, per_group):
    white, inv_std = whiten(lat_ref[...], stats_ref[...], count, per_group)
    affine = affine_of(stats_ref)
    normed = white * affine[0:1] + affine[1:2]
    return white, normed, jax.nn.sigmoid(normed)


def first_body(sizes, lat_ref, cot_ref, halo_ref, stats_ref, wt_ref, *rest):
    D, W, frames, cells, cols, count, per_group, aligned = sizes
    firsts, rest = rest[: D - 1], rest[D - 1 :]
    full_wt, act_pad, gsa_t = rest[-3:]
    gsa_ref, seen_ref, keep_ref = rest[:3]
    send_ref = rest[3] if aligned else None
    channels = lat_ref.shape[1]
    core = lax.rem(lax.axis_index("wide"), 2)
    fill_temporal(full_wt, wt_ref, firsts, D)
    rows = frames * cells
    extended = jnp.concatenate([cot_ref[...], halo_ref[...]], axis=0)
    gsa = jnp.zeros((rows, channels), F32)
    for k in range(3):
        gsa += mm(
            extended[k * cells : k * cells + rows],
            full_wt[k * channels : (k + 1) * channels],
            NT,
        )
    gsa_ref[...] = gsa.astype(BF16)
    gsa_t[...] = gsa.astype(BF16).astype(F32).T.astype(BF16)
    _, normed, sig = normalise(lat_ref, stats_ref, count, per_group)
    act = (normed * sig).astype(BF16).astype(F32)
    store_shifted(act_pad, act, frames, cells, cols)
    left = core_order(gsa_t, W, core) if aligned else gsa_t[...]
    shard = wt_ref.shape[0] * 3
    for dy in range(3):
        for dx in range(3):
            at = (3 * dy + dx) * channels
            seen = window(act_pad, dy, dx, frames, cells, cols)
            seen_ref[:, at : at + channels] = seen
            put(mm(left, seen), at, shard, keep_ref, send_ref)


def second_body(
    sizes, lat_ref, cot_t_ref, halo_ref, stats_ref, gsa_ref, seen_ref, ws_ref, *rest
):
    D, W, frames, cells, cols, count, per_group, aligned = sizes
    pieces, rest = rest[: 2 * (D - 1)], rest[2 * (D - 1) :]
    full_ws, side_ws, gsa_pad, gsa_seen, cot_t = rest[-5:]
    spatial_ref, grad_ref, keep_ref, other_ref = rest[:4]
    send_ref = other_ref if aligned else None
    channels = lat_ref.shape[1]
    core = lax.rem(lax.axis_index("wide"), 2)
    fill_spatial(full_ws, ws_ref, pieces, D)
    rows = frames * cells
    white, normed, sig = normalise(lat_ref, stats_ref, count, per_group)
    store_shifted(gsa_pad, gsa_ref[...].astype(F32), frames, cells, cols)
    cot_t[:, :rows] = cot_t_ref[...]
    for f in range(2):
        cot_t[:, rows + f * cells : rows + (f + 1) * cells] = (
            halo_ref[f * cells : (f + 1) * cells].astype(F32).T.astype(BF16)
        )
    left = core_order(cot_t, W, core) if aligned else cot_t[...]
    spatial = mm(seen_ref[...], full_ws[...]).astype(BF16)
    spatial_ref[...] = spatial
    shard = ws_ref.shape[0] // 3
    for k in range(3):
        block = mm(left[:, k * cells : k * cells + rows], spatial)
        put(block, k * channels, shard, keep_ref, send_ref)

    for dy in range(3):
        for dx in range(3):
            at = (3 * dy + dx) * channels
            gsa_seen[:, at : at + channels] = window(
                gsa_pad, 2 - dy, 2 - dx, frames, cells, cols
            )
            side_ws[:, at : at + channels] = full_ws[at : at + channels]
    grad = mm(gsa_seen[...], side_ws[...], NT)
    grad = grad * (sig * (1.0 + normed * (1.0 - sig)))
    grad_ref[...] = grad
    gain_term = jnp.sum(grad * white, axis=0, keepdims=True)
    bias_term = jnp.sum(grad, axis=0, keepdims=True)
    if not aligned:
        both = jnp.concatenate([gain_term, bias_term], axis=0)
        other_ref[...] = jnp.broadcast_to(both[None], other_ref.shape)
        return
    d = lax.axis_index("dp")
    quarter = jnp.concatenate(
        [term[:, at : at + 128] for term in (gain_term, bias_term) for at in (0, 128)], axis=0
    )
    low = in_parts(
        jnp.concatenate([jnp.where(d == s, quarter, 0.0) for s in range(2)], axis=0)
    )
    for target in (keep_ref, send_ref):
        for owner in range(D):
            for at in range(0, channels // 2, 16):
                target[owner, at : at + 16, shard:] = low


def block_body(sizes, lat_ref, spatial_ref, before_ref, wt_ref, *rest):
    D, W, frames, cells, cols, count, per_group, aligned = sizes
    firsts = rest[: D - 1]
    block_ref, full_wt = rest[D - 1 :]
    channels = lat_ref.shape[1]
    fill_temporal(full_wt, wt_ref, firsts, D)
    extended = jnp.concatenate([before_ref[...], spatial_ref[...]], axis=0)
    rows = frames * cells
    temporal = jnp.zeros((rows, channels), F32)
    for k in range(3):
        start = (2 - k) * cells
        temporal += mm(
            extended[start : start + rows], full_wt[k * channels : (k + 1) * channels]
        )
    block_ref[...] = (lat_ref[...].astype(F32) + temporal).astype(BF16)


def latent_gradient(sizes, total, lat_ref, cot_ref, stats_ref, grad_ref):
    D, W, frames, cells, cols, count, per_group, aligned = sizes
    white, inv_std = whiten(lat_ref[...], stats_ref[...], count, per_group)
    gain = affine_of(stats_ref)[0:1]
    means = group_total(total * gain, per_group) / count
    inner = inv_std * (grad_ref[...] * gain - means[1:2] - white * means[0:1])
    return (cot_ref[...].astype(F32) + inner).astype(BF16)


def plane_body(keep_s, got_s, keep_t, got_t, *outs):
    d = lax.axis_index("dp")
    y = lax.rem(lax.axis_index("wide") // 2, 2)
    split = keep_s.shape[-1]
    ride = outs[0].shape[-1] - 128
    for a in range(2):
        for b in range(2):
            owner, side = lax.rem(d + a, 2), lax.rem(y + b, 2)
            out = outs[2 * a + b]
            for z in range(out.shape[0]):
                out[z, :, :split] = add([keep_s[owner, z, side], got_s[owner, z, side]]).astype(
                    BF16
                )
                both = [keep_t[owner, z, side], got_t[owner, z, side]]
                out[z, :, split:ride] = add([t[:, : ride - split] for t in both]).astype(BF16)
                out[z, :, ride:] = in_parts(from_parts([t[:, ride - split :] for t in both]))


def line_body(depth, *refs):
    terms, outs = refs[:4], refs[4:]
    z = lax.axis_index("wide") // 4
    ride = outs[0].shape[-1] - 128
    for s in range(depth):
        owner = lax.rem(z + s, depth)
        seen = [term[owner] for term in terms]
        outs[s][:, :ride] = add([t[:, :ride] for t in seen]).astype(BF16)
        outs[s][:, ride:] = in_parts(from_parts([t[:, ride:] for t in seen]))


def last_body(sizes, scale, depth, *refs):
    terms, operands, outs = refs[:depth], refs[depth:-4], refs[-4:]
    spatial_ref, temporal_ref, norm_ref, glat_ref = outs
    split = spatial_ref.shape[1]
    ride = terms[0].shape[1] - 128
    sums = from_parts([term[:, ride:] for term in terms])

    def rows_of(part):
        return jnp.concatenate(
            [jnp.concatenate([part[at : at + 1], part[at + 1 : at + 2]], axis=1) for at in (0, 2)],
            axis=0,
        )

    first, second = rows_of(sums[0:4]), rows_of(sums[4:8])
    own = jnp.where(lax.axis_index("dp") == 0, first, second)
    glat_ref[...] = latent_gradient(sizes, own, *operands)
    norm_columns(scale, first + second, norm_ref)
    total = add([term[:, :ride] for term in terms]) * scale
    spatial_ref[...] = total[:, :split]
    temporal_ref[...] = total[:, split:]


def apart_body(sizes, scale, sums_ref, *refs):
    norm_ref, glat_ref = refs[-2:]
    W = sizes[1]
    own = jnp.sum(sums_ref[pl.ds(lax.axis_index("dp") * W, W)], axis=0)
    norm_columns(scale, jnp.sum(sums_ref[...], axis=0), norm_ref)
    glat_ref[...] = latent_gradient(sizes, own, *refs[:-2])


def norm_columns(scale, norm, norm_ref):
    channels, width = norm.shape[1], norm_ref.shape[1]
    row = lax.broadcasted_iota(jnp.int32, (channels, width), 0)
    column = lax.broadcasted_iota(jnp.int32, (channels, width), 1)
    pick = (row == column + lax.axis_index("wide") * width).astype(F32)
    norm_ref[...] = (
        lax.dot_general(
            norm, pick, NN, precision=lax.Precision.HIGHEST, preferred_element_type=F32
        )
        * scale
    )


def local(latents, cotangent, norm_gain, norm_bias, w_spatial, w_temporal):
    D, W = lax.axis_size("dp"), lax.axis_size("wide")
    _, frames, rows_here, cols, channels = latents.shape
    cells = rows_here * cols
    rows = frames * cells
    per_group = channels // GROUPS
    count = W * frames * cells * per_group
    shard_s, shard_t = w_spatial.shape[0], w_temporal.shape[0]
    aligned = (channels // W) % 16 == 0 and shard_s % 128 == 0 and shard_t % 128 == 0
    aligned = aligned and W % 4 == 0 and D == 2 and channels == 256
    sizes = (D, W, frames, cells, cols, count, per_group, aligned)
    scale = 1.0 / math.sqrt(D * W * frames * cells)

    lat, cot = latents.reshape(rows, channels), cotangent.reshape(rows, channels)
    gain, bias = norm_gain.reshape(1, channels), norm_bias.reshape(1, channels)

    def over_all(moves):
        pairs = []
        for d in range(D):
            for w in range(W):
                to = moves(d, w)
                pairs.append((d * W + w, to[0] * W + to[1]))
        return pairs

    def send(value, moves):
        return lax.ppermute(value, ("dp", "wide"), over_all(moves))

    R = shard_s + shard_t
    stats, half = call(
        stats_body,
        [
            shape((W, 2, 2 * channels), F32),
            shape((shard_s // 2 + shard_t, channels), BF16),
        ],
        [
            pltpu.VMEM((rows, channels), BF16),
            pltpu.VMEM((1, channels), F32),
            pltpu.VMEM((1, channels), F32),
            pltpu.SemaphoreType.DMA((5,)),
        ],
        in_specs=[HBM] * 5,
        vmem=FIRST_VMEM,
    )(lat, gain, bias, w_spatial, w_temporal)
    cot_t = call(transpose_body, shape((channels, rows), BF16), moved=300_000)(cot)
    firsts = [send(half, lambda d, w: ((d + s) % D, w)) for s in range(1, D)]

    halo = lax.ppermute(cot, "wide", [(w + 1, w) for w in range(W - 1)])
    stats = lax.all_to_all(stats, "wide", split_axis=0, concat_axis=0, tiled=True)
    firsts, stats, halo, cot_t = lax.optimization_barrier((firsts, stats, halo, cot_t))
    pieces = []
    for first in firsts:
        pieces += [first, send(first, lambda d, w: (d, w ^ 1))]

    ride = 128 if aligned else 0
    if aligned:
        terms_s = [shape((D, channels // 2, shard_s), BF16)] * 2
        terms_t = [shape((D, channels // 2, shard_t + ride), BF16)] * 2
    else:
        terms_s = [shape((channels, D * shard_s), BF16)]
        terms_t = [shape((channels, D * shard_t), BF16), shape((D * W, 2, channels), F32)]
    pad = pltpu.VMEM((3, frames, cells + 2 * cols, channels), BF16)
    taps = D * shard_s
    gsa, seen, *grads_s = call(
        functools.partial(first_body, sizes),
        [shape((rows, channels), BF16), shape((rows, taps), BF16)] + terms_s,
        [pltpu.VMEM((D * shard_t, channels), BF16), pad, pltpu.VMEM((channels, rows), BF16)],
        flops=2 * 12 * rows * channels * channels,
        moved=3_000_000,
    )(lat, cot, halo, stats, w_temporal, *firsts)
    spatial, grad, *grads_t = call(
        functools.partial(second_body, sizes),
        [shape((rows, channels), BF16), shape((rows, channels), F32)] + terms_t,
        [
            pltpu.VMEM((taps, channels), BF16),
            pltpu.VMEM((channels, taps), BF16),
            pad,
            pltpu.VMEM((rows, taps), BF16),
            pltpu.VMEM((channels, rows + 2 * cells), BF16),
        ],
        flops=2 * 21 * rows * channels * channels,
        moved=3_000_000,
    )(lat, cot_t, halo, stats, gsa, seen, w_spatial, *pieces)
    def finish_block(spatial):
        before = lax.ppermute(spatial, "wide", [(w, w + 1) for w in range(W - 1)])
        return call(
            functools.partial(block_body, sizes),
            shape((rows, channels), BF16),
            [pltpu.VMEM((D * shard_t, channels), BF16)],
            flops=2 * 3 * rows * channels * channels,
            moved=1_000_000,
        )(lat, spatial, before, w_temporal, *firsts)

    width = channels // W
    operands = (lat, cot, stats, grad)
    if aligned:
        Z = W // 4

        def over_core(away):
            return send(away, lambda d, w: (d, w ^ 1))

        pairs = []
        for keep, away in (grads_s, grads_t):
            view = (D, Z, 2, width, keep.shape[-1])
            pairs += [keep.reshape(view), over_core(away).reshape(view)]
        plane = call(
            plane_body, [shape((Z, width, R + ride), BF16)] * (2 * D), moved=3_000_000
        )(*pairs)
        parts = [plane[0]] + [
            send(plane[2 * a + b], lambda d, w: ((d + a) % D, w ^ (2 * b)))
            for a, b in ((0, 1), (1, 0), (1, 1))
        ]
        line = call(
            functools.partial(line_body, Z),
            [shape((width, R + ride), BF16)] * Z,
            moved=1_000_000,
        )(*parts)
        line, spatial = lax.optimization_barrier((line, spatial))
        block_out = finish_block(spatial)
        terms = [line[0]]
        for s in range(1, Z):
            terms.append(send(line[s], lambda d, w: (d, (w + 4 * s) % W)))
        grad_s, grad_t, norm, grad_latents = call(
            functools.partial(last_body, sizes, scale, Z),
            [
                shape((width, shard_s), F32),
                shape((width, shard_t), F32),
                shape((2, width), F32),
                shape((rows, channels), BF16),
            ],
            moved=1_000_000,
        )(*terms, *operands)
        grad_s, grad_t = grad_s.T, grad_t.T
    else:
        block_out = finish_block(spatial)
        sums = lax.all_to_all(
            grads_t[1], ("dp", "wide"), split_axis=0, concat_axis=0, tiled=True
        )
        norm, grad_latents = call(
            functools.partial(apart_body, sizes, scale),
            [shape((2, width), F32), shape((rows, channels), BF16)],
        )(sums, *operands)
        outs = []
        for full in (grads_s[0], grads_t[0]):
            part = lax.psum_scatter(
                full.astype(F32), "wide", scatter_dimension=0, tiled=True
            ).T.astype(BF16)
            part = lax.psum_scatter(part, "dp", scatter_dimension=0, tiled=True)
            outs.append(part.astype(F32) * scale)
        grad_s, grad_t = outs
    return (
        block_out.reshape(latents.shape),
        grad_latents.reshape(latents.shape),
        grad_s,
        grad_t,
        norm,
    )


def solution(mesh):
    return jax.shard_map(
        local,
        mesh=mesh,
        in_specs=(
            P("dp", "wide", None, None, None),
            P("dp", "wide", None, None, None),
            P(),
            P(),
            P("dp", None),
            P("dp", None),
        ),
        out_specs=(
            P("dp", "wide", None, None, None),
            P("dp", "wide", None, None, None),
            P("dp", "wide"),
            P("dp", "wide"),
            P(None, "wide"),
        ),
        check_vma=False,
    )
```

```python
import functools
import math

import jax
import jax.numpy as jnp
from jax import lax
from jax.experimental import pallas as pl
from jax.experimental.pallas import tpu as pltpu
from jax.sharding import PartitionSpec as P

GROUPS = 32
EPSILON = 1e-05
F32 = jnp.float32
BF16 = jnp.bfloat16
VMEM = pl.BlockSpec(memory_space=pltpu.VMEM)
HBM = pl.BlockSpec(memory_space=pltpu.HBM)
FIRST_VMEM = 60 << 20
NT = (((1,), (1,)), ((), ()))
NN = (((1,), (0,)), ((), ()))


def call(body, out_shapes, scratch=(), flops=0, moved=0, in_specs=None, vmem=40 << 20):
    many = isinstance(out_shapes, (tuple, list))

    def run(*operands):
        return pl.pallas_call(
            body,
            out_shape=out_shapes,
            in_specs=in_specs or [VMEM] * len(operands),
            out_specs=[VMEM] * len(out_shapes) if many else VMEM,
            scratch_shapes=list(scratch),
            compiler_params=pltpu.CompilerParams(vmem_limit_bytes=vmem),
            cost_estimate=pl.CostEstimate(
                flops=flops, bytes_accessed=moved, transcendentals=0
            ),
        )(*operands)

    return run


def shape(dims, kind):
    return jax.ShapeDtypeStruct(dims, kind)


def mm(left, right, dims=NN):
    return lax.dot_general(left, right, dims, preferred_element_type=F32)


def group_total(rows, per_group):
    channels = rows.shape[-1]
    first = lax.broadcasted_iota(jnp.int32, (channels, channels), 0) // per_group
    second = lax.broadcasted_iota(jnp.int32, (channels, channels), 1) // per_group
    same = (first == second).astype(F32)
    return lax.dot_general(
        rows, same, NN, precision=lax.Precision.HIGHEST, preferred_element_type=F32
    )


def stats_body(lat_ref, gain_ref, bias_ref, ws_ref, wt_ref, out_ref, half_ref, *scratch):
    lat_here, gain_here, bias_here, sems = scratch
    core = lax.rem(lax.axis_index("wide"), 2)
    moves = [(lat_ref, lat_here), (gain_ref, gain_here), (bias_ref, bias_here)]
    half = ws_ref.shape[0] // 2
    start = pl.multiple_of(core * half, 16)
    moves.append((ws_ref.at[pl.ds(start, half)], half_ref.at[pl.ds(0, half)]))
    moves.append((wt_ref, half_ref.at[pl.ds(half, wt_ref.shape[0])]))
    copies = [pltpu.make_async_copy(*move, sems.at[at]) for at, move in enumerate(moves)]
    for copy in copies:
        copy.start()
    for copy in copies[:3]:
        copy.wait()
    x = lat_here[...].astype(F32)
    sums = [jnp.sum(x, axis=0, keepdims=True), jnp.sum(x * x, axis=0, keepdims=True)]
    both = jnp.concatenate(
        [
            jnp.concatenate([sums[0], gain_here[...]], axis=1),
            jnp.concatenate([sums[1], bias_here[...]], axis=1),
        ],
        axis=0,
    )
    out_ref[...] = jnp.broadcast_to(both[None], out_ref.shape)
    for copy in copies[3:]:
        copy.wait()


def transpose_body(cot_ref, out_ref):
    out_ref[...] = cot_ref[...].astype(F32).T.astype(BF16)


def fill_spatial(full, shard_ref, pieces, D):
    d = lax.axis_index("dp")
    core = lax.rem(lax.axis_index("wide"), 2)
    n = shard_ref.shape[0]
    half = n // 2
    full[pl.ds(pl.multiple_of(d * n, 16), n)] = shard_ref[...]
    for s in range(1, D):
        source = lax.rem(d + D - s, D)
        for which in range(2):
            holder = core if which == 0 else 1 - core
            start = pl.multiple_of(source * n + holder * half, 16)
            full[pl.ds(start, half)] = pieces[2 * (s - 1) + which][0:half]


def fill_temporal(full, shard_ref, firsts, D):
    d = lax.axis_index("dp")
    n = shard_ref.shape[0]
    full[pl.ds(pl.multiple_of(d * n, 16), n)] = shard_ref[...]
    for s in range(1, D):
        start = pl.multiple_of(lax.rem(d + D - s, D) * n, 16)
        full[pl.ds(start, n)] = firsts[s - 1][firsts[s - 1].shape[0] - n :]


def whiten(lat, stats, count, per_group):
    total = group_total(jnp.sum(stats[:, :, : lat.shape[1]], axis=0), per_group) / count
    mean = total[0:1]
    inv_std = 1.0 / jnp.sqrt(total[1:2] - mean * mean + EPSILON)
    return (lat.astype(F32) - mean) * inv_std, inv_std


def store_shifted(pad_ref, values, frames, cells, cols):
    total = frames * cells
    column = lax.broadcasted_iota(jnp.int32, (total, 1), 0) % cols
    left = jnp.where(column == 0, 0.0, pltpu.roll(values, 1, 0))
    right = jnp.where(column == cols - 1, 0.0, pltpu.roll(values, total - 1, 0))
    edge = jnp.zeros((cols, values.shape[1]), BF16)
    for at, form in enumerate((left, values, right)):
        low = form.astype(BF16)
        for f in range(frames):
            pad_ref[at, f, 0:cols] = edge
            pad_ref[at, f, cols : cols + cells] = low[f * cells : (f + 1) * cells]
            pad_ref[at, f, cols + cells :] = edge


def window(pad_ref, dy, dx, frames, cells, cols):
    return jnp.concatenate(
        [pad_ref[dx, f, dy * cols : dy * cols + cells] for f in range(frames)], axis=0
    )


def in_parts(total):
    high = total.astype(BF16).astype(F32)
    return jnp.concatenate([high, total - high], axis=0).astype(BF16)


def from_parts(terms):
    total = 0.0
    for term in terms:
        wide = term.astype(F32)
        total = total + (wide[0:8] + wide[8:16])
    return total


def add(terms):
    total = terms[0].astype(F32)
    for term in terms[1:]:
        total += term.astype(F32)
    return total


def core_order(transposed_ref, W, core):
    step = transposed_ref.shape[0] // W
    order = [(2 * j + core) * step for j in range(W // 2)]
    order += [(2 * j + 1 - core) * step for j in range(W // 2)]
    return jnp.concatenate(
        [transposed_ref[pl.ds(pl.multiple_of(at, 16), step)] for at in order], axis=0
    )


def put(block, column, shard, keep_ref, send_ref):
    low = block.astype(BF16)
    if send_ref is None:
        keep_ref[:, column : column + block.shape[1]] = low
        return
    half = block.shape[0] // 2
    for at in range(0, block.shape[1], 128):
        owner, place = (column + at) // shard, (column + at) % shard
        keep_ref[owner, :, place : place + 128] = low[:half, at : at + 128]
        send_ref[owner, :, place : place + 128] = low[half:, at : at + 128]


def affine_of(stats_ref):
    return stats_ref[0, :, stats_ref.shape[2] // 2 :]


def normalise(lat_ref, stats_ref, count, per_group):
    white, inv_std = whiten(lat_ref[...], stats_ref[...], count, per_group)
    affine = affine_of(stats_ref)
    normed = white * affine[0:1] + affine[1:2]
    return white, normed, jax.nn.sigmoid(normed)


def first_body(sizes, lat_ref, cot_ref, halo_ref, stats_ref, wt_ref, *rest):
    D, W, frames, cells, cols, count, per_group, aligned = sizes
    firsts, rest = rest[: D - 1], rest[D - 1 :]
    full_wt, act_pad, gsa_t = rest[-3:]
    gsa_ref, seen_ref, keep_ref = rest[:3]
    send_ref = rest[3] if aligned else None
    channels = lat_ref.shape[1]
    core = lax.rem(lax.axis_index("wide"), 2)
    fill_temporal(full_wt, wt_ref, firsts, D)
    rows = frames * cells
    extended = jnp.concatenate([cot_ref[...], halo_ref[...]], axis=0)
    gsa = jnp.zeros((rows, channels), F32)
    for k in range(3):
        gsa += mm(
            extended[k * cells : k * cells + rows],
            full_wt[k * channels : (k + 1) * channels],
            NT,
        )
    gsa_ref[...] = gsa.astype(BF16)
    gsa_t[...] = gsa.astype(BF16).astype(F32).T.astype(BF16)
    _, normed, sig = normalise(lat_ref, stats_ref, count, per_group)
    act = (normed * sig).astype(BF16).astype(F32)
    store_shifted(act_pad, act, frames, cells, cols)
    left = core_order(gsa_t, W, core) if aligned else gsa_t[...]
    shard = wt_ref.shape[0] * 3
    for dy in range(3):
        for dx in range(3):
            at = (3 * dy + dx) * channels
            seen = window(act_pad, dy, dx, frames, cells, cols)
            seen_ref[:, at : at + channels] = seen
            put(mm(left, seen), at, shard, keep_ref, send_ref)


def second_body(
    sizes, lat_ref, cot_t_ref, halo_ref, stats_ref, gsa_ref, seen_ref, ws_ref, *rest
):
    D, W, frames, cells, cols, count, per_group, aligned = sizes
    pieces, rest = rest[: 2 * (D - 1)], rest[2 * (D - 1) :]
    full_ws, side_ws, gsa_pad, gsa_seen, cot_t = rest[-5:]
    spatial_ref, grad_ref, keep_ref, other_ref = rest[:4]
    send_ref = other_ref if aligned else None
    channels = lat_ref.shape[1]
    core = lax.rem(lax.axis_index("wide"), 2)
    fill_spatial(full_ws, ws_ref, pieces, D)
    rows = frames * cells
    white, normed, sig = normalise(lat_ref, stats_ref, count, per_group)
    store_shifted(gsa_pad, gsa_ref[...].astype(F32), frames, cells, cols)
    cot_t[:, :rows] = cot_t_ref[...]
    for f in range(2):
        cot_t[:, rows + f * cells : rows + (f + 1) * cells] = (
            halo_ref[f * cells : (f + 1) * cells].astype(F32).T.astype(BF16)
        )
    left = core_order(cot_t, W, core) if aligned else cot_t[...]
    spatial = mm(seen_ref[...], full_ws[...]).astype(BF16)
    spatial_ref[...] = spatial
    shard = ws_ref.shape[0] // 3
    for k in range(3):
        block = mm(left[:, k * cells : k * cells + rows], spatial)
        put(block, k * channels, shard, keep_ref, send_ref)

    for dy in range(3):
        for dx in range(3):
            at = (3 * dy + dx) * channels
            gsa_seen[:, at : at + channels] = window(
                gsa_pad, 2 - dy, 2 - dx, frames, cells, cols
            )
            side_ws[:, at : at + channels] = full_ws[at : at + channels]
    grad = mm(gsa_seen[...], side_ws[...], NT)
    grad = grad * (sig * (1.0 + normed * (1.0 - sig)))
    grad_ref[...] = grad
    gain_term = jnp.sum(grad * white, axis=0, keepdims=True)
    bias_term = jnp.sum(grad, axis=0, keepdims=True)
    if not aligned:
        both = jnp.concatenate([gain_term, bias_term], axis=0)
        other_ref[...] = jnp.broadcast_to(both[None], other_ref.shape)
        return
    d = lax.axis_index("dp")
    quarter = jnp.concatenate(
        [term[:, at : at + 128] for term in (gain_term, bias_term) for at in (0, 128)], axis=0
    )
    low = in_parts(
        jnp.concatenate([jnp.where(d == s, quarter, 0.0) for s in range(2)], axis=0)
    )
    for target in (keep_ref, send_ref):
        for owner in range(D):
            for at in range(0, channels // 2, 16):
                target[owner, at : at + 16, shard:] = low


def block_body(sizes, lat_ref, spatial_ref, before_ref, wt_ref, *rest):
    D, W, frames, cells, cols, count, per_group, aligned = sizes
    firsts = rest[: D - 1]
    block_ref, full_wt = rest[D - 1 :]
    channels = lat_ref.shape[1]
    fill_temporal(full_wt, wt_ref, firsts, D)
    extended = jnp.concatenate([before_ref[...], spatial_ref[...]], axis=0)
    rows = frames * cells
    temporal = jnp.zeros((rows, channels), F32)
    for k in range(3):
        start = (2 - k) * cells
        temporal += mm(
            extended[start : start + rows], full_wt[k * channels : (k + 1) * channels]
        )
    block_ref[...] = (lat_ref[...].astype(F32) + temporal).astype(BF16)


def latent_gradient(sizes, total, lat_ref, cot_ref, stats_ref, grad_ref):
    D, W, frames, cells, cols, count, per_group, aligned = sizes
    white, inv_std = whiten(lat_ref[...], stats_ref[...], count, per_group)
    gain = affine_of(stats_ref)[0:1]
    means = group_total(total * gain, per_group) / count
    inner = inv_std * (grad_ref[...] * gain - means[1:2] - white * means[0:1])
    return (cot_ref[...].astype(F32) + inner).astype(BF16)


def plane_body(keep_s, got_s, keep_t, got_t, *outs):
    d = lax.axis_index("dp")
    y = lax.rem(lax.axis_index("wide") // 2, 2)
    split = keep_s.shape[-1]
    ride = outs[0].shape[-1] - 128
    for a in range(2):
        for b in range(2):
            owner, side = lax.rem(d + a, 2), lax.rem(y + b, 2)
            out = outs[2 * a + b]
            for z in range(out.shape[0]):
                out[z, :, :split] = add([keep_s[owner, z, side], got_s[owner, z, side]]).astype(
                    BF16
                )
                both = [keep_t[owner, z, side], got_t[owner, z, side]]
                out[z, :, split:ride] = add([t[:, : ride - split] for t in both]).astype(BF16)
                out[z, :, ride:] = in_parts(from_parts([t[:, ride - split :] for t in both]))


def line_body(depth, *refs):
    terms, outs = refs[:4], refs[4:]
    z = lax.axis_index("wide") // 4
    ride = outs[0].shape[-1] - 128
    for s in range(depth):
        owner = lax.rem(z + s, depth)
        seen = [term[owner] for term in terms]
        outs[s][:, :ride] = add([t[:, :ride] for t in seen]).astype(BF16)
        outs[s][:, ride:] = in_parts(from_parts([t[:, ride:] for t in seen]))


def last_body(sizes, scale, depth, *refs):
    terms, operands, outs = refs[:depth], refs[depth:-4], refs[-4:]
    spatial_ref, temporal_ref, norm_ref, glat_ref = outs
    split = spatial_ref.shape[1]
    ride = terms[0].shape[1] - 128
    sums = from_parts([term[:, ride:] for term in terms])

    def rows_of(part):
        return jnp.concatenate(
            [jnp.concatenate([part[at : at + 1], part[at + 1 : at + 2]], axis=1) for at in (0, 2)],
            axis=0,
        )

    first, second = rows_of(sums[0:4]), rows_of(sums[4:8])
    own = jnp.where(lax.axis_index("dp") == 0, first, second)
    glat_ref[...] = latent_gradient(sizes, own, *operands)
    norm_columns(scale, first + second, norm_ref)
    total = add([term[:, :ride] for term in terms]) * scale
    spatial_ref[...] = total[:, :split]
    temporal_ref[...] = total[:, split:]


def apart_body(sizes, scale, sums_ref, *refs):
    norm_ref, glat_ref = refs[-2:]
    W = sizes[1]
    own = jnp.sum(sums_ref[pl.ds(lax.axis_index("dp") * W, W)], axis=0)
    norm_columns(scale, jnp.sum(sums_ref[...], axis=0), norm_ref)
    glat_ref[...] = latent_gradient(sizes, own, *refs[:-2])


def norm_columns(scale, norm, norm_ref):
    channels, width = norm.shape[1], norm_ref.shape[1]
    row = lax.broadcasted_iota(jnp.int32, (channels, width), 0)
    column = lax.broadcasted_iota(jnp.int32, (channels, width), 1)
    pick = (row == column + lax.axis_index("wide") * width).astype(F32)
    norm_ref[...] = (
        lax.dot_general(
            norm, pick, NN, precision=lax.Precision.HIGHEST, preferred_element_type=F32
        )
        * scale
    )


def local(latents, cotangent, norm_gain, norm_bias, w_spatial, w_temporal):
    D, W = lax.axis_size("dp"), lax.axis_size("wide")
    _, frames, rows_here, cols, channels = latents.shape
    cells = rows_here * cols
    rows = frames * cells
    per_group = channels // GROUPS
    count = W * frames * cells * per_group
    shard_s, shard_t = w_spatial.shape[0], w_temporal.shape[0]
    aligned = (channels // W) % 16 == 0 and shard_s % 128 == 0 and shard_t % 128 == 0
    aligned = aligned and W % 4 == 0 and D == 2 and channels == 256
    sizes = (D, W, frames, cells, cols, count, per_group, aligned)
    scale = 1.0 / math.sqrt(D * W * frames * cells)

    lat, cot = latents.reshape(rows, channels), cotangent.reshape(rows, channels)
    gain, bias = norm_gain.reshape(1, channels), norm_bias.reshape(1, channels)

    def over_all(moves):
        pairs = []
        for d in range(D):
            for w in range(W):
                to = moves(d, w)
                pairs.append((d * W + w, to[0] * W + to[1]))
        return pairs

    def send(value, moves):
        return lax.ppermute(value, ("dp", "wide"), over_all(moves))

    R = shard_s + shard_t
    stats, half = call(
        stats_body,
        [
            shape((W, 2, 2 * channels), F32),
            shape((shard_s // 2 + shard_t, channels), BF16),
        ],
        [
            pltpu.VMEM((rows, channels), BF16),
            pltpu.VMEM((1, channels), F32),
            pltpu.VMEM((1, channels), F32),
            pltpu.SemaphoreType.DMA((5,)),
        ],
        in_specs=[HBM] * 5,
        vmem=FIRST_VMEM,
    )(lat, gain, bias, w_spatial, w_temporal)
    cot_t = call(transpose_body, shape((channels, rows), BF16), moved=300_000)(cot)
    firsts = [send(half, lambda d, w: ((d + s) % D, w)) for s in range(1, D)]

    halo = lax.ppermute(cot, "wide", [(w + 1, w) for w in range(W - 1)])
    stats = lax.all_to_all(stats, "wide", split_axis=0, concat_axis=0, tiled=True)
    firsts, stats, halo, cot_t = lax.optimization_barrier((firsts, stats, halo, cot_t))
    pieces = []
    for first in firsts:
        pieces += [first, send(first, lambda d, w: (d, w ^ 1))]

    ride = 128 if aligned else 0
    if aligned:
        terms_s = [shape((D, channels // 2, shard_s), BF16)] * 2
        terms_t = [shape((D, channels // 2, shard_t + ride), BF16)] * 2
    else:
        terms_s = [shape((channels, D * shard_s), BF16)]
        terms_t = [shape((channels, D * shard_t), BF16), shape((D * W, 2, channels), F32)]
    pad = pltpu.VMEM((3, frames, cells + 2 * cols, channels), BF16)
    taps = D * shard_s
    gsa, seen, *grads_s = call(
        functools.partial(first_body, sizes),
        [shape((rows, channels), BF16), shape((rows, taps), BF16)] + terms_s,
        [pltpu.VMEM((D * shard_t, channels), BF16), pad, pltpu.VMEM((channels, rows), BF16)],
        flops=2 * 12 * rows * channels * channels,
        moved=3_000_000,
    )(lat, cot, halo, stats, w_temporal, *firsts)
    spatial, grad, *grads_t = call(
        functools.partial(second_body, sizes),
        [shape((rows, channels), BF16), shape((rows, channels), F32)] + terms_t,
        [
            pltpu.VMEM((taps, channels), BF16),
            pltpu.VMEM((channels, taps), BF16),
            pad,
            pltpu.VMEM((rows, taps), BF16),
            pltpu.VMEM((channels, rows + 2 * cells), BF16),
        ],
        flops=2 * 21 * rows * channels * channels,
        moved=3_000_000,
    )(lat, cot_t, halo, stats, gsa, seen, w_spatial, *pieces)
    before = lax.ppermute(spatial, "wide", [(w, w + 1) for w in range(W - 1)])
    block_out = call(
        functools.partial(block_body, sizes),
        shape((rows, channels), BF16),
        [pltpu.VMEM((D * shard_t, channels), BF16)],
        flops=2 * 3 * rows * channels * channels,
        moved=1_000_000,
    )(lat, spatial, before, w_temporal, *firsts)

    width = channels // W
    operands = (lat, cot, stats, grad)
    if aligned:
        Z = W // 4

        def over_core(away):
            return send(away, lambda d, w: (d, w ^ 1))

        pairs = []
        for keep, away in (grads_s, grads_t):
            view = (D, Z, 2, width, keep.shape[-1])
            pairs += [keep.reshape(view), over_core(away).reshape(view)]
        plane = call(
            plane_body, [shape((Z, width, R + ride), BF16)] * (2 * D), moved=3_000_000
        )(*pairs)
        parts = [plane[0]] + [
            send(plane[2 * a + b], lambda d, w: ((d + a) % D, w ^ (2 * b)))
            for a, b in ((1, 0), (0, 1), (1, 1))
        ]
        line = call(
            functools.partial(line_body, Z),
            [shape((width, R + ride), BF16)] * Z,
            moved=1_000_000,
        )(*parts)
        terms = [line[0]]
        for s in range(1, Z):
            terms.append(send(line[s], lambda d, w: (d, (w + 4 * s) % W)))
        grad_s, grad_t, norm, grad_latents = call(
            functools.partial(last_body, sizes, scale, Z),
            [
                shape((width, shard_s), F32),
                shape((width, shard_t), F32),
                shape((2, width), F32),
                shape((rows, channels), BF16),
            ],
            moved=1_000_000,
        )(*terms, *operands)
        grad_s, grad_t = grad_s.T, grad_t.T
    else:
        sums = lax.all_to_all(
            grads_t[1], ("dp", "wide"), split_axis=0, concat_axis=0, tiled=True
        )
        norm, grad_latents = call(
            functools.partial(apart_body, sizes, scale),
            [shape((2, width), F32), shape((rows, channels), BF16)],
        )(sums, *operands)
        outs = []
        for full in (grads_s[0], grads_t[0]):
            part = lax.psum_scatter(
                full.astype(F32), "wide", scatter_dimension=0, tiled=True
            ).T.astype(BF16)
            part = lax.psum_scatter(part, "dp", scatter_dimension=0, tiled=True)
            outs.append(part.astype(F32) * scale)
        grad_s, grad_t = outs
    return (
        block_out.reshape(latents.shape),
        grad_latents.reshape(latents.shape),
        grad_s,
        grad_t,
        norm,
    )


def solution(mesh):
    return jax.shard_map(
        local,
        mesh=mesh,
        in_specs=(
            P("dp", "wide", None, None, None),
            P("dp", "wide", None, None, None),
            P(),
            P(),
            P("dp", None),
            P("dp", None),
        ),
        out_specs=(
            P("dp", "wide", None, None, None),
            P("dp", "wide", None, None, None),
            P("dp", "wide"),
            P("dp", "wide"),
            P(None, "wide"),
        ),
        check_vma=False,
    )
```
